256 devices in a mesh: dom: 256 (over z, x, y, core).
Axes of the slice: x: 4, y: 4, z: 8, core: 2. Of those that a mesh axis runs over, the one named last changes fastest.
Arguments:
- wing_jitter: float32 [3, 2097152], P(None, 'dom'), may hold values from 0 to 1
- live_blocks: int32 [256], P('dom'), may hold values from 1 to 64, as said below
- smoothing: float32 [2097152], P('dom'), may hold values from 0.3 to 3
- displacement: float32 [3, 2097152], P(None, 'dom'), may hold values from -20 to 20
- fluid_jitter: float32 [3, 786432], P(None, 'dom'), may hold values from 0 to 1
Outputs:
- coefs: float32 [3, 2097152], P(None, 'dom')
- residual: float32 [3, 2097152], P(None, 'dom')
- fluid_values: float32 [3, 786432], P(None, 'dom')
The draws below stay inside these ranges and needn't reach their ends.
Inputs may be any that keep to these rules, and one draw needn't show every extreme that they name: `live_blocks`: some device holds 64 live blocks, and some device other than the first and the last holds 1.
All inputs are finite; a program needn't handle non-finite values.
Results may differ from the reference program's by a relative error of at most 0.0003.
Values sent between devices are 32-bit elements; how exact they have to be, the bound alone decides.
No kernel may reach another device: no remote copies, remote signals or barrier semaphores. Data moves between devices by JAX's collectives and lax.ppermute only.
A program may use at most 64 MiB of HBM per device.

```python
import math
import jax
import jax.numpy as jnp
from jax import lax

BLK = 128
NBD = 64
FB = 24
ITERS = 3
ROWS = 2097152
FROWS = 786432
N_DOM = 256


def draw_live_blocks(key, part):
    key_counts, key_small, key_large = jax.random.split(key, 3)
    counts = jax.random.randint(key_counts, (N_DOM,), 1, NBD + 1)
    small_index = jax.random.randint(key_small, (), 1, N_DOM - 1)
    large_index = (small_index + 1 + jax.random.randint(key_large, (), 0, N_DOM - 2)) % N_DOM
    places = jnp.arange(N_DOM)
    counts = jnp.where(places == large_index, NBD, counts)
    counts = jnp.where(places == small_index, 1, counts)
    return counts.astype(jnp.int32)


def draw_displacement(key, part):
    key_values = jax.random.fold_in(key, 0)
    values = jax.random.truncated_normal(key_values, -6.0, 6.0, (3, ROWS), jnp.float32)
    rising = 1.0 + 2.0 * jnp.arange(ROWS, dtype=jnp.float32) / (ROWS - 1)
    values = values * rising[None, :]
    return values


def shard_levels(key, extent, shards, smallest, largest):
    level = 1.0
    for position, shards_of in shards:
        steps = jax.random.uniform(jax.random.fold_in(jax.random.fold_in(key, 6), position), (shards_of,), jnp.float32, smallest / len(shards), largest / len(shards))
        level = level * jnp.repeat(jnp.exp(steps), extent[position] // shards_of).reshape((-1,) + (1,) * (len(extent) - 1 - position))
    return level


def setup_inputs(seed: int = 0) -> dict:
    splits = jax.random.split(jax.random.key(seed), 6)
    return {
        "wing_jitter": jnp.clip(1.0 * jax.random.uniform(splits[0], (3, ROWS), jnp.float32) ** shard_levels(splits[0], (3, ROWS), ((1, 256),), -0.2, 0.2), 0.0, 1.0),
        "live_blocks": draw_live_blocks(jax.random.fold_in(splits[5], 71), 0),
        "smoothing": jnp.clip(jnp.exp(math.log(3.0) - 2.3025851 * jax.random.uniform(splits[2], (ROWS,), jnp.float32) ** shard_levels(splits[2], (ROWS,), ((0, 256),), -0.2, 0.2)), 0.3, 3.0),
        "displacement": draw_displacement(jax.random.fold_in(splits[5], 71), 0),
        "fluid_jitter": jnp.clip(1.0 * jax.random.uniform(splits[4], (3, FROWS), jnp.float32) ** shard_levels(splits[4], (3, FROWS), ((1, 256),), -0.2, 0.2), 0.0, 1.0),
    }


def wendland(row_points, col_points):
    spread = (row_points[0][:, None] - col_points[0][None, :]) ** 2
    spread = spread + (row_points[1][:, None] - col_points[1][None, :]) ** 2
    spread = spread + (row_points[2][:, None] - col_points[2][None, :]) ** 2
    scaled = jnp.sqrt(spread) * 0.5
    remain = jnp.maximum(1.0 - scaled, 0.0)
    return remain * remain * remain * remain * (4.0 * scaled + 1.0)

def reference(wing_jitter, live_blocks, smoothing, displacement, fluid_jitter):
    block_count = N_DOM * NBD
    starts = (jnp.cumsum(live_blocks) - live_blocks).astype(jnp.int32)
    total = jnp.sum(live_blocks).astype(jnp.int32)
    block_ids = jnp.arange(block_count, dtype=jnp.int32)
    owners = block_ids // NBD
    local_ids = block_ids % NBD
    valid = local_ids < live_blocks[owners]
    chain = (starts[owners] + local_ids).astype(jnp.int32)
    slots = jnp.where(valid, chain, block_count).astype(jnp.int32)
    lookup = jnp.zeros((block_count,), jnp.int32).at[slots].set(block_ids, mode='drop')
    scales = jnp.array([1.0, 6.0, 6.0], jnp.float32)[None, :, None]
    unit_x = jnp.array([1.0, 0.0, 0.0], jnp.float32)[:, None]
    wing = wing_jitter.reshape(3, block_count, BLK).transpose(1, 0, 2) * scales
    row_mask = jnp.repeat(valid.astype(jnp.float32), BLK)

    def band_sum(points, chain_at, usable, vectors):
        summed = jnp.zeros((3, BLK), jnp.float32)
        for delta in range(-2, 3):
            target = chain_at + delta
            usable_here = usable & (target >= 0) & (target < total)
            source = lookup[jnp.clip(target, 0, block_count - 1)]
            col_points = wing[source] + delta * unit_x
            kernel = wendland(points, col_points)
            product = jnp.dot(vectors[source], kernel.T, precision=lax.Precision.HIGHEST)
            summed = summed + jnp.where(usable_here, product, 0.0)
        return summed

    def apply(vector):
        blocks = vector.reshape(3, block_count, BLK).transpose(1, 0, 2)

        def one_block(index):
            return band_sum(wing[index], chain[index], valid[index], blocks)

        def one_group(indices):
            return jax.vmap(one_block)(indices)
        result = lax.map(one_group, block_ids.reshape(-1, 16))
        result = result.reshape(block_count, 3, BLK).transpose(1, 0, 2).reshape(3, -1)
        return result * row_mask + smoothing * vector
    rhs = displacement * row_mask
    diagonal = 1.0 + smoothing
    coefs = jnp.zeros_like(rhs)
    residual = rhs
    precond = residual / diagonal
    direction = precond
    norm_now = lax.optimization_barrier(jnp.sum(residual * precond, axis=1))
    for iteration in range(ITERS):
        image = apply(direction)
        step_size = norm_now / lax.optimization_barrier(jnp.sum(direction * image, axis=1))
        coefs = coefs + step_size[:, None] * direction
        residual = residual - step_size[:, None] * image
        precond = residual / diagonal
        norm_next = lax.optimization_barrier(jnp.sum(residual * precond, axis=1))
        direction = precond + (norm_next / norm_now)[:, None] * direction
        norm_now = norm_next
    fluid_count = N_DOM * FB
    fluid_ids = jnp.arange(fluid_count, dtype=jnp.int32)
    fluid_owner = fluid_ids // FB
    anchors = fluid_ids % FB * live_blocks[fluid_owner] // FB
    fluid_chain = (starts[fluid_owner] + anchors).astype(jnp.int32)
    fluid = fluid_jitter.reshape(3, fluid_count, BLK).transpose(1, 0, 2) * scales
    coef_blocks = coefs.reshape(3, block_count, BLK).transpose(1, 0, 2)

    def one_fluid(index):
        return band_sum(fluid[index], fluid_chain[index], jnp.array(True), coef_blocks)

    def fluid_group(indices):
        return jax.vmap(one_fluid)(indices)
    fluid_values = lax.map(fluid_group, fluid_ids.reshape(-1, 8))
    fluid_values = fluid_values.reshape(fluid_count, 3, BLK).transpose(1, 0, 2).reshape(3, -1)
    return (coefs, residual, fluid_values)
```

```python
import functools
import jax
import jax.numpy as jnp
from jax import lax
from jax.experimental import pallas as pl
from jax.experimental.pallas import tpu as pltpu
from jax.sharding import PartitionSpec as P

BLK = 128
ITERS = 3
HALO = 6
BASE = 2 * HALO
NEAR = 4
PIECES = 48
MAX_AMPLIFICATION = 50.0

stretch_factors = (1.0, 6.0, 6.0)


def pack_kernel(live_ref, jitter_ref, smoothing_ref, displacement_ref, ends_ref):
    live = live_ref[0]
    count = jnp.full((1, BLK), jnp.minimum(live, HALO), jnp.int32).astype(jnp.float32)
    for slot in range(HALO):
        tail_block = live - HALO + slot
        tail_start = pl.multiple_of(jnp.maximum(tail_block, 0) * BLK, BLK)
        starts = ((tail_block >= 0, tail_start), (slot < live, slot * BLK))
        for end, (kept, start) in enumerate(starts):
            lanes = pl.ds(start, BLK)
            mask = kept.astype(jnp.float32)
            ends_ref[end, slot, 0:3, :] = jitter_ref[:, lanes] * mask
            ends_ref[end, slot, 3:4, :] = smoothing_ref[:, lanes] * mask
            ends_ref[end, slot, 4:7, :] = displacement_ref[:, lanes] * mask
            ends_ref[end, slot, 7:8, :] = count


def count_in(row):
    return jnp.max(row).astype(jnp.int32)


def join_kernel(axes, end, near_ref, far_ref, joined_ref, buffer):
    core = lax.rem(lax.axis_index(axes), 2)
    near = near_ref[core] if end else near_ref[...]
    far = far_ref[core] if end else far_ref[...]
    count = near[0, 7:8, :] + far[0, 7:8, :]
    held = count_in(near[0, 7:8, :])
    buffer[pl.ds(HALO, HALO)] = near
    buffer[pl.ds(HALO + jnp.where(core == 0, -held, held), HALO)] = far
    joined_ref[...] = buffer[pl.ds(HALO, HALO)]
    for slot in range(HALO):
        joined_ref[slot, 7:8, :] = jnp.minimum(count, float(HALO))


def split(values):
    high = values.astype(jnp.bfloat16).astype(jnp.float32)
    rest = values - high
    middle = rest.astype(jnp.bfloat16).astype(jnp.float32)
    return high, middle, rest - middle


def rows_of(row):
    return lax.broadcasted_iota(jnp.int32, (8, BLK), 0) == row


def centred(jitter):
    row = lax.broadcasted_iota(jnp.int32, (8, BLK), 0)
    scale = jnp.where(row == 0, 0.5, 3.0)
    shift = jnp.where(row == 0, 0.25, 1.5)
    return jnp.where(row < 3, jitter * scale - shift, 0.0)


def source_rows(points, norm):
    extended = jnp.where(rows_of(3), norm, jnp.where(rows_of(4), 1.0, points))
    high, middle, low = split(extended)
    return jnp.concatenate([high, high, middle, high, low, middle], axis=0)


def target_parts(points, norm):
    base = jnp.where(rows_of(4), norm, -2.0 * points)
    slope = jnp.where(rows_of(0), 1.0, jnp.where(rows_of(4), -points[0:1], 0.0))
    return base, slope


def target_rows(base, slope, delta):
    moved = base + float(delta) * slope + jnp.where(rows_of(4), 0.25 * delta * delta, 0.0)
    high, middle, low = split(moved)
    first = jnp.where(rows_of(3), 1.0, high)
    return jnp.concatenate([first, middle, first, low, first, middle], axis=0).astype(jnp.bfloat16)


def wendland_of_quarter(quarter):
    quarter = jnp.maximum(quarter, 1e-30)
    scaled = quarter * lax.rsqrt(quarter)
    remain = jnp.maximum(1.0 - scaled, 0.0)
    square = remain * remain
    return square * square * (4.0 * scaled + 1.0)


def store_pair(ref, values, first_row):
    high = values.astype(jnp.bfloat16)
    low = (values - high.astype(jnp.float32)).astype(jnp.bfloat16)
    ref[pl.ds(first_row, BLK), 0:BLK] = high
    ref[pl.ds(first_row, BLK), BLK : 2 * BLK] = low


def vector_pair(values):
    high = values.astype(jnp.bfloat16).astype(jnp.float32)
    return jnp.concatenate([high, values - high], axis=0).astype(jnp.bfloat16)


def sum_pairs(product, first):
    upper = product[first : first + 8] + product[first + 8 : first + 16]
    return upper[:, :BLK] + upper[:, BLK:]


def chain_kernel(
    axes, block_count, fluid_count,
    live_ref, jitter_ref, smoothing_ref, displacement_ref, fluid_ref, partner_ref, mine_ref, other_ref,
    w1_ref, w2_ref, w3_ref, moments_ref, fluid_basis_ref,
    joined, source, base, slope, inverse, w0, z0, z1, z2, b0, b1, b2, matrix, fluid_matrix,
):
    live = live_ref[0]
    width = block_count + 2 * HALO

    for extra in range(HALO):
        joined[BASE + block_count + extra] = jnp.zeros((8, BLK), jnp.float32)

    def put_own(block, carry):
        lanes = pl.ds(pl.multiple_of(block * BLK, BLK), BLK)
        kept = (block < live).astype(jnp.float32)
        joined[BASE + block, 0:3, :] = jitter_ref[:, lanes]
        joined[BASE + block, 3:4, :] = smoothing_ref[:, lanes] * kept
        joined[BASE + block, 4:7, :] = displacement_ref[:, lanes]
        return carry

    lax.fori_loop(0, block_count, put_own, 0, unroll=8)
    core = lax.rem(lax.axis_index(axes), 2)
    mine, other = mine_ref[...], other_ref[...]
    left_near = jnp.where(core == 0, 0, count_in(partner_ref[0, 0, 7:8, :]))
    right_near = jnp.where(core == 0, count_in(partner_ref[1, 0, 7:8, :]), 0)
    joined[pl.ds(BASE - HALO, HALO)] = partner_ref[0]
    joined[pl.ds(BASE - HALO - left_near, HALO)] = jnp.where(core == 0, mine, other)
    joined[pl.ds(BASE + live, HALO)] = partner_ref[1]
    joined[pl.ds(BASE + live + right_near, HALO)] = jnp.where(core == 0, other, mine)

    def prepare(block, carry):
        packed = joined[BASE - HALO + block]
        points = centred(packed)
        norm = jnp.sum(points * points, axis=0, keepdims=True)
        source[block] = jnp.transpose(source_rows(points, norm)).astype(jnp.bfloat16)
        base[block], slope[block] = target_parts(points, norm)
        scale = jnp.where(packed[3:4] > 0.0, 1.0 / (1.0 + packed[3:4]), 0.0)
        scale = jnp.broadcast_to(scale, (8, BLK))
        rhs = jnp.concatenate([packed[4:7], jnp.zeros((5, BLK), jnp.float32)], axis=0)
        inverse[block] = scale
        w0[block] = rhs
        z0[block] = rhs * scale
        b0[block] = vector_pair(rhs * scale)
        return carry

    lax.fori_loop(0, width, prepare, 0, unroll=4)

    def generate(row, carry):
        for place in range(5):
            columns = target_rows(base[row + 2], slope[row + 2], place - 2)
            quarter = jnp.dot(source[row + place], columns, preferred_element_type=jnp.float32)
            store_pair(matrix.at[row], wendland_of_quarter(quarter), place * BLK)
        return carry

    lax.fori_loop(0, block_count + 2 * NEAR, generate, 0)

    def apply(values, pairs, first, last, place_next):
        def one_row(row, carry):
            near = jnp.concatenate([pairs[row + place] for place in range(5)], axis=1)
            product = jnp.dot(near, matrix[row], preferred_element_type=jnp.float32)
            place_next(row + 2, sum_pairs(product, 0) - values[row + 2])
            return carry

        lax.fori_loop(first, last, one_row, 0, unroll=4)

    rows = block_count + 2 * NEAR

    def first_next(block, image):
        scaled = image * inverse[block]
        z1[block] = scaled
        b1[block] = vector_pair(scaled)
        w1_ref[block] = image

    def second_next(block, image):
        scaled = image * inverse[block]
        z2[block] = scaled
        b2[block] = vector_pair(scaled)
        w2_ref[block] = image

    def third_next(block, image):
        w3_ref[block] = image

    apply(z0, b0, 0, rows, first_next)
    apply(z1, b1, 2, rows - 2, second_next)
    apply(z2, b2, 4, rows - 4, third_next)

    def add_up(own, sums):
        block = own + HALO
        kept = (own < live).astype(jnp.float32)
        third = w3_ref[block]
        pairs = (
            (z0[block], w0[block]),
            (z0[block], w1_ref[block]),
            (z1[block], w1_ref[block]),
            (z1[block], w2_ref[block]),
            (z2[block], w2_ref[block]),
            (z2[block], third),
            (third * inverse[block], third),
        )
        return tuple(s + kept * (a * b) for s, (a, b) in zip(sums, pairs))

    zero = jnp.zeros((8, BLK), jnp.float32)
    sums = lax.fori_loop(0, block_count, add_up, (zero,) * 7, unroll=4)
    lane = lax.broadcasted_iota(jnp.int32, (8, BLK), 1)
    moments = zero
    for k in range(7):
        moments = jnp.where(lane == k, jnp.sum(sums[k], axis=1, keepdims=True), moments)
    moments_ref[...] = moments

    def fluid_block(index, carry):
        anchor = lax.div(index * live, jnp.int32(fluid_count))
        lanes = pl.ds(pl.multiple_of(index * BLK, BLK), BLK)
        jitter = jnp.concatenate([fluid_ref[:, lanes], jnp.zeros((5, BLK), jnp.float32)], axis=0)
        points = centred(jitter)
        norm = jnp.sum(points * points, axis=0, keepdims=True)
        base_here, slope_here = target_parts(points, norm)
        near = []
        for place in range(5):
            block = anchor + (HALO - 2 + place)
            columns = target_rows(base_here, slope_here, place - 2)
            quarter = jnp.dot(source[block], columns, preferred_element_type=jnp.float32)
            store_pair(fluid_matrix, wendland_of_quarter(quarter), place * BLK)
            near.append(jnp.concatenate([b0[block], b1[block], b2[block]], axis=0))
        near = jnp.concatenate(near, axis=1)
        product = jnp.dot(near, fluid_matrix[...], preferred_element_type=jnp.float32)
        for k in range(3):
            fluid_basis_ref[index, k] = sum_pairs(product, 16 * k)
        return carry

    lax.fori_loop(0, fluid_count, fluid_block, 0)


def step_coefficients(moments):
    def inner(left, right):
        total = 0.0
        for i, a in enumerate(left):
            for j, b in enumerate(right):
                total = total + a * b * moments[i + j]
        return total

    one = jnp.ones_like(moments[0])
    solution_part, residual, direction = [], [one], [one]
    norm = moments[0]
    for iteration in range(ITERS):
        image = [
            (direction[k] if k < len(direction) else 0.0) + (direction[k - 1] if k else 0.0)
            for k in range(len(direction) + 1)
        ]
        step = norm / inner(direction, image)
        old = solution_part + [0.0] * (len(direction) - len(solution_part))
        solution_part = [a + step * b for a, b in zip(old, direction)]
        residual = [
            (residual[k] if k < len(residual) else 0.0) - step * image[k] for k in range(len(image))
        ]
        following = inner(residual, residual)
        ratio = following / norm
        direction = [
            residual[k] + ratio * (direction[k] if k < len(direction) else 0.0)
            for k in range(len(residual))
        ]
        norm = following
    spread = 0.0
    for k, a in enumerate(residual):
        spread = spread + jnp.abs(a) * jnp.sqrt(jnp.maximum(moments[2 * k], 0.0))
    return solution_part, residual, spread * spread <= MAX_AMPLIFICATION**2 * norm


def finish_kernel(
    block_count, fluid_count, live_ref, moments_ref, smoothing_ref, displacement_ref,
    w1_ref, w2_ref, w3_ref, fluid_basis_ref, coefs_ref, residual_ref, fluid_ref, good_ref,
):
    live = live_ref[0]
    moments = moments_ref[...]
    solved, left, good = step_coefficients([moments[:, k : k + 1] for k in range(7)])
    row = lax.broadcasted_iota(jnp.int32, (8, 1), 0)
    good_ref[0] = jnp.min(jnp.where(good | (row > 2), 1.0, 0.0)).astype(jnp.int32)
    solved = [jnp.broadcast_to(v, (8, BLK))[0:3] for v in solved]
    left = [jnp.broadcast_to(v, (8, BLK))[0:3] for v in left]

    def one_block(own, carry):
        lanes = pl.ds(pl.multiple_of(own * BLK, BLK), BLK)
        block = own + HALO
        parts = [displacement_ref[:, lanes]] + [r[block][0:3] for r in (w1_ref, w2_ref, w3_ref)]
        scaled = sum(a * b for a, b in zip(solved, parts)) / (1.0 + smoothing_ref[:, lanes])
        remaining = sum(a * b for a, b in zip(left, parts))
        is_live = own < live
        coefs_ref[:, lanes] = jnp.where(is_live, scaled, 0.0)
        residual_ref[:, lanes] = jnp.where(is_live, remaining, 0.0)
        return carry

    lax.fori_loop(0, block_count, one_block, 0, unroll=4)

    def one_fluid(index, carry):
        lanes = pl.ds(pl.multiple_of(index * BLK, BLK), BLK)
        fluid_ref[:, lanes] = sum(a * fluid_basis_ref[index, k][0:3] for k, a in enumerate(solved))
        return carry

    lax.fori_loop(0, fluid_count, one_fluid, 0, unroll=4)


def wendland(row_points, col_points):
    spread = (row_points[0][:, None] - col_points[0][None, :]) ** 2
    spread = spread + (row_points[1][:, None] - col_points[1][None, :]) ** 2
    spread = spread + (row_points[2][:, None] - col_points[2][None, :]) ** 2
    scaled = jnp.sqrt(spread) * 0.5
    remain = jnp.maximum(1.0 - scaled, 0.0)
    return remain * remain * remain * remain * (4.0 * scaled + 1.0)


def block_ends(blocks, live_count):
    tail_index = live_count - 2 + jnp.arange(2, dtype=jnp.int32)
    tail_flags = (tail_index >= 0).astype(jnp.float32)
    padded = jnp.pad(blocks, ((0, 0), (2, 0), (0, 0)))
    tail_blocks = lax.dynamic_slice_in_dim(padded, live_count, 2, axis=1)
    head_flags = (jnp.arange(2, dtype=jnp.int32) < live_count).astype(jnp.float32)
    return (tail_blocks, tail_flags, blocks[:, :2], head_flags)


def join_left(nearer, farther, pick):
    return jnp.stack([jnp.where(pick, nearer[:, 0], farther[:, 1]), nearer[:, 1]], axis=1)


def join_right(nearer, farther, pick):
    return jnp.stack([nearer[:, 0], jnp.where(pick, nearer[:, 1], farther[:, 0])], axis=1)


def extend(own_blocks, left_pair, right_pair, live_count):
    padded = jnp.concatenate([left_pair, own_blocks, jnp.zeros_like(left_pair)], axis=1)
    return lax.dynamic_update_slice_in_dim(padded, right_pair, live_count + 2, axis=1)


def shifted(block, axes, distance):
    devices = range(lax.axis_size(axes))
    route = [(i - distance, i) for i in devices if i - distance in devices]
    return lax.ppermute(block, axes, route)


def iterate_with_reductions(axes, wing_jitter, live_blocks, smoothing, displacement, fluid_jitter):
    block_count = wing_jitter.shape[1] // BLK
    fluid_count = fluid_jitter.shape[1] // BLK
    live_count = live_blocks[0]
    factors = jnp.array(stretch_factors, jnp.float32)[:, None, None]
    own_points = wing_jitter.reshape(3, block_count, BLK) * factors
    own_flags = (jnp.arange(block_count, dtype=jnp.int32) < live_count).astype(jnp.float32)
    ends_of = {}
    neighbour_counts = {}
    for offset in (1, 2, -1, -2):
        points, counts = shifted((own_points, live_blocks), axes, offset)
        tail_blocks, tail_flags, head_blocks, head_flags = block_ends(points, counts[0])
        neighbour_counts[offset] = counts[0]
        ends_of[offset] = (tail_blocks, tail_flags) if offset > 0 else (head_blocks, head_flags)
    left_pick = ends_of[1][1][0] > 0
    right_pick = ends_of[-1][1][1] > 0
    left_points = join_left(ends_of[1][0], ends_of[2][0], left_pick)
    right_points = join_right(ends_of[-1][0], ends_of[-2][0], right_pick)
    left_flags = join_left(ends_of[1][1][None, :, None], ends_of[2][1][None, :, None], left_pick)
    right_flags = join_right(
        ends_of[-1][1][None, :, None], ends_of[-2][1][None, :, None], right_pick
    )
    ext_points = extend(own_points, left_points, right_points, live_count)
    ext_flags = extend(own_flags[None, :, None], left_flags, right_flags, live_count)
    ext_along = jnp.arange(block_count + 4, dtype=jnp.float32) - 2.0
    ext_points = ext_points.at[0].add(ext_along[:, None]).reshape(3, -1)
    col_flags = jnp.broadcast_to(ext_flags[0], (block_count + 4, BLK)).reshape(-1)
    row_points = (
        own_points.at[0].add(jnp.arange(block_count, dtype=jnp.float32)[:, None]).reshape(3, -1)
    )
    row_mask = jnp.repeat(own_flags, BLK)
    diagonal = 1.0 + smoothing

    def value_context(blocks):
        pieces = {}
        for offset in (1, 2, -1, -2):
            moved = shifted(blocks, axes, offset)
            tail_part, _, head_part, _ = block_ends(moved, neighbour_counts[offset])
            pieces[offset] = tail_part if offset > 0 else head_part
        left_values = join_left(pieces[1], pieces[2], left_pick)
        right_values = join_right(pieces[-1], pieces[-2], right_pick)
        return extend(blocks, left_values, right_values, live_count).reshape(3, -1)

    def apply(vector):
        ext_values = value_context(vector.reshape(3, block_count, BLK))

        def row_group(group):
            first_row = group * (2 * BLK)
            points = lax.dynamic_slice_in_dim(row_points, first_row, 2 * BLK, 1)
            col_points = lax.dynamic_slice_in_dim(ext_points, first_row, 6 * BLK, 1)
            flags = lax.dynamic_slice_in_dim(col_flags, first_row, 6 * BLK, 0)
            kernel = wendland(points, col_points) * flags[None, :]
            col_values = lax.dynamic_slice_in_dim(ext_values, first_row, 6 * BLK, 1)
            return jnp.einsum("cj,ij->ci", col_values, kernel, precision=lax.Precision.HIGHEST)

        result = lax.map(row_group, jnp.arange(block_count // 2, dtype=jnp.int32))
        result = result.transpose(1, 0, 2).reshape(3, -1)
        return result * row_mask + smoothing * vector

    def total(left, right):
        return lax.psum(jnp.sum(left * right, axis=1), axes)

    rhs = displacement * row_mask
    coefs = jnp.zeros_like(rhs)
    residual = rhs
    direction = precond = residual / diagonal
    norm_now = total(residual, precond)
    for iteration in range(ITERS):
        image = apply(direction)
        step_size = norm_now / total(direction, image)
        coefs = coefs + step_size[:, None] * direction
        residual = residual - step_size[:, None] * image
        if iteration + 1 < ITERS:
            precond = residual / diagonal
            norm_next = total(residual, precond)
            direction = precond + (norm_next / norm_now)[:, None] * direction
            norm_now = norm_next
    anchors = jnp.arange(fluid_count, dtype=jnp.int32) * live_count // fluid_count
    fluid_points = fluid_jitter.reshape(3, fluid_count, BLK) * factors
    fluid_points = fluid_points.at[0].add(anchors.astype(jnp.float32)[:, None])
    coef_ext = value_context(coefs.reshape(3, block_count, BLK))

    def fluid_block(points_and_anchor):
        points, anchor = points_and_anchor
        start_col = anchor * BLK
        col_points = lax.dynamic_slice_in_dim(ext_points, start_col, 5 * BLK, 1)
        flags = lax.dynamic_slice_in_dim(col_flags, start_col, 5 * BLK, 0)
        kernel = wendland(points, col_points) * flags[None, :]
        col_values = lax.dynamic_slice_in_dim(coef_ext, start_col, 5 * BLK, 1)
        return jnp.einsum("cj,ij->ci", col_values, kernel, precision=lax.Precision.HIGHEST)

    fluid_values = lax.map(fluid_block, (fluid_points.transpose(1, 0, 2), anchors))
    fluid_values = fluid_values.transpose(1, 0, 2).reshape(3, -1)
    return (coefs, residual, fluid_values)


def add_over_all(values, axes, partners):
    count = lax.axis_size(axes)
    for bits in partners:
        values = values + lax.ppermute(values, axes, [(i, i ^ bits) for i in range(count)])
    return values


def along_chips(values, axes, chips):
    count = lax.axis_size(axes)
    route = [(i, i + 2 * chips * (1 - 2 * (i % 2))) for i in range(count)]
    return lax.ppermute(values, axes, [(i, j) for i, j in route if 0 <= j < count])


def per_device(axes, partners, wing_jitter, live_blocks, smoothing, displacement, fluid_jitter):
    block_count = wing_jitter.shape[1] // BLK
    fluid_count = fluid_jitter.shape[1] // BLK
    width = block_count + 2 * HALO
    smoothing_row = smoothing.reshape(1, -1)
    in_smem = pl.BlockSpec(memory_space=pltpu.SMEM)
    in_vmem = pl.BlockSpec(memory_space=pltpu.VMEM)

    def floats(*shape):
        return jax.ShapeDtypeStruct(shape, jnp.float32)

    ends = pl.pallas_call(
        pack_kernel,
        out_shape=floats(2, HALO, 8, BLK),
        in_specs=[in_smem] + [in_vmem] * 3,
        out_specs=in_vmem,
    )(live_blocks, wing_jitter, smoothing_row, displacement)

    def join(near, far, end=False):
        return pl.pallas_call(
            functools.partial(join_kernel, axes, end),
            out_shape=floats(HALO, 8, BLK),
            in_specs=[in_vmem] * 2,
            out_specs=in_vmem,
            scratch_shapes=[pltpu.VMEM((3 * HALO, 8, BLK), jnp.float32)],
        )(near, far)

    cores = [(i, i ^ 1) for i in range(lax.axis_size(axes))]
    partner = lax.ppermute(ends, axes, cores)
    chip = join(partner, ends, end=True)
    next_chip = along_chips(chip, axes, 1)
    beyond = along_chips(join(chip, next_chip), axes, 2)
    mine = join(next_chip, beyond)
    other = lax.ppermute(mine, axes, cores)

    basis = floats(width, 8, BLK)
    vectors = pltpu.VMEM((width, 8, BLK), jnp.float32)
    pairs = pltpu.VMEM((width, 16, BLK), jnp.bfloat16)
    w1, w2, w3, moments, fluid_basis = pl.pallas_call(
        functools.partial(chain_kernel, axes, block_count, fluid_count),
        out_shape=(basis, basis, basis, floats(8, BLK), floats(fluid_count, 3, 8, BLK)),
        in_specs=[in_smem] + [in_vmem] * 7,
        out_specs=(in_vmem,) * 5,
        scratch_shapes=[
            pltpu.VMEM((2 * BASE + block_count, 8, BLK), jnp.float32),
            pltpu.VMEM((width, BLK, PIECES), jnp.bfloat16),
            *[vectors] * 7,
            *[pairs] * 3,
            pltpu.VMEM((block_count + 2 * NEAR, 5 * BLK, 2 * BLK), jnp.bfloat16),
            pltpu.VMEM((5 * BLK, 2 * BLK), jnp.bfloat16),
        ],
        compiler_params=pltpu.CompilerParams(vmem_limit_bytes=48 * 2**20),
    )(live_blocks, wing_jitter, smoothing_row, displacement, fluid_jitter, partner, mine, other)
    moments = add_over_all(moments, axes, partners)
    coefs, residual, fluid_values, good = pl.pallas_call(
        functools.partial(finish_kernel, block_count, fluid_count),
        out_shape=(
            floats(3, block_count * BLK),
            floats(3, block_count * BLK),
            floats(3, fluid_count * BLK),
            jax.ShapeDtypeStruct((1,), jnp.int32),
        ),
        in_specs=[in_smem] + [in_vmem] * 7,
        out_specs=(in_vmem, in_vmem, in_vmem, in_smem),
    )(live_blocks, moments, smoothing_row, displacement, w1, w2, w3, fluid_basis)
    return lax.cond(
        good[0] == 1,
        lambda: (coefs, residual, fluid_values),
        lambda: iterate_with_reductions(
            axes, wing_jitter, live_blocks, smoothing, displacement, fluid_jitter
        ),
    )


def solution(mesh):
    placed = (P(None, "dom"), P("dom"), P("dom"), P(None, "dom"), P(None, "dom"))
    partners = (1, 2, 6, 8, 24, 32, 64, 192)
    return jax.shard_map(
        functools.partial(per_device, "dom", partners),
        mesh=mesh,
        in_specs=placed,
        out_specs=(P(None, "dom"),) * 3,
        check_vma=False,
    )
```

```python
import functools
import jax
import jax.numpy as jnp
from jax import lax
from jax.experimental import pallas as pl
from jax.experimental.pallas import tpu as pltpu
from jax.sharding import PartitionSpec as P

BLK = 128
ITERS = 3
HALO = 6
BASE = 2 * HALO
NEAR = 4
PIECES = 48
MAX_AMPLIFICATION = 50.0
MOMENTS = 2 * ITERS + 1
GROUP = 4
APPLY_UNROLL = 8

stretch_factors = (1.0, 6.0, 6.0)


def pack_kernel(live_ref, jitter_ref, smoothing_ref, displacement_ref, ends_ref):
    live = live_ref[0]
    count = jnp.full((1, BLK), jnp.minimum(live, HALO), jnp.int32).astype(jnp.float32)
    for slot in range(HALO):
        tail_block = live - HALO + slot
        tail_start = pl.multiple_of(jnp.maximum(tail_block, 0) * BLK, BLK)
        starts = ((tail_block >= 0, tail_start), (slot < live, slot * BLK))
        for end, (kept, start) in enumerate(starts):
            lanes = pl.ds(start, BLK)
            mask = kept.astype(jnp.float32)
            ends_ref[end, slot, 0:3, :] = jitter_ref[:, lanes] * mask
            ends_ref[end, slot, 3:4, :] = smoothing_ref[:, lanes] * mask
            ends_ref[end, slot, 4:7, :] = displacement_ref[:, lanes] * mask
            ends_ref[end, slot, 7:8, :] = count


def count_in(row):
    return jnp.max(row).astype(jnp.int32)


def join_kernel(axes, end, near_ref, far_ref, joined_ref, buffer):
    core = lax.rem(lax.axis_index(axes), 2)
    near = near_ref[core] if end else near_ref[...]
    far = far_ref[core] if end else far_ref[...]
    count = near[0, 7:8, :] + far[0, 7:8, :]
    held = count_in(near[0, 7:8, :])
    buffer[pl.ds(HALO, HALO)] = near
    buffer[pl.ds(HALO + jnp.where(core == 0, -held, held), HALO)] = far
    joined_ref[...] = buffer[pl.ds(HALO, HALO)]
    for slot in range(HALO):
        joined_ref[slot, 7:8, :] = jnp.minimum(count, float(HALO))


def split(values):
    high = values.astype(jnp.bfloat16).astype(jnp.float32)
    rest = values - high
    middle = rest.astype(jnp.bfloat16).astype(jnp.float32)
    return high, middle, rest - middle


def rows_of(row):
    return lax.broadcasted_iota(jnp.int32, (8, BLK), 0) == row


def centred(jitter):
    row = lax.broadcasted_iota(jnp.int32, (8, BLK), 0)
    scale = jnp.where(row == 0, 0.5, 3.0)
    shift = jnp.where(row == 0, 0.25, 1.5)
    return jnp.where(row < 3, jitter * scale - shift, 0.0)


def source_rows(points, norm):
    extended = jnp.where(rows_of(3), norm, jnp.where(rows_of(4), 1.0, points))
    high, middle, low = split(extended)
    return jnp.concatenate([high, high, middle, high, low, middle], axis=0)


def target_parts(points, norm):
    base = jnp.where(rows_of(4), norm, -2.0 * points)
    slope = jnp.where(rows_of(0), 1.0, jnp.where(rows_of(4), -points[0:1], 0.0))
    return base, slope


def target_rows(base, slope, delta):
    moved = base + float(delta) * slope + jnp.where(rows_of(4), 0.25 * delta * delta, 0.0)
    high, middle, low = split(moved)
    first = jnp.where(rows_of(3), 1.0, high)
    return jnp.concatenate([first, middle, first, low, first, middle], axis=0).astype(jnp.bfloat16)


def wendland_of_quarter(quarter):
    quarter = jnp.maximum(quarter, 1e-30)
    scaled = quarter * lax.rsqrt(quarter)
    remain = jnp.maximum(1.0 - scaled, 0.0)
    square = remain * remain
    return square * square * (4.0 * scaled + 1.0)


def store_pair(ref, values, first_row):
    high = values.astype(jnp.bfloat16)
    low = (values - high.astype(jnp.float32)).astype(jnp.bfloat16)
    ref[pl.ds(first_row, BLK), 0:BLK] = high
    ref[pl.ds(first_row, BLK), BLK : 2 * BLK] = low


def vector_pair(values):
    high = values.astype(jnp.bfloat16).astype(jnp.float32)
    return jnp.concatenate([high, values - high], axis=0).astype(jnp.bfloat16)


def sum_pairs(product, first):
    upper = product[first : first + 8] + product[first + 8 : first + 16]
    return upper[:, :BLK] + upper[:, BLK:]


def join_chain(axes, live, jitter_ref, smoothing_ref, displacement_ref, partner_ref, mine_ref, other_ref, joined):
    block_count = jitter_ref.shape[1] // BLK
    for extra in range(HALO):
        joined[BASE + block_count + extra] = jnp.zeros((8, BLK), jnp.float32)

    def put_own(block, carry):
        lanes = pl.ds(pl.multiple_of(block * BLK, BLK), BLK)
        kept = (block < live).astype(jnp.float32)
        joined[BASE + block, 0:3, :] = jitter_ref[:, lanes]
        joined[BASE + block, 3:4, :] = smoothing_ref[:, lanes] * kept
        joined[BASE + block, 4:7, :] = displacement_ref[:, lanes]
        return carry

    lax.fori_loop(0, block_count, put_own, 0, unroll=8)
    core = lax.rem(lax.axis_index(axes), 2)
    mine, other = mine_ref[...], other_ref[...]
    left_near = jnp.where(core == 0, 0, count_in(partner_ref[0, 0, 7:8, :]))
    right_near = jnp.where(core == 0, count_in(partner_ref[1, 0, 7:8, :]), 0)
    joined[pl.ds(BASE - HALO, HALO)] = partner_ref[0]
    joined[pl.ds(BASE - HALO - left_near, HALO)] = jnp.where(core == 0, mine, other)
    joined[pl.ds(BASE + live, HALO)] = partner_ref[1]
    joined[pl.ds(BASE + live + right_near, HALO)] = jnp.where(core == 0, other, mine)


def parts_of(packed):
    points = centred(packed)
    norm = jnp.sum(points * points, axis=0, keepdims=True)
    inverse = jnp.where(packed[3:4] > 0.0, 1.0 / (1.0 + packed[3:4]), 0.0)
    rhs = jnp.concatenate([packed[4:7], jnp.zeros((5, BLK), jnp.float32)], axis=0)
    return points, norm, jnp.broadcast_to(inverse, (8, BLK)), rhs


def source_of(points, norm):
    return jnp.transpose(source_rows(points, norm)).astype(jnp.bfloat16)


def chain_kernel(
    axes, block_count,
    live_ref, jitter_ref, smoothing_ref, displacement_ref, partner_ref, mine_ref, other_ref,
    basis_ref, moments_ref,
    joined, source, base, slope, inverse, w0, z0, z1, z2, b0, b1, b2, matrix,
):
    w1_ref, w2_ref, w3_ref = (basis_ref.at[k] for k in range(3))
    live = live_ref[0]
    width = block_count + 2 * HALO
    join_chain(
        axes, live, jitter_ref, smoothing_ref, displacement_ref, partner_ref, mine_ref, other_ref, joined
    )

    def prepare(block, carry):
        points, norm, scale, rhs = parts_of(joined[BASE - HALO + block])
        source[block] = source_of(points, norm)
        base[block], slope[block] = target_parts(points, norm)
        inverse[block] = scale
        w0[block] = rhs
        z0[block] = rhs * scale
        b0[block] = vector_pair(rhs * scale)
        return carry

    lax.fori_loop(0, width, prepare, 0, unroll=4)

    def generate_two(row):
        for place in range(6):
            columns = []
            if place < 5:
                columns.append(target_rows(base[row + 2], slope[row + 2], place - 2))
            if place > 0:
                columns.append(target_rows(base[row + 3], slope[row + 3], place - 3))
            quarter = jnp.dot(
                source[row + place],
                jnp.concatenate(columns, axis=1),
                preferred_element_type=jnp.float32,
            )
            values = wendland_of_quarter(quarter)
            if place < 5:
                store_pair(matrix.at[row], values[:, :BLK], place * BLK)
            if place > 0:
                store_pair(matrix.at[row + 1], values[:, -BLK:], (place - 1) * BLK)

    def apply_row(row, values, pairs, place_next):
        near = jnp.concatenate([pairs[row + place] for place in range(5)], axis=1)
        product = jnp.dot(near, matrix[row], preferred_element_type=jnp.float32)
        place_next(row + 2, sum_pairs(product, 0) - values[row + 2])

    def apply(values, pairs, first, last, place_next):
        def one_row(row, carry):
            apply_row(row, values, pairs, place_next)
            return carry

        lax.fori_loop(first, last, one_row, 0, unroll=APPLY_UNROLL)

    rows = block_count + 2 * NEAR

    def first_next(block, image):
        scaled = image * inverse[block]
        z1[block] = scaled
        b1[block] = vector_pair(scaled)
        w1_ref[block] = image

    def second_next(block, image):
        scaled = image * inverse[block]
        z2[block] = scaled
        b2[block] = vector_pair(scaled)
        w2_ref[block] = image

    def third_next(block, image):
        w3_ref[block] = image

    def generate_group(group):
        for row in range(0, GROUP, 2):
            generate_two(group * GROUP + row)

    def apply_group(group):
        for row in range(GROUP):
            apply_row(group * GROUP + row, z0, b0, first_next)

    def apply_then_generate(group, carry):
        apply_group(group - 1)
        generate_group(group)
        return carry

    generate_group(0)
    lax.fori_loop(1, rows // GROUP, apply_then_generate, 0)
    apply_group(rows // GROUP - 1)
    apply(z1, b1, 2, rows - 2, second_next)
    apply(z2, b2, 4, rows - 4, third_next)

    def add_up(own, sums):
        block = own + HALO
        kept = (own < live).astype(jnp.float32)
        third = w3_ref[block]
        pairs = (
            (z0[block], w0[block]),
            (z0[block], w1_ref[block]),
            (z1[block], w1_ref[block]),
            (z1[block], w2_ref[block]),
            (z2[block], w2_ref[block]),
            (z2[block], third),
            (third * inverse[block], third),
        )
        return tuple(s + kept * (a * b) for s, (a, b) in zip(sums, pairs))

    zero = jnp.zeros((8, BLK), jnp.float32)
    sums = lax.fori_loop(0, block_count, add_up, (zero,) * MOMENTS, unroll=4)
    lane = lax.broadcasted_iota(jnp.int32, (8, BLK), 1)
    row = lax.broadcasted_iota(jnp.int32, (8, BLK), 0)
    moments = zero
    for k in range(MOMENTS):
        moments = jnp.where(lane == 8 * row + k, jnp.sum(sums[k], axis=1, keepdims=True), moments)
    moments = jnp.sum(moments, axis=0, keepdims=True)
    moments_ref[...] = jnp.broadcast_to(moments, moments_ref.shape)


def fluid_kernel(
    axes, fluid_count,
    live_ref, jitter_ref, smoothing_ref, displacement_ref, fluid_ref, partner_ref, mine_ref, other_ref,
    basis_ref,
    fluid_basis_ref,
    joined, source, b0, b1, b2, matrix,
):
    live = live_ref[0]
    width = jitter_ref.shape[1] // BLK + 2 * HALO
    join_chain(
        axes, live, jitter_ref, smoothing_ref, displacement_ref, partner_ref, mine_ref, other_ref, joined
    )

    def prepare(block, carry):
        points, norm, scale, rhs = parts_of(joined[BASE - HALO + block])
        source[block] = source_of(points, norm)
        b0[block] = vector_pair(rhs * scale)
        b1[block] = vector_pair(basis_ref[0, block] * scale)
        b2[block] = vector_pair(basis_ref[1, block] * scale)
        return carry

    lax.fori_loop(HALO - 2, width - HALO + 2, prepare, 0, unroll=4)

    def anchor_of(index):
        return lax.div(index * live, jnp.int32(fluid_count))

    def generate_fluid(index, carry):
        lanes = pl.ds(pl.multiple_of(index * BLK, BLK), BLK)
        jitter = jnp.concatenate([fluid_ref[:, lanes], jnp.zeros((5, BLK), jnp.float32)], axis=0)
        points = centred(jitter)
        norm = jnp.sum(points * points, axis=0, keepdims=True)
        base_here, slope_here = target_parts(points, norm)
        first = anchor_of(index) + (HALO - 2)
        for place in range(5):
            columns = target_rows(base_here, slope_here, place - 2)
            quarter = jnp.dot(source[first + place], columns, preferred_element_type=jnp.float32)
            store_pair(matrix.at[index], wendland_of_quarter(quarter), place * BLK)
        return carry

    def apply_fluid(index, carry):
        first = anchor_of(index) + (HALO - 2)
        near = [
            jnp.concatenate([ref[first + place] for place in range(5)], axis=1)
            for ref in (b0, b1, b2)
        ]
        near = jnp.concatenate(near, axis=0)
        product = jnp.dot(near, matrix[index], preferred_element_type=jnp.float32)
        for k in range(3):
            fluid_basis_ref[index, k] = sum_pairs(product, 16 * k)
        return carry

    lax.fori_loop(0, fluid_count, generate_fluid, 0, unroll=4)
    lax.fori_loop(0, fluid_count, apply_fluid, 0, unroll=4)


def step_coefficients(moments):
    def inner(left, right):
        total = 0.0
        for i, a in enumerate(left):
            for j, b in enumerate(right):
                total = total + a * b * moments[i + j]
        return total

    one = jnp.ones_like(moments[0])
    solution_part, residual, direction = [], [one], [one]
    norm = moments[0]
    for iteration in range(ITERS):
        image = [
            (direction[k] if k < len(direction) else 0.0) + (direction[k - 1] if k else 0.0)
            for k in range(len(direction) + 1)
        ]
        step = norm / inner(direction, image)
        old = solution_part + [0.0] * (len(direction) - len(solution_part))
        solution_part = [a + step * b for a, b in zip(old, direction)]
        residual = [
            (residual[k] if k < len(residual) else 0.0) - step * image[k] for k in range(len(image))
        ]
        following = inner(residual, residual)
        ratio = following / norm
        direction = [
            residual[k] + ratio * (direction[k] if k < len(direction) else 0.0)
            for k in range(len(residual))
        ]
        norm = following
    spread = 0.0
    for k, a in enumerate(residual):
        spread = spread + jnp.abs(a) * jnp.sqrt(jnp.maximum(moments[2 * k], 0.0))
    return solution_part, residual, spread * spread <= MAX_AMPLIFICATION**2 * norm


def finish_kernel(
    block_count, fluid_count, live_ref, moments_ref, smoothing_ref, displacement_ref,
    basis_ref, fluid_basis_ref, coefs_ref, residual_ref, fluid_ref, good_ref,
):
    live = live_ref[0]
    row = lax.broadcasted_iota(jnp.int32, (8, BLK), 0)
    lane = lax.broadcasted_iota(jnp.int32, (8, BLK), 1)
    summed = jnp.broadcast_to(jnp.sum(moments_ref[...], axis=0, keepdims=True), (8, BLK))
    moments = [
        jnp.sum(jnp.where(lane == 8 * row + k, summed, 0.0), axis=1, keepdims=True)
        for k in range(MOMENTS)
    ]
    solved, left, good = step_coefficients(moments)
    row = lax.broadcasted_iota(jnp.int32, (8, 1), 0)
    good_ref[0] = jnp.min(jnp.where(good | (row > 2), 1.0, 0.0)).astype(jnp.int32)
    solved = [jnp.broadcast_to(v, (8, BLK))[0:3] for v in solved]
    left = [jnp.broadcast_to(v, (8, BLK))[0:3] for v in left]

    def one_block(own, carry):
        lanes = pl.ds(pl.multiple_of(own * BLK, BLK), BLK)
        block = own + HALO
        parts = [displacement_ref[:, lanes]] + [basis_ref[k, block][0:3] for k in range(3)]
        scaled = sum(a * b for a, b in zip(solved, parts)) / (1.0 + smoothing_ref[:, lanes])
        remaining = sum(a * b for a, b in zip(left, parts))
        is_live = own < live
        coefs_ref[:, lanes] = jnp.where(is_live, scaled, 0.0)
        residual_ref[:, lanes] = jnp.where(is_live, remaining, 0.0)
        return carry

    lax.fori_loop(0, block_count, one_block, 0, unroll=4)

    def one_fluid(index, carry):
        lanes = pl.ds(pl.multiple_of(index * BLK, BLK), BLK)
        fluid_ref[:, lanes] = sum(a * fluid_basis_ref[index, k][0:3] for k, a in enumerate(solved))
        return carry

    lax.fori_loop(0, fluid_count, one_fluid, 0, unroll=4)


def wendland(row_points, col_points):
    spread = (row_points[0][:, None] - col_points[0][None, :]) ** 2
    spread = spread + (row_points[1][:, None] - col_points[1][None, :]) ** 2
    spread = spread + (row_points[2][:, None] - col_points[2][None, :]) ** 2
    scaled = jnp.sqrt(spread) * 0.5
    remain = jnp.maximum(1.0 - scaled, 0.0)
    return remain * remain * remain * remain * (4.0 * scaled + 1.0)


def block_ends(blocks, live_count):
    tail_index = live_count - 2 + jnp.arange(2, dtype=jnp.int32)
    tail_flags = (tail_index >= 0).astype(jnp.float32)
    padded = jnp.pad(blocks, ((0, 0), (2, 0), (0, 0)))
    tail_blocks = lax.dynamic_slice_in_dim(padded, live_count, 2, axis=1)
    head_flags = (jnp.arange(2, dtype=jnp.int32) < live_count).astype(jnp.float32)
    return (tail_blocks, tail_flags, blocks[:, :2], head_flags)


def join_left(nearer, farther, pick):
    return jnp.stack([jnp.where(pick, nearer[:, 0], farther[:, 1]), nearer[:, 1]], axis=1)


def join_right(nearer, farther, pick):
    return jnp.stack([nearer[:, 0], jnp.where(pick, nearer[:, 1], farther[:, 0])], axis=1)


def extend(own_blocks, left_pair, right_pair, live_count):
    padded = jnp.concatenate([left_pair, own_blocks, jnp.zeros_like(left_pair)], axis=1)
    return lax.dynamic_update_slice_in_dim(padded, right_pair, live_count + 2, axis=1)


def shifted(block, axes, distance):
    devices = range(lax.axis_size(axes))
    route = [(i - distance, i) for i in devices if i - distance in devices]
    return lax.ppermute(block, axes, route)


def iterate_with_reductions(axes, wing_jitter, live_blocks, smoothing, displacement, fluid_jitter):
    block_count = wing_jitter.shape[1] // BLK
    fluid_count = fluid_jitter.shape[1] // BLK
    live_count = live_blocks[0]
    factors = jnp.array(stretch_factors, jnp.float32)[:, None, None]
    own_points = wing_jitter.reshape(3, block_count, BLK) * factors
    own_flags = (jnp.arange(block_count, dtype=jnp.int32) < live_count).astype(jnp.float32)
    ends_of = {}
    neighbour_counts = {}
    for offset in (1, 2, -1, -2):
        points, counts = shifted((own_points, live_blocks), axes, offset)
        tail_blocks, tail_flags, head_blocks, head_flags = block_ends(points, counts[0])
        neighbour_counts[offset] = counts[0]
        ends_of[offset] = (tail_blocks, tail_flags) if offset > 0 else (head_blocks, head_flags)
    left_pick = ends_of[1][1][0] > 0
    right_pick = ends_of[-1][1][1] > 0
    left_points = join_left(ends_of[1][0], ends_of[2][0], left_pick)
    right_points = join_right(ends_of[-1][0], ends_of[-2][0], right_pick)
    left_flags = join_left(ends_of[1][1][None, :, None], ends_of[2][1][None, :, None], left_pick)
    right_flags = join_right(
        ends_of[-1][1][None, :, None], ends_of[-2][1][None, :, None], right_pick
    )
    ext_points = extend(own_points, left_points, right_points, live_count)
    ext_flags = extend(own_flags[None, :, None], left_flags, right_flags, live_count)
    ext_along = jnp.arange(block_count + 4, dtype=jnp.float32) - 2.0
    ext_points = ext_points.at[0].add(ext_along[:, None]).reshape(3, -1)
    col_flags = jnp.broadcast_to(ext_flags[0], (block_count + 4, BLK)).reshape(-1)
    row_points = (
        own_points.at[0].add(jnp.arange(block_count, dtype=jnp.float32)[:, None]).reshape(3, -1)
    )
    row_mask = jnp.repeat(own_flags, BLK)
    diagonal = 1.0 + smoothing

    def value_context(blocks):
        pieces = {}
        for offset in (1, 2, -1, -2):
            moved = shifted(blocks, axes, offset)
            tail_part, _, head_part, _ = block_ends(moved, neighbour_counts[offset])
            pieces[offset] = tail_part if offset > 0 else head_part
        left_values = join_left(pieces[1], pieces[2], left_pick)
        right_values = join_right(pieces[-1], pieces[-2], right_pick)
        return extend(blocks, left_values, right_values, live_count).reshape(3, -1)

    def apply(vector):
        ext_values = value_context(vector.reshape(3, block_count, BLK))

        def row_group(group):
            first_row = group * (2 * BLK)
            points = lax.dynamic_slice_in_dim(row_points, first_row, 2 * BLK, 1)
            col_points = lax.dynamic_slice_in_dim(ext_points, first_row, 6 * BLK, 1)
            flags = lax.dynamic_slice_in_dim(col_flags, first_row, 6 * BLK, 0)
            kernel = wendland(points, col_points) * flags[None, :]
            col_values = lax.dynamic_slice_in_dim(ext_values, first_row, 6 * BLK, 1)
            return jnp.einsum("cj,ij->ci", col_values, kernel, precision=lax.Precision.HIGHEST)

        result = lax.map(row_group, jnp.arange(block_count // 2, dtype=jnp.int32))
        result = result.transpose(1, 0, 2).reshape(3, -1)
        return result * row_mask + smoothing * vector

    def total(left, right):
        return lax.psum(jnp.sum(left * right, axis=1), axes)

    rhs = displacement * row_mask
    coefs = jnp.zeros_like(rhs)
    residual = rhs
    direction = precond = residual / diagonal
    norm_now = total(residual, precond)
    for iteration in range(ITERS):
        image = apply(direction)
        step_size = norm_now / total(direction, image)
        coefs = coefs + step_size[:, None] * direction
        residual = residual - step_size[:, None] * image
        if iteration + 1 < ITERS:
            precond = residual / diagonal
            norm_next = total(residual, precond)
            direction = precond + (norm_next / norm_now)[:, None] * direction
            norm_now = norm_next
    anchors = jnp.arange(fluid_count, dtype=jnp.int32) * live_count // fluid_count
    fluid_points = fluid_jitter.reshape(3, fluid_count, BLK) * factors
    fluid_points = fluid_points.at[0].add(anchors.astype(jnp.float32)[:, None])
    coef_ext = value_context(coefs.reshape(3, block_count, BLK))

    def fluid_block(points_and_anchor):
        points, anchor = points_and_anchor
        start_col = anchor * BLK
        col_points = lax.dynamic_slice_in_dim(ext_points, start_col, 5 * BLK, 1)
        flags = lax.dynamic_slice_in_dim(col_flags, start_col, 5 * BLK, 0)
        kernel = wendland(points, col_points) * flags[None, :]
        col_values = lax.dynamic_slice_in_dim(coef_ext, start_col, 5 * BLK, 1)
        return jnp.einsum("cj,ij->ci", col_values, kernel, precision=lax.Precision.HIGHEST)

    fluid_values = lax.map(fluid_block, (fluid_points.transpose(1, 0, 2), anchors))
    fluid_values = fluid_values.transpose(1, 0, 2).reshape(3, -1)
    return (coefs, residual, fluid_values)


def along_chips(values, axes, chips):
    count = lax.axis_size(axes)
    route = [(i, i + 2 * chips * (1 - 2 * (i % 2))) for i in range(count)]
    return lax.ppermute(values, axes, [(i, j) for i, j in route if 0 <= j < count])


def per_device(axes, wing_jitter, live_blocks, smoothing, displacement, fluid_jitter):
    block_count = wing_jitter.shape[1] // BLK
    fluid_count = fluid_jitter.shape[1] // BLK
    width = block_count + 2 * HALO
    smoothing_row = smoothing.reshape(1, -1)
    in_smem = pl.BlockSpec(memory_space=pltpu.SMEM)
    in_vmem = pl.BlockSpec(memory_space=pltpu.VMEM)

    def floats(*shape):
        return jax.ShapeDtypeStruct(shape, jnp.float32)

    small = pltpu.CompilerParams(vmem_limit_bytes=8 * 2**20)
    ends = pl.pallas_call(
        pack_kernel,
        out_shape=floats(2, HALO, 8, BLK),
        in_specs=[in_smem] + [in_vmem] * 3,
        out_specs=in_vmem,
        compiler_params=small,
    )(live_blocks, wing_jitter, smoothing_row, displacement)

    def join(near, far, end=False):
        return pl.pallas_call(
            functools.partial(join_kernel, axes, end),
            out_shape=floats(HALO, 8, BLK),
            in_specs=[in_vmem] * 2,
            out_specs=in_vmem,
            scratch_shapes=[pltpu.VMEM((3 * HALO, 8, BLK), jnp.float32)],
            compiler_params=small,
        )(near, far)

    cores = [(i, i ^ 1) for i in range(lax.axis_size(axes))]
    partner = lax.ppermute(ends, axes, cores)
    chip = join(partner, ends, end=True)
    next_chip = along_chips(chip, axes, 1)
    beyond = along_chips(join(chip, next_chip), axes, 2)
    mine = join(next_chip, beyond)
    other = lax.ppermute(mine, axes, cores)

    vectors = pltpu.VMEM((width, 8, BLK), jnp.float32)
    pairs = pltpu.VMEM((width, 16, BLK), jnp.bfloat16)
    joined = pltpu.VMEM((2 * BASE + block_count, 8, BLK), jnp.float32)
    source = pltpu.VMEM((width, BLK, PIECES), jnp.bfloat16)
    basis, moments = pl.pallas_call(
        functools.partial(chain_kernel, axes, block_count),
        out_shape=(floats(3, width, 8, BLK), floats(lax.axis_size(axes), BLK)),
        in_specs=[in_smem] + [in_vmem] * 6,
        out_specs=(in_vmem,) * 2,
        scratch_shapes=[
            joined,
            source,
            *[vectors] * 7,
            *[pairs] * 3,
            pltpu.VMEM((block_count + 2 * NEAR, 5 * BLK, 2 * BLK), jnp.bfloat16),
        ],
        compiler_params=pltpu.CompilerParams(vmem_limit_bytes=48 * 2**20),
    )(live_blocks, wing_jitter, smoothing_row, displacement, partner, mine, other)
    moments = lax.all_to_all(moments, axes, 0, 0, tiled=True)
    fluid_basis = pl.pallas_call(
        functools.partial(fluid_kernel, axes, fluid_count),
        out_shape=floats(fluid_count, 3, 8, BLK),
        in_specs=[in_smem] + [in_vmem] * 8,
        out_specs=in_vmem,
        scratch_shapes=[
            joined,
            source,
            *[pairs] * 3,
            pltpu.VMEM((fluid_count, 5 * BLK, 2 * BLK), jnp.bfloat16),
        ],
        compiler_params=pltpu.CompilerParams(vmem_limit_bytes=24 * 2**20),
        cost_estimate=pl.CostEstimate(flops=6 * 10**9, bytes_accessed=10**7, transcendentals=2 * 10**6),
    )(live_blocks, wing_jitter, smoothing_row, displacement, fluid_jitter, partner, mine, other, basis)
    coefs, residual, fluid_values, good = pl.pallas_call(
        functools.partial(finish_kernel, block_count, fluid_count),
        out_shape=(
            floats(3, block_count * BLK),
            floats(3, block_count * BLK),
            floats(3, fluid_count * BLK),
            jax.ShapeDtypeStruct((1,), jnp.int32),
        ),
        in_specs=[in_smem] + [in_vmem] * 5,
        out_specs=(in_vmem, in_vmem, in_vmem, in_smem),
        compiler_params=small,
    )(live_blocks, moments, smoothing_row, displacement, basis, fluid_basis)
    return lax.cond(
        good[0] == 1,
        lambda: (coefs, residual, fluid_values),
        lambda: iterate_with_reductions(
            axes, wing_jitter, live_blocks, smoothing, displacement, fluid_jitter
        ),
    )


def solution(mesh):
    placed = (P(None, "dom"), P("dom"), P("dom"), P(None, "dom"), P(None, "dom"))
    return jax.shard_map(
        functools.partial(per_device, "dom"),
        mesh=mesh,
        in_specs=placed,
        out_specs=(P(None, "dom"),) * 3,
        check_vma=False,
    )
```

```python
import functools
import jax
import jax.numpy as jnp
from jax import lax
from jax.experimental import pallas as pl
from jax.experimental.pallas import tpu as pltpu
from jax.sharding import PartitionSpec as P

BLK = 128
ITERS = 3
HALO = 6
BASE = 2 * HALO
PIECES = 48
MAX_AMPLIFICATION = 50.0
MOMENTS = 2 * ITERS + 1
GROUP = 8
APPLY_UNROLL = 16

stretch_factors = (1.0, 6.0, 6.0)


def pack_kernel(live_ref, jitter_ref, smoothing_ref, displacement_ref, ends_ref):
    live = live_ref[0]
    count = jnp.full((1, BLK), jnp.minimum(live, HALO), jnp.int32).astype(jnp.float32)
    for slot in range(HALO):
        tail_block = live - HALO + slot
        tail_start = pl.multiple_of(jnp.maximum(tail_block, 0) * BLK, BLK)
        starts = ((tail_block >= 0, tail_start), (slot < live, slot * BLK))
        for end, (kept, start) in enumerate(starts):
            lanes = pl.ds(start, BLK)
            mask = kept.astype(jnp.float32)
            ends_ref[end, slot, 0:3, :] = jitter_ref[:, lanes] * mask
            ends_ref[end, slot, 3:4, :] = smoothing_ref[:, lanes] * mask
            ends_ref[end, slot, 4:7, :] = displacement_ref[:, lanes] * mask
            ends_ref[end, slot, 7:8, :] = count


def count_in(row):
    return jnp.max(row).astype(jnp.int32)


def join_kernel(axes, end, near_ref, far_ref, joined_ref, buffer):
    core = lax.rem(lax.axis_index(axes), 2)
    near = near_ref[core] if end else near_ref[...]
    far = far_ref[core] if end else far_ref[...]
    count = near[0, 7:8, :] + far[0, 7:8, :]
    held = count_in(near[0, 7:8, :])
    buffer[pl.ds(HALO, HALO)] = near
    buffer[pl.ds(HALO + jnp.where(core == 0, -held, held), HALO)] = far
    joined_ref[...] = buffer[pl.ds(HALO, HALO)]
    for slot in range(HALO):
        joined_ref[slot, 7:8, :] = jnp.minimum(count, float(HALO))


def split(values):
    high = values.astype(jnp.bfloat16).astype(jnp.float32)
    rest = values - high
    middle = rest.astype(jnp.bfloat16).astype(jnp.float32)
    return high, middle, rest - middle


def rows_of(row):
    return lax.broadcasted_iota(jnp.int32, (8, BLK), 0) == row


def centred(jitter):
    row = lax.broadcasted_iota(jnp.int32, (8, BLK), 0)
    scale = jnp.where(row == 0, 2.0, 12.0)
    shift = jnp.where(row == 0, 1.0, 6.0)
    return jnp.where(row < 3, jitter * scale - shift, 0.0)


def source_rows(points, norm):
    row = lax.broadcasted_iota(jnp.int32, (8, BLK), 0)
    extended = jnp.where(row >= 4, 1.0, points)
    extended = jnp.where(row == 3, norm, jnp.where(row == 5, points[0:1], extended))
    high, middle, low = split(extended)
    return jnp.concatenate([high, high, middle, high, low, middle], axis=0)


def target_values(points, norm):
    return jnp.where(rows_of(4), norm, -2.0 * points)


def target_groups(values):
    high, middle, low = split(values)
    bases = (jnp.where(rows_of(3), 1.0, high), middle, low)
    slopes = [jnp.where(rows_of(6), 2.0 * piece[0:1], 0.0) for piece in (high, middle, low)]
    slopes[0] = jnp.where(rows_of(5), 4.0, slopes[0])
    return bases, slopes


def target_rows(groups, delta):
    bases, slopes = groups
    if delta:
        bases = [base + float(delta) * slope for base, slope in zip(bases, slopes)]
        bases[0] = jnp.where(rows_of(7), 4.0 * delta * delta, bases[0])
    first = jnp.concatenate([bases[0], bases[1]], axis=0).astype(jnp.bfloat16)
    second = jnp.concatenate([bases[0], bases[2]], axis=0).astype(jnp.bfloat16)
    return jnp.concatenate([first, second, first], axis=0)


PHI_SCALE = 256.0


def wendland_scaled(distances):
    distances = jnp.maximum(distances, 1e-30)
    scaled = distances * lax.rsqrt(distances)
    remain = jnp.maximum(4.0 - scaled, 0.0)
    square = remain * remain
    return square * square * (scaled + 1.0)


def store_pair(ref, values, first_row):
    high = values.astype(jnp.bfloat16)
    low = (values - high.astype(jnp.float32)).astype(jnp.bfloat16)
    ref[pl.ds(first_row, BLK), 0:BLK] = high
    ref[pl.ds(first_row, BLK), BLK : 2 * BLK] = low


def vector_pair(values):
    values = values * (1.0 / PHI_SCALE)
    high = values.astype(jnp.bfloat16).astype(jnp.float32)
    return jnp.concatenate([high, values - high], axis=0).astype(jnp.bfloat16)


def sum_pairs(product, first):
    upper = product[first : first + 8] + product[first + 8 : first + 16]
    return upper[:, :BLK] + upper[:, BLK:]


def join_chain(axes, live, jitter_ref, smoothing_ref, displacement_ref, partner_ref, mine_ref, other_ref, joined):
    block_count = jitter_ref.shape[1] // BLK
    for extra in range(HALO):
        joined[BASE + block_count + extra] = jnp.zeros((8, BLK), jnp.float32)

    def put_own(block, carry):
        lanes = pl.ds(pl.multiple_of(block * BLK, BLK), BLK)
        kept = (block < live).astype(jnp.float32)
        joined[BASE + block, 0:3, :] = jitter_ref[:, lanes]
        joined[BASE + block, 3:4, :] = smoothing_ref[:, lanes] * kept
        joined[BASE + block, 4:7, :] = displacement_ref[:, lanes]
        return carry

    lax.fori_loop(0, block_count, put_own, 0, unroll=8)
    core = lax.rem(lax.axis_index(axes), 2)
    mine, other = mine_ref[...], other_ref[...]
    left_near = jnp.where(core == 0, 0, count_in(partner_ref[0, 0, 7:8, :]))
    right_near = jnp.where(core == 0, count_in(partner_ref[1, 0, 7:8, :]), 0)
    joined[pl.ds(BASE - HALO, HALO)] = partner_ref[0]
    joined[pl.ds(BASE - HALO - left_near, HALO)] = jnp.where(core == 0, mine, other)
    joined[pl.ds(BASE + live, HALO)] = partner_ref[1]
    joined[pl.ds(BASE + live + right_near, HALO)] = jnp.where(core == 0, other, mine)


def parts_of(packed):
    points = centred(packed)
    norm = jnp.sum(points * points, axis=0, keepdims=True)
    inverse = jnp.where(packed[3:4] > 0.0, 1.0 / (1.0 + packed[3:4]), 0.0)
    rhs = jnp.concatenate([packed[4:7], jnp.zeros((5, BLK), jnp.float32)], axis=0)
    return points, norm, jnp.broadcast_to(inverse, (8, BLK)), rhs


def source_of(points, norm):
    return jnp.transpose(source_rows(points, norm)).astype(jnp.bfloat16)


def chain_kernel(
    axes, block_count,
    live_ref, jitter_ref, smoothing_ref, displacement_ref, partner_ref, mine_ref, other_ref,
    basis_ref, moments_ref,
    joined, source, target, inverse, w0, z0, z1, z2, b0, b1, b2, matrix,
):
    w1_ref, w2_ref, w3_ref = (basis_ref.at[k] for k in range(3))
    live = live_ref[0]
    width = block_count + 2 * HALO
    join_chain(
        axes, live, jitter_ref, smoothing_ref, displacement_ref, partner_ref, mine_ref, other_ref, joined
    )

    def prepare(block, carry):
        points, norm, scale, rhs = parts_of(joined[BASE - HALO + block])
        source[block] = source_of(points, norm)
        target[block] = target_values(points, norm)
        inverse[block] = scale
        w0[block] = rhs
        z0[block] = rhs * scale
        b0[block] = vector_pair(rhs * scale)
        return carry

    lax.fori_loop(0, width, prepare, 0, unroll=4)


    def generate_two(block):
        first, second = target_groups(target[block]), target_groups(target[block + 1])
        for place in range(4):
            columns = []
            if place < 3:
                columns.append(target_rows(first, place))
            if place > 0:
                columns.append(target_rows(second, place - 1))
            distances = jnp.dot(
                source[block + place],
                jnp.concatenate(columns, axis=1),
                preferred_element_type=jnp.float32,
            )
            values = wendland_scaled(distances)
            if place < 3:
                store_pair(matrix.at[block], values[:, :BLK], place * BLK)
            if place > 0:
                store_pair(matrix.at[block + 1], values[:, -BLK:], (place - 1) * BLK)

    def apply_row(block, values, pairs, place_next):
        near = jnp.concatenate([pairs[block + place] for place in range(3)], axis=1)
        product = jnp.dot(near, matrix[block], preferred_element_type=jnp.float32)
        image = sum_pairs(product, 0) - values[block]
        for back in (1, 2):
            behind = pairs[block - back]
            product = lax.dot_general(
                jnp.concatenate([behind, behind], axis=1),
                matrix[block - back, back * BLK : (back + 1) * BLK, :],
                (((1,), (1,)), ((), ())),
                preferred_element_type=jnp.float32,
            )
            image = image + (product[0:8] + product[8:16])
        place_next(block, image)

    def apply(values, pairs, first, last, place_next):
        def one_row(block, carry):
            apply_row(block, values, pairs, place_next)
            return carry

        lax.fori_loop(first, last, one_row, 0, unroll=APPLY_UNROLL)

    def first_next(block, image):
        scaled = image * inverse[block]
        z1[block] = scaled
        b1[block] = vector_pair(scaled)
        w1_ref[block] = image

    def second_next(block, image):
        scaled = image * inverse[block]
        z2[block] = scaled
        b2[block] = vector_pair(scaled)
        w2_ref[block] = image

    def third_next(block, image):
        w3_ref[block] = image

    def generate_group(group):
        for row in range(0, GROUP, 2):
            generate_two(2 + group * GROUP + row)

    def apply_group(group):
        for row in range(GROUP):
            apply_row(2 + group * GROUP + row, z0, b0, first_next)

    def apply_then_generate(group, carry):
        apply_group(group - 1)
        generate_group(group)
        return carry

    groups = (width - 4) // GROUP
    generate_two(0)
    generate_group(0)
    lax.fori_loop(1, groups, apply_then_generate, 0)
    apply_group(groups - 1)
    apply(z1, b1, 4, width - 4, second_next)
    apply(z2, b2, 6, width - 6, third_next)

    def add_up(own, sums):
        block = own + HALO
        kept = (own < live).astype(jnp.float32)
        third = w3_ref[block]
        pairs = (
            (z0[block], w0[block]),
            (z0[block], w1_ref[block]),
            (z1[block], w1_ref[block]),
            (z1[block], w2_ref[block]),
            (z2[block], w2_ref[block]),
            (z2[block], third),
            (third * inverse[block], third),
        )
        return tuple(s + kept * (a * b) for s, (a, b) in zip(sums, pairs))

    zero = jnp.zeros((8, BLK), jnp.float32)
    sums = lax.fori_loop(0, block_count, add_up, (zero,) * MOMENTS, unroll=4)
    lane = lax.broadcasted_iota(jnp.int32, (8, BLK), 1)
    row = lax.broadcasted_iota(jnp.int32, (8, BLK), 0)
    moments = zero
    for k in range(MOMENTS):
        moments = jnp.where(lane == 8 * row + k, jnp.sum(sums[k], axis=1, keepdims=True), moments)
    moments = jnp.sum(moments, axis=0, keepdims=True)
    moments_ref[...] = jnp.broadcast_to(moments, moments_ref.shape)


def fluid_kernel(
    axes, fluid_count,
    live_ref, jitter_ref, smoothing_ref, displacement_ref, fluid_ref, partner_ref, mine_ref, other_ref,
    basis_ref,
    fluid_basis_ref,
    joined, source, b0, b1, b2, matrix,
):
    live = live_ref[0]
    width = jitter_ref.shape[1] // BLK + 2 * HALO
    join_chain(
        axes, live, jitter_ref, smoothing_ref, displacement_ref, partner_ref, mine_ref, other_ref, joined
    )

    def prepare(block, carry):
        points, norm, scale, rhs = parts_of(joined[BASE - HALO + block])
        source[block] = source_of(points, norm)
        b0[block] = vector_pair(rhs * scale)
        b1[block] = vector_pair(basis_ref[0, block] * scale)
        b2[block] = vector_pair(basis_ref[1, block] * scale)
        return carry

    lax.fori_loop(HALO - 2, width - HALO + 2, prepare, 0, unroll=4)

    def anchor_of(index):
        return lax.div(index * live, jnp.int32(fluid_count))

    def generate_fluid(index, carry):
        lanes = pl.ds(pl.multiple_of(index * BLK, BLK), BLK)
        jitter = jnp.concatenate([fluid_ref[:, lanes], jnp.zeros((5, BLK), jnp.float32)], axis=0)
        points = centred(jitter)
        norm = jnp.sum(points * points, axis=0, keepdims=True)
        groups = target_groups(target_values(points, norm))
        first = anchor_of(index) + (HALO - 2)
        for place in range(5):
            columns = target_rows(groups, place - 2)
            distances = jnp.dot(source[first + place], columns, preferred_element_type=jnp.float32)
            store_pair(matrix.at[index], wendland_scaled(distances), place * BLK)
        return carry

    def apply_fluid(index, carry):
        first = anchor_of(index) + (HALO - 2)
        near = [
            jnp.concatenate([ref[first + place] for place in range(5)], axis=1)
            for ref in (b0, b1, b2)
        ]
        near = jnp.concatenate(near, axis=0)
        product = jnp.dot(near, matrix[index], preferred_element_type=jnp.float32)
        for k in range(3):
            fluid_basis_ref[index, k] = sum_pairs(product, 16 * k)
        return carry

    lax.fori_loop(0, fluid_count, generate_fluid, 0, unroll=4)
    lax.fori_loop(0, fluid_count, apply_fluid, 0, unroll=4)


def step_coefficients(moments):
    def inner(left, right):
        total = 0.0
        for i, a in enumerate(left):
            for j, b in enumerate(right):
                total = total + a * b * moments[i + j]
        return total

    one = jnp.ones_like(moments[0])
    solution_part, residual, direction = [], [one], [one]
    norm = moments[0]
    for iteration in range(ITERS):
        image = [
            (direction[k] if k < len(direction) else 0.0) + (direction[k - 1] if k else 0.0)
            for k in range(len(direction) + 1)
        ]
        step = norm / inner(direction, image)
        old = solution_part + [0.0] * (len(direction) - len(solution_part))
        solution_part = [a + step * b for a, b in zip(old, direction)]
        residual = [
            (residual[k] if k < len(residual) else 0.0) - step * image[k] for k in range(len(image))
        ]
        following = inner(residual, residual)
        ratio = following / norm
        direction = [
            residual[k] + ratio * (direction[k] if k < len(direction) else 0.0)
            for k in range(len(residual))
        ]
        norm = following
    spread = 0.0
    for k, a in enumerate(residual):
        spread = spread + jnp.abs(a) * jnp.sqrt(jnp.maximum(moments[2 * k], 0.0))
    return solution_part, residual, spread * spread <= MAX_AMPLIFICATION**2 * norm


def finish_kernel(
    block_count, fluid_count, live_ref, moments_ref, smoothing_ref, displacement_ref,
    basis_ref, fluid_basis_ref, coefs_ref, residual_ref, fluid_ref, good_ref,
):
    live = live_ref[0]
    row = lax.broadcasted_iota(jnp.int32, (8, BLK), 0)
    lane = lax.broadcasted_iota(jnp.int32, (8, BLK), 1)
    summed = jnp.broadcast_to(jnp.sum(moments_ref[...], axis=0, keepdims=True), (8, BLK))
    moments = [
        jnp.sum(jnp.where(lane == 8 * row + k, summed, 0.0), axis=1, keepdims=True)
        for k in range(MOMENTS)
    ]
    solved, left, good = step_coefficients(moments)
    row = lax.broadcasted_iota(jnp.int32, (8, 1), 0)
    good_ref[0] = jnp.min(jnp.where(good | (row > 2), 1.0, 0.0)).astype(jnp.int32)
    solved = [jnp.broadcast_to(v, (8, BLK))[0:3] for v in solved]
    left = [jnp.broadcast_to(v, (8, BLK))[0:3] for v in left]

    def one_block(own, carry):
        lanes = pl.ds(pl.multiple_of(own * BLK, BLK), BLK)
        block = own + HALO
        parts = [displacement_ref[:, lanes]] + [basis_ref[k, block][0:3] for k in range(3)]
        scaled = sum(a * b for a, b in zip(solved, parts)) / (1.0 + smoothing_ref[:, lanes])
        remaining = sum(a * b for a, b in zip(left, parts))
        is_live = own < live
        coefs_ref[:, lanes] = jnp.where(is_live, scaled, 0.0)
        residual_ref[:, lanes] = jnp.where(is_live, remaining, 0.0)
        return carry

    lax.fori_loop(0, block_count, one_block, 0, unroll=4)

    def one_fluid(index, carry):
        lanes = pl.ds(pl.multiple_of(index * BLK, BLK), BLK)
        fluid_ref[:, lanes] = sum(a * fluid_basis_ref[index, k][0:3] for k, a in enumerate(solved))
        return carry

    lax.fori_loop(0, fluid_count, one_fluid, 0, unroll=4)


def wendland(row_points, col_points):
    spread = (row_points[0][:, None] - col_points[0][None, :]) ** 2
    spread = spread + (row_points[1][:, None] - col_points[1][None, :]) ** 2
    spread = spread + (row_points[2][:, None] - col_points[2][None, :]) ** 2
    scaled = jnp.sqrt(spread) * 0.5
    remain = jnp.maximum(1.0 - scaled, 0.0)
    return remain * remain * remain * remain * (4.0 * scaled + 1.0)


def block_ends(blocks, live_count):
    tail_index = live_count - 2 + jnp.arange(2, dtype=jnp.int32)
    tail_flags = (tail_index >= 0).astype(jnp.float32)
    padded = jnp.pad(blocks, ((0, 0), (2, 0), (0, 0)))
    tail_blocks = lax.dynamic_slice_in_dim(padded, live_count, 2, axis=1)
    head_flags = (jnp.arange(2, dtype=jnp.int32) < live_count).astype(jnp.float32)
    return (tail_blocks, tail_flags, blocks[:, :2], head_flags)


def join_left(nearer, farther, pick):
    return jnp.stack([jnp.where(pick, nearer[:, 0], farther[:, 1]), nearer[:, 1]], axis=1)


def join_right(nearer, farther, pick):
    return jnp.stack([nearer[:, 0], jnp.where(pick, nearer[:, 1], farther[:, 0])], axis=1)


def extend(own_blocks, left_pair, right_pair, live_count):
    padded = jnp.concatenate([left_pair, own_blocks, jnp.zeros_like(left_pair)], axis=1)
    return lax.dynamic_update_slice_in_dim(padded, right_pair, live_count + 2, axis=1)


def shifted(block, axes, distance):
    devices = range(lax.axis_size(axes))
    route = [(i - distance, i) for i in devices if i - distance in devices]
    return lax.ppermute(block, axes, route)


def iterate_with_reductions(axes, wing_jitter, live_blocks, smoothing, displacement, fluid_jitter):
    block_count = wing_jitter.shape[1] // BLK
    fluid_count = fluid_jitter.shape[1] // BLK
    live_count = live_blocks[0]
    factors = jnp.array(stretch_factors, jnp.float32)[:, None, None]
    own_points = wing_jitter.reshape(3, block_count, BLK) * factors
    own_flags = (jnp.arange(block_count, dtype=jnp.int32) < live_count).astype(jnp.float32)
    ends_of = {}
    neighbour_counts = {}
    for offset in (1, 2, -1, -2):
        points, counts = shifted((own_points, live_blocks), axes, offset)
        tail_blocks, tail_flags, head_blocks, head_flags = block_ends(points, counts[0])
        neighbour_counts[offset] = counts[0]
        ends_of[offset] = (tail_blocks, tail_flags) if offset > 0 else (head_blocks, head_flags)
    left_pick = ends_of[1][1][0] > 0
    right_pick = ends_of[-1][1][1] > 0
    left_points = join_left(ends_of[1][0], ends_of[2][0], left_pick)
    right_points = join_right(ends_of[-1][0], ends_of[-2][0], right_pick)
    left_flags = join_left(ends_of[1][1][None, :, None], ends_of[2][1][None, :, None], left_pick)
    right_flags = join_right(
        ends_of[-1][1][None, :, None], ends_of[-2][1][None, :, None], right_pick
    )
    ext_points = extend(own_points, left_points, right_points, live_count)
    ext_flags = extend(own_flags[None, :, None], left_flags, right_flags, live_count)
    ext_along = jnp.arange(block_count + 4, dtype=jnp.float32) - 2.0
    ext_points = ext_points.at[0].add(ext_along[:, None]).reshape(3, -1)
    col_flags = jnp.broadcast_to(ext_flags[0], (block_count + 4, BLK)).reshape(-1)
    row_points = (
        own_points.at[0].add(jnp.arange(block_count, dtype=jnp.float32)[:, None]).reshape(3, -1)
    )
    row_mask = jnp.repeat(own_flags, BLK)
    diagonal = 1.0 + smoothing

    def value_context(blocks):
        pieces = {}
        for offset in (1, 2, -1, -2):
            moved = shifted(blocks, axes, offset)
            tail_part, _, head_part, _ = block_ends(moved, neighbour_counts[offset])
            pieces[offset] = tail_part if offset > 0 else head_part
        left_values = join_left(pieces[1], pieces[2], left_pick)
        right_values = join_right(pieces[-1], pieces[-2], right_pick)
        return extend(blocks, left_values, right_values, live_count).reshape(3, -1)

    def apply(vector):
        ext_values = value_context(vector.reshape(3, block_count, BLK))

        def row_group(group):
            first_row = group * (2 * BLK)
            points = lax.dynamic_slice_in_dim(row_points, first_row, 2 * BLK, 1)
            col_points = lax.dynamic_slice_in_dim(ext_points, first_row, 6 * BLK, 1)
            flags = lax.dynamic_slice_in_dim(col_flags, first_row, 6 * BLK, 0)
            kernel = wendland(points, col_points) * flags[None, :]
            col_values = lax.dynamic_slice_in_dim(ext_values, first_row, 6 * BLK, 1)
            return jnp.einsum("cj,ij->ci", col_values, kernel, precision=lax.Precision.HIGHEST)

        result = lax.map(row_group, jnp.arange(block_count // 2, dtype=jnp.int32))
        result = result.transpose(1, 0, 2).reshape(3, -1)
        return result * row_mask + smoothing * vector

    def total(left, right):
        return lax.psum(jnp.sum(left * right, axis=1), axes)

    rhs = displacement * row_mask
    coefs = jnp.zeros_like(rhs)
    residual = rhs
    direction = precond = residual / diagonal
    norm_now = total(residual, precond)
    for iteration in range(ITERS):
        image = apply(direction)
        step_size = norm_now / total(direction, image)
        coefs = coefs + step_size[:, None] * direction
        residual = residual - step_size[:, None] * image
        if iteration + 1 < ITERS:
            precond = residual / diagonal
            norm_next = total(residual, precond)
            direction = precond + (norm_next / norm_now)[:, None] * direction
            norm_now = norm_next
    anchors = jnp.arange(fluid_count, dtype=jnp.int32) * live_count // fluid_count
    fluid_points = fluid_jitter.reshape(3, fluid_count, BLK) * factors
    fluid_points = fluid_points.at[0].add(anchors.astype(jnp.float32)[:, None])
    coef_ext = value_context(coefs.reshape(3, block_count, BLK))

    def fluid_block(points_and_anchor):
        points, anchor = points_and_anchor
        start_col = anchor * BLK
        col_points = lax.dynamic_slice_in_dim(ext_points, start_col, 5 * BLK, 1)
        flags = lax.dynamic_slice_in_dim(col_flags, start_col, 5 * BLK, 0)
        kernel = wendland(points, col_points) * flags[None, :]
        col_values = lax.dynamic_slice_in_dim(coef_ext, start_col, 5 * BLK, 1)
        return jnp.einsum("cj,ij->ci", col_values, kernel, precision=lax.Precision.HIGHEST)

    fluid_values = lax.map(fluid_block, (fluid_points.transpose(1, 0, 2), anchors))
    fluid_values = fluid_values.transpose(1, 0, 2).reshape(3, -1)
    return (coefs, residual, fluid_values)


def along_chips(values, axes, chips):
    count = lax.axis_size(axes)
    route = [(i, i + 2 * chips * (1 - 2 * (i % 2))) for i in range(count)]
    return lax.ppermute(values, axes, [(i, j) for i, j in route if 0 <= j < count])


def per_device(axes, wing_jitter, live_blocks, smoothing, displacement, fluid_jitter):
    block_count = wing_jitter.shape[1] // BLK
    fluid_count = fluid_jitter.shape[1] // BLK
    width = block_count + 2 * HALO
    smoothing_row = smoothing.reshape(1, -1)
    in_smem = pl.BlockSpec(memory_space=pltpu.SMEM)
    in_vmem = pl.BlockSpec(memory_space=pltpu.VMEM)

    def floats(*shape):
        return jax.ShapeDtypeStruct(shape, jnp.float32)

    small = pltpu.CompilerParams(vmem_limit_bytes=8 * 2**20)
    ends = pl.pallas_call(
        pack_kernel,
        out_shape=floats(2, HALO, 8, BLK),
        in_specs=[in_smem] + [in_vmem] * 3,
        out_specs=in_vmem,
        compiler_params=small,
    )(live_blocks, wing_jitter, smoothing_row, displacement)

    def join(near, far, end=False):
        return pl.pallas_call(
            functools.partial(join_kernel, axes, end),
            out_shape=floats(HALO, 8, BLK),
            in_specs=[in_vmem] * 2,
            out_specs=in_vmem,
            scratch_shapes=[pltpu.VMEM((3 * HALO, 8, BLK), jnp.float32)],
            compiler_params=small,
        )(near, far)

    cores = [(i, i ^ 1) for i in range(lax.axis_size(axes))]
    partner = lax.ppermute(ends, axes, cores)
    chip = join(partner, ends, end=True)
    next_chip = along_chips(chip, axes, 1)
    beyond = along_chips(join(chip, next_chip), axes, 2)
    mine = join(next_chip, beyond)
    other = lax.ppermute(mine, axes, cores)

    vectors = pltpu.VMEM((width, 8, BLK), jnp.float32)
    pairs = pltpu.VMEM((width, 16, BLK), jnp.bfloat16)
    joined = pltpu.VMEM((2 * BASE + block_count, 8, BLK), jnp.float32)
    source = pltpu.VMEM((width, BLK, PIECES), jnp.bfloat16)
    basis, moments = pl.pallas_call(
        functools.partial(chain_kernel, axes, block_count),
        out_shape=(floats(3, width, 8, BLK), floats(lax.axis_size(axes), BLK)),
        in_specs=[in_smem] + [in_vmem] * 6,
        out_specs=(in_vmem,) * 2,
        scratch_shapes=[
            joined,
            source,
            *[vectors] * 6,
            *[pairs] * 3,
            pltpu.VMEM((width - 2, 3 * BLK, 2 * BLK), jnp.bfloat16),
        ],
        compiler_params=pltpu.CompilerParams(vmem_limit_bytes=48 * 2**20),
    )(live_blocks, wing_jitter, smoothing_row, displacement, partner, mine, other)
    moments = lax.all_to_all(moments, axes, 0, 0, tiled=True)
    fluid_basis = pl.pallas_call(
        functools.partial(fluid_kernel, axes, fluid_count),
        out_shape=floats(fluid_count, 3, 8, BLK),
        in_specs=[in_smem] + [in_vmem] * 8,
        out_specs=in_vmem,
        scratch_shapes=[
            joined,
            source,
            *[pairs] * 3,
            pltpu.VMEM((fluid_count, 5 * BLK, 2 * BLK), jnp.bfloat16),
        ],
        compiler_params=pltpu.CompilerParams(vmem_limit_bytes=24 * 2**20),
        cost_estimate=pl.CostEstimate(flops=6 * 10**9, bytes_accessed=10**7, transcendentals=2 * 10**6),
    )(live_blocks, wing_jitter, smoothing_row, displacement, fluid_jitter, partner, mine, other, basis)
    coefs, residual, fluid_values, good = pl.pallas_call(
        functools.partial(finish_kernel, block_count, fluid_count),
        out_shape=(
            floats(3, block_count * BLK),
            floats(3, block_count * BLK),
            floats(3, fluid_count * BLK),
            jax.ShapeDtypeStruct((1,), jnp.int32),
        ),
        in_specs=[in_smem] + [in_vmem] * 5,
        out_specs=(in_vmem, in_vmem, in_vmem, in_smem),
        compiler_params=small,
    )(live_blocks, moments, smoothing_row, displacement, basis, fluid_basis)
    return lax.cond(
        good[0] == 1,
        lambda: (coefs, residual, fluid_values),
        lambda: iterate_with_reductions(
            axes, wing_jitter, live_blocks, smoothing, displacement, fluid_jitter
        ),
    )


def solution(mesh):
    placed = (P(None, "dom"), P("dom"), P("dom"), P(None, "dom"), P(None, "dom"))
    return jax.shard_map(
        functools.partial(per_device, "dom"),
        mesh=mesh,
        in_specs=placed,
        out_specs=(P(None, "dom"),) * 3,
        check_vma=False,
    )
```

```python
import functools
import jax
import jax.numpy as jnp
from jax import lax
from jax.experimental import pallas as pl
from jax.experimental.pallas import tpu as pltpu
from jax.sharding import PartitionSpec as P

BLK = 128
ITERS = 3
HALO = 6
BASE = 2 * HALO
PIECES = 48
MAX_AMPLIFICATION = 50.0
MOMENTS = 2 * ITERS + 1
APPLY_UNROLL = 16

stretch_factors = (1.0, 6.0, 6.0)


def pack_kernel(live_ref, jitter_ref, smoothing_ref, displacement_ref, ends_ref):
    live = live_ref[0]
    count = jnp.full((1, BLK), jnp.minimum(live, HALO), jnp.int32).astype(jnp.float32)
    for slot in range(HALO):
        tail_block = live - HALO + slot
        tail_start = pl.multiple_of(jnp.maximum(tail_block, 0) * BLK, BLK)
        starts = ((tail_block >= 0, tail_start), (slot < live, slot * BLK))
        for end, (kept, start) in enumerate(starts):
            lanes = pl.ds(start, BLK)
            mask = kept.astype(jnp.float32)
            ends_ref[end, slot, 0:3, :] = jitter_ref[:, lanes] * mask
            ends_ref[end, slot, 3:4, :] = smoothing_ref[:, lanes] * mask
            ends_ref[end, slot, 4:7, :] = displacement_ref[:, lanes] * mask
            ends_ref[end, slot, 7:8, :] = count


def count_in(row):
    return jnp.max(row).astype(jnp.int32)


def join_kernel(axes, end, near_ref, far_ref, joined_ref, buffer):
    core = lax.rem(lax.axis_index(axes), 2)
    near = near_ref[core] if end else near_ref[...]
    far = far_ref[core] if end else far_ref[...]
    count = near[0, 7:8, :] + far[0, 7:8, :]
    held = count_in(near[0, 7:8, :])
    buffer[pl.ds(HALO, HALO)] = near
    buffer[pl.ds(HALO + jnp.where(core == 0, -held, held), HALO)] = far
    joined_ref[...] = buffer[pl.ds(HALO, HALO)]
    for slot in range(HALO):
        joined_ref[slot, 7:8, :] = jnp.minimum(count, float(HALO))


def split(values):
    high = values.astype(jnp.bfloat16).astype(jnp.float32)
    rest = values - high
    middle = rest.astype(jnp.bfloat16).astype(jnp.float32)
    return high, middle, rest - middle


def rows_of(row):
    return lax.broadcasted_iota(jnp.int32, (8, BLK), 0) == row


def centred(jitter):
    row = lax.broadcasted_iota(jnp.int32, (8, BLK), 0)
    scale = jnp.where(row == 0, 2.0, 12.0)
    shift = jnp.where(row == 0, 1.0, 6.0)
    return jnp.where(row < 3, jitter * scale - shift, 0.0)


def source_rows(points, norm):
    row = lax.broadcasted_iota(jnp.int32, (8, BLK), 0)
    extended = jnp.where(row >= 4, 1.0, points)
    extended = jnp.where(row == 3, norm, jnp.where(row == 5, points[0:1], extended))
    high, middle, low = split(extended)
    return jnp.concatenate([high, high, middle, high, low, middle], axis=0)


def target_values(points, norm):
    return jnp.where(rows_of(4), norm, -2.0 * points)


def target_groups(values):
    high, middle, low = split(values)
    bases = (jnp.where(rows_of(3), 1.0, high), middle, low)
    slopes = [jnp.where(rows_of(6), 2.0 * piece[0:1], 0.0) for piece in (high, middle, low)]
    slopes[0] = jnp.where(rows_of(5), 4.0, slopes[0])
    return bases, slopes


def target_rows(groups, delta):
    bases, slopes = groups
    if delta:
        bases = [base + float(delta) * slope for base, slope in zip(bases, slopes)]
        bases[0] = jnp.where(rows_of(7), 4.0 * delta * delta, bases[0])
    first = jnp.concatenate([bases[0], bases[1]], axis=0).astype(jnp.bfloat16)
    second = jnp.concatenate([bases[0], bases[2]], axis=0).astype(jnp.bfloat16)
    return jnp.concatenate([first, second, first], axis=0)


PHI_SCALE = 256.0


def wendland_scaled(distances):
    distances = jnp.maximum(distances, 1e-30)
    scaled = distances * lax.rsqrt(distances)
    remain = jnp.maximum(4.0 - scaled, 0.0)
    square = remain * remain
    return square * square * (scaled + 1.0)


def store_pair(ref, values, first_row):
    high = values.astype(jnp.bfloat16)
    low = (values - high.astype(jnp.float32)).astype(jnp.bfloat16)
    ref[pl.ds(first_row, BLK), 0:BLK] = high
    ref[pl.ds(first_row, BLK), BLK : 2 * BLK] = low


def vector_pair(values):
    values = values * (1.0 / PHI_SCALE)
    high = values.astype(jnp.bfloat16).astype(jnp.float32)
    return jnp.concatenate([high, values - high], axis=0).astype(jnp.bfloat16)


def sum_pairs(product, first):
    upper = product[first : first + 8] + product[first + 8 : first + 16]
    return upper[:, :BLK] + upper[:, BLK:]


def join_chain(axes, live, jitter_ref, smoothing_ref, displacement_ref, partner_ref, mine_ref, other_ref, joined):
    block_count = jitter_ref.shape[1] // BLK
    for extra in range(HALO):
        joined[BASE + block_count + extra] = jnp.zeros((8, BLK), jnp.float32)

    def put_own(block, carry):
        lanes = pl.ds(pl.multiple_of(block * BLK, BLK), BLK)
        kept = (block < live).astype(jnp.float32)
        joined[BASE + block, 0:3, :] = jitter_ref[:, lanes]
        joined[BASE + block, 3:4, :] = smoothing_ref[:, lanes] * kept
        joined[BASE + block, 4:7, :] = displacement_ref[:, lanes]
        return carry

    lax.fori_loop(0, block_count, put_own, 0, unroll=8)
    core = lax.rem(lax.axis_index(axes), 2)
    mine, other = mine_ref[...], other_ref[...]
    left_near = jnp.where(core == 0, 0, count_in(partner_ref[0, 0, 7:8, :]))
    right_near = jnp.where(core == 0, count_in(partner_ref[1, 0, 7:8, :]), 0)
    joined[pl.ds(BASE - HALO, HALO)] = partner_ref[0]
    joined[pl.ds(BASE - HALO - left_near, HALO)] = jnp.where(core == 0, mine, other)
    joined[pl.ds(BASE + live, HALO)] = partner_ref[1]
    joined[pl.ds(BASE + live + right_near, HALO)] = jnp.where(core == 0, other, mine)


def parts_of(packed):
    points = centred(packed)
    norm = jnp.sum(points * points, axis=0, keepdims=True)
    inverse = jnp.where(packed[3:4] > 0.0, 1.0 / (1.0 + packed[3:4]), 0.0)
    rhs = jnp.concatenate([packed[4:7], jnp.zeros((5, BLK), jnp.float32)], axis=0)
    return points, norm, jnp.broadcast_to(inverse, (8, BLK)), rhs


def source_of(points, norm):
    return jnp.transpose(source_rows(points, norm)).astype(jnp.bfloat16)


def generate_two(source, target, matrix, block, row):
    first, second = target_groups(target[block]), target_groups(target[block + 1])
    for place in range(4):
        columns = []
        if place < 3:
            columns.append(target_rows(first, place))
        if place > 0:
            columns.append(target_rows(second, place - 1))
        distances = jnp.dot(
            source[block + place],
            jnp.concatenate(columns, axis=1),
            preferred_element_type=jnp.float32,
        )
        values = wendland_scaled(distances)
        if place < 3:
            store_pair(matrix.at[row], values[:, :BLK], place * BLK)
        if place > 0:
            store_pair(matrix.at[row + 1], values[:, -BLK:], (place - 1) * BLK)


def own_kernel(first, rows, last, jitter_ref, *refs):
    matrix, source, target = refs[-3:]

    def prepare(block, carry):
        lanes = pl.ds(pl.multiple_of((first + block) * BLK, BLK), BLK)
        jitter = jnp.concatenate([jitter_ref[:, lanes], jnp.zeros((5, BLK), jnp.float32)], axis=0)
        points = centred(jitter)
        norm = jnp.sum(points * points, axis=0, keepdims=True)
        source[block] = source_of(points, norm)
        target[block] = target_values(points, norm)
        return carry

    lax.fori_loop(0, rows + 2, prepare, 0, unroll=4)

    def generate(pair, carry):
        generate_two(source, target, matrix, 2 * pair, HALO + first + 2 * pair)
        return carry

    lax.fori_loop(0, rows // 2, generate, 0, unroll=4)
    if last:
        for row in range(HALO + first + rows, matrix.shape[0]):
            matrix[row] = jnp.zeros(matrix.shape[1:], matrix.dtype)


def chain_kernel(
    axes, block_count,
    live_ref, jitter_ref, smoothing_ref, displacement_ref, partner_ref, mine_ref, other_ref, _,
    basis_ref, moments_ref, matrix,
    joined, source, target, inverse, w0, z0, z1, z2, b0, b1, b2,
):
    w1_ref, w2_ref, w3_ref = (basis_ref.at[k] for k in range(3))
    live = live_ref[0]
    width = block_count + 2 * HALO
    join_chain(
        axes, live, jitter_ref, smoothing_ref, displacement_ref, partner_ref, mine_ref, other_ref, joined
    )

    def prepare(block, carry):
        _, _, scale, rhs = parts_of(joined[BASE - HALO + block])
        inverse[block] = scale
        w0[block] = rhs
        z0[block] = rhs * scale
        b0[block] = vector_pair(rhs * scale)
        return carry

    lax.fori_loop(0, width, prepare, 0, unroll=4)

    for start in (0, live + HALO - 2):
        for block in range(HALO + 2):
            points, norm, _, _ = parts_of(joined[BASE - HALO + start + block])
            source[block] = source_of(points, norm)
            target[block] = target_values(points, norm)
        for row in range(0, HALO, 2):
            generate_two(source, target, matrix, row, start + row)

    def apply_row(block, values, pairs, place_next):
        near = jnp.concatenate([pairs[block + place] for place in range(3)], axis=1)
        product = jnp.dot(near, matrix[block], preferred_element_type=jnp.float32)
        image = sum_pairs(product, 0) - values[block]
        for back in (1, 2):
            behind = pairs[block - back]
            product = lax.dot_general(
                jnp.concatenate([behind, behind], axis=1),
                matrix[block - back, back * BLK : (back + 1) * BLK, :],
                (((1,), (1,)), ((), ())),
                preferred_element_type=jnp.float32,
            )
            image = image + (product[0:8] + product[8:16])
        place_next(block, image)

    def apply(values, pairs, first, last, place_next):
        def one_row(block, carry):
            apply_row(block, values, pairs, place_next)
            return carry

        lax.fori_loop(first, last, one_row, 0, unroll=APPLY_UNROLL)

    def first_next(block, image):
        scaled = image * inverse[block]
        z1[block] = scaled
        b1[block] = vector_pair(scaled)
        w1_ref[block] = image

    def second_next(block, image):
        scaled = image * inverse[block]
        z2[block] = scaled
        b2[block] = vector_pair(scaled)
        w2_ref[block] = image

    def third_next(block, image):
        w3_ref[block] = image

    apply(z0, b0, 2, width - 2, first_next)
    apply(z1, b1, 4, width - 4, second_next)
    apply(z2, b2, 6, width - 6, third_next)

    def add_up(own, sums):
        block = own + HALO
        kept = (own < live).astype(jnp.float32)
        third = w3_ref[block]
        pairs = (
            (z0[block], w0[block]),
            (z0[block], w1_ref[block]),
            (z1[block], w1_ref[block]),
            (z1[block], w2_ref[block]),
            (z2[block], w2_ref[block]),
            (z2[block], third),
            (third * inverse[block], third),
        )
        return tuple(s + kept * (a * b) for s, (a, b) in zip(sums, pairs))

    zero = jnp.zeros((8, BLK), jnp.float32)
    sums = lax.fori_loop(0, block_count, add_up, (zero,) * MOMENTS, unroll=4)
    lane = lax.broadcasted_iota(jnp.int32, (8, BLK), 1)
    row = lax.broadcasted_iota(jnp.int32, (8, BLK), 0)
    moments = zero
    for k in range(MOMENTS):
        moments = jnp.where(lane == 8 * row + k, jnp.sum(sums[k], axis=1, keepdims=True), moments)
    moments = jnp.sum(moments, axis=0, keepdims=True)
    moments_ref[...] = jnp.broadcast_to(moments, moments_ref.shape)


def fluid_kernel(
    axes, fluid_count,
    live_ref, jitter_ref, smoothing_ref, displacement_ref, fluid_ref, partner_ref, mine_ref, other_ref,
    basis_ref,
    fluid_basis_ref,
    joined, source, b0, b1, b2, matrix,
):
    live = live_ref[0]
    width = jitter_ref.shape[1] // BLK + 2 * HALO
    join_chain(
        axes, live, jitter_ref, smoothing_ref, displacement_ref, partner_ref, mine_ref, other_ref, joined
    )

    def prepare(block, carry):
        points, norm, scale, rhs = parts_of(joined[BASE - HALO + block])
        source[block] = source_of(points, norm)
        b0[block] = vector_pair(rhs * scale)
        b1[block] = vector_pair(basis_ref[0, block] * scale)
        b2[block] = vector_pair(basis_ref[1, block] * scale)
        return carry

    lax.fori_loop(HALO - 2, width - HALO + 2, prepare, 0, unroll=4)

    def anchor_of(index):
        return lax.div(index * live, jnp.int32(fluid_count))

    def generate_fluid(index, carry):
        lanes = pl.ds(pl.multiple_of(index * BLK, BLK), BLK)
        jitter = jnp.concatenate([fluid_ref[:, lanes], jnp.zeros((5, BLK), jnp.float32)], axis=0)
        points = centred(jitter)
        norm = jnp.sum(points * points, axis=0, keepdims=True)
        groups = target_groups(target_values(points, norm))
        first = anchor_of(index) + (HALO - 2)
        for place in range(5):
            columns = target_rows(groups, place - 2)
            distances = jnp.dot(source[first + place], columns, preferred_element_type=jnp.float32)
            store_pair(matrix.at[index], wendland_scaled(distances), place * BLK)
        return carry

    def apply_fluid(index, carry):
        first = anchor_of(index) + (HALO - 2)
        near = [
            jnp.concatenate([ref[first + place] for place in range(5)], axis=1)
            for ref in (b0, b1, b2)
        ]
        near = jnp.concatenate(near, axis=0)
        product = jnp.dot(near, matrix[index], preferred_element_type=jnp.float32)
        for k in range(3):
            fluid_basis_ref[index, k] = sum_pairs(product, 16 * k)
        return carry

    lax.fori_loop(0, fluid_count, generate_fluid, 0, unroll=4)
    lax.fori_loop(0, fluid_count, apply_fluid, 0, unroll=4)


def step_coefficients(moments):
    def inner(left, right):
        total = 0.0
        for i, a in enumerate(left):
            for j, b in enumerate(right):
                total = total + a * b * moments[i + j]
        return total

    one = jnp.ones_like(moments[0])
    solution_part, residual, direction = [], [one], [one]
    norm = moments[0]
    for iteration in range(ITERS):
        image = [
            (direction[k] if k < len(direction) else 0.0) + (direction[k - 1] if k else 0.0)
            for k in range(len(direction) + 1)
        ]
        step = norm / inner(direction, image)
        old = solution_part + [0.0] * (len(direction) - len(solution_part))
        solution_part = [a + step * b for a, b in zip(old, direction)]
        residual = [
            (residual[k] if k < len(residual) else 0.0) - step * image[k] for k in range(len(image))
        ]
        following = inner(residual, residual)
        ratio = following / norm
        direction = [
            residual[k] + ratio * (direction[k] if k < len(direction) else 0.0)
            for k in range(len(residual))
        ]
        norm = following
    spread = 0.0
    for k, a in enumerate(residual):
        spread = spread + jnp.abs(a) * jnp.sqrt(jnp.maximum(moments[2 * k], 0.0))
    return solution_part, residual, spread * spread <= MAX_AMPLIFICATION**2 * norm


def finish_kernel(
    block_count, fluid_count, live_ref, moments_ref, smoothing_ref, displacement_ref,
    basis_ref, fluid_basis_ref, coefs_ref, residual_ref, fluid_ref, good_ref,
):
    live = live_ref[0]
    row = lax.broadcasted_iota(jnp.int32, (8, BLK), 0)
    lane = lax.broadcasted_iota(jnp.int32, (8, BLK), 1)
    summed = jnp.broadcast_to(jnp.sum(moments_ref[...], axis=0, keepdims=True), (8, BLK))
    moments = [
        jnp.sum(jnp.where(lane == 8 * row + k, summed, 0.0), axis=1, keepdims=True)
        for k in range(MOMENTS)
    ]
    solved, left, good = step_coefficients(moments)
    row = lax.broadcasted_iota(jnp.int32, (8, 1), 0)
    good_ref[0] = jnp.min(jnp.where(good | (row > 2), 1.0, 0.0)).astype(jnp.int32)
    solved = [jnp.broadcast_to(v, (8, BLK))[0:3] for v in solved]
    left = [jnp.broadcast_to(v, (8, BLK))[0:3] for v in left]

    def one_block(own, carry):
        lanes = pl.ds(pl.multiple_of(own * BLK, BLK), BLK)
        block = own + HALO
        parts = [displacement_ref[:, lanes]] + [basis_ref[k, block][0:3] for k in range(3)]
        scaled = sum(a * b for a, b in zip(solved, parts)) / (1.0 + smoothing_ref[:, lanes])
        remaining = sum(a * b for a, b in zip(left, parts))
        is_live = own < live
        coefs_ref[:, lanes] = jnp.where(is_live, scaled, 0.0)
        residual_ref[:, lanes] = jnp.where(is_live, remaining, 0.0)
        return carry

    lax.fori_loop(0, block_count, one_block, 0, unroll=4)

    def one_fluid(index, carry):
        lanes = pl.ds(pl.multiple_of(index * BLK, BLK), BLK)
        fluid_ref[:, lanes] = sum(a * fluid_basis_ref[index, k][0:3] for k, a in enumerate(solved))
        return carry

    lax.fori_loop(0, fluid_count, one_fluid, 0, unroll=4)


def wendland(row_points, col_points):
    spread = (row_points[0][:, None] - col_points[0][None, :]) ** 2
    spread = spread + (row_points[1][:, None] - col_points[1][None, :]) ** 2
    spread = spread + (row_points[2][:, None] - col_points[2][None, :]) ** 2
    scaled = jnp.sqrt(spread) * 0.5
    remain = jnp.maximum(1.0 - scaled, 0.0)
    return remain * remain * remain * remain * (4.0 * scaled + 1.0)


def block_ends(blocks, live_count):
    tail_index = live_count - 2 + jnp.arange(2, dtype=jnp.int32)
    tail_flags = (tail_index >= 0).astype(jnp.float32)
    padded = jnp.pad(blocks, ((0, 0), (2, 0), (0, 0)))
    tail_blocks = lax.dynamic_slice_in_dim(padded, live_count, 2, axis=1)
    head_flags = (jnp.arange(2, dtype=jnp.int32) < live_count).astype(jnp.float32)
    return (tail_blocks, tail_flags, blocks[:, :2], head_flags)


def join_left(nearer, farther, pick):
    return jnp.stack([jnp.where(pick, nearer[:, 0], farther[:, 1]), nearer[:, 1]], axis=1)


def join_right(nearer, farther, pick):
    return jnp.stack([nearer[:, 0], jnp.where(pick, nearer[:, 1], farther[:, 0])], axis=1)


def extend(own_blocks, left_pair, right_pair, live_count):
    padded = jnp.concatenate([left_pair, own_blocks, jnp.zeros_like(left_pair)], axis=1)
    return lax.dynamic_update_slice_in_dim(padded, right_pair, live_count + 2, axis=1)


def shifted(block, axes, distance):
    devices = range(lax.axis_size(axes))
    route = [(i - distance, i) for i in devices if i - distance in devices]
    return lax.ppermute(block, axes, route)


def iterate_with_reductions(axes, wing_jitter, live_blocks, smoothing, displacement, fluid_jitter):
    block_count = wing_jitter.shape[1] // BLK
    fluid_count = fluid_jitter.shape[1] // BLK
    live_count = live_blocks[0]
    factors = jnp.array(stretch_factors, jnp.float32)[:, None, None]
    own_points = wing_jitter.reshape(3, block_count, BLK) * factors
    own_flags = (jnp.arange(block_count, dtype=jnp.int32) < live_count).astype(jnp.float32)
    ends_of = {}
    neighbour_counts = {}
    for offset in (1, 2, -1, -2):
        points, counts = shifted((own_points, live_blocks), axes, offset)
        tail_blocks, tail_flags, head_blocks, head_flags = block_ends(points, counts[0])
        neighbour_counts[offset] = counts[0]
        ends_of[offset] = (tail_blocks, tail_flags) if offset > 0 else (head_blocks, head_flags)
    left_pick = ends_of[1][1][0] > 0
    right_pick = ends_of[-1][1][1] > 0
    left_points = join_left(ends_of[1][0], ends_of[2][0], left_pick)
    right_points = join_right(ends_of[-1][0], ends_of[-2][0], right_pick)
    left_flags = join_left(ends_of[1][1][None, :, None], ends_of[2][1][None, :, None], left_pick)
    right_flags = join_right(
        ends_of[-1][1][None, :, None], ends_of[-2][1][None, :, None], right_pick
    )
    ext_points = extend(own_points, left_points, right_points, live_count)
    ext_flags = extend(own_flags[None, :, None], left_flags, right_flags, live_count)
    ext_along = jnp.arange(block_count + 4, dtype=jnp.float32) - 2.0
    ext_points = ext_points.at[0].add(ext_along[:, None]).reshape(3, -1)
    col_flags = jnp.broadcast_to(ext_flags[0], (block_count + 4, BLK)).reshape(-1)
    row_points = (
        own_points.at[0].add(jnp.arange(block_count, dtype=jnp.float32)[:, None]).reshape(3, -1)
    )
    row_mask = jnp.repeat(own_flags, BLK)
    diagonal = 1.0 + smoothing

    def value_context(blocks):
        pieces = {}
        for offset in (1, 2, -1, -2):
            moved = shifted(blocks, axes, offset)
            tail_part, _, head_part, _ = block_ends(moved, neighbour_counts[offset])
            pieces[offset] = tail_part if offset > 0 else head_part
        left_values = join_left(pieces[1], pieces[2], left_pick)
        right_values = join_right(pieces[-1], pieces[-2], right_pick)
        return extend(blocks, left_values, right_values, live_count).reshape(3, -1)

    def apply(vector):
        ext_values = value_context(vector.reshape(3, block_count, BLK))

        def row_group(group):
            first_row = group * (2 * BLK)
            points = lax.dynamic_slice_in_dim(row_points, first_row, 2 * BLK, 1)
            col_points = lax.dynamic_slice_in_dim(ext_points, first_row, 6 * BLK, 1)
            flags = lax.dynamic_slice_in_dim(col_flags, first_row, 6 * BLK, 0)
            kernel = wendland(points, col_points) * flags[None, :]
            col_values = lax.dynamic_slice_in_dim(ext_values, first_row, 6 * BLK, 1)
            return jnp.einsum("cj,ij->ci", col_values, kernel, precision=lax.Precision.HIGHEST)

        result = lax.map(row_group, jnp.arange(block_count // 2, dtype=jnp.int32))
        result = result.transpose(1, 0, 2).reshape(3, -1)
        return result * row_mask + smoothing * vector

    def total(left, right):
        return lax.psum(jnp.sum(left * right, axis=1), axes)

    rhs = displacement * row_mask
    coefs = jnp.zeros_like(rhs)
    residual = rhs
    direction = precond = residual / diagonal
    norm_now = total(residual, precond)
    for iteration in range(ITERS):
        image = apply(direction)
        step_size = norm_now / total(direction, image)
        coefs = coefs + step_size[:, None] * direction
        residual = residual - step_size[:, None] * image
        if iteration + 1 < ITERS:
            precond = residual / diagonal
            norm_next = total(residual, precond)
            direction = precond + (norm_next / norm_now)[:, None] * direction
            norm_now = norm_next
    anchors = jnp.arange(fluid_count, dtype=jnp.int32) * live_count // fluid_count
    fluid_points = fluid_jitter.reshape(3, fluid_count, BLK) * factors
    fluid_points = fluid_points.at[0].add(anchors.astype(jnp.float32)[:, None])
    coef_ext = value_context(coefs.reshape(3, block_count, BLK))

    def fluid_block(points_and_anchor):
        points, anchor = points_and_anchor
        start_col = anchor * BLK
        col_points = lax.dynamic_slice_in_dim(ext_points, start_col, 5 * BLK, 1)
        flags = lax.dynamic_slice_in_dim(col_flags, start_col, 5 * BLK, 0)
        kernel = wendland(points, col_points) * flags[None, :]
        col_values = lax.dynamic_slice_in_dim(coef_ext, start_col, 5 * BLK, 1)
        return jnp.einsum("cj,ij->ci", col_values, kernel, precision=lax.Precision.HIGHEST)

    fluid_values = lax.map(fluid_block, (fluid_points.transpose(1, 0, 2), anchors))
    fluid_values = fluid_values.transpose(1, 0, 2).reshape(3, -1)
    return (coefs, residual, fluid_values)


def along_chips(values, axes, chips):
    count = lax.axis_size(axes)
    route = [(i, i + 2 * chips * (1 - 2 * (i % 2))) for i in range(count)]
    return lax.ppermute(values, axes, [(i, j) for i, j in route if 0 <= j < count])


def per_device(axes, wing_jitter, live_blocks, smoothing, displacement, fluid_jitter):
    block_count = wing_jitter.shape[1] // BLK
    fluid_count = fluid_jitter.shape[1] // BLK
    width = block_count + 2 * HALO
    smoothing_row = smoothing.reshape(1, -1)
    in_smem = pl.BlockSpec(memory_space=pltpu.SMEM)
    in_vmem = pl.BlockSpec(memory_space=pltpu.VMEM)

    def floats(*shape):
        return jax.ShapeDtypeStruct(shape, jnp.float32)

    small = pltpu.CompilerParams(vmem_limit_bytes=8 * 2**20)
    ends = pl.pallas_call(
        pack_kernel,
        out_shape=floats(2, HALO, 8, BLK),
        in_specs=[in_smem] + [in_vmem] * 3,
        out_specs=in_vmem,
        compiler_params=small,
    )(live_blocks, wing_jitter, smoothing_row, displacement)

    def join(near, far, end=False):
        return pl.pallas_call(
            functools.partial(join_kernel, axes, end),
            out_shape=floats(HALO, 8, BLK),
            in_specs=[in_vmem] * 2,
            out_specs=in_vmem,
            scratch_shapes=[pltpu.VMEM((3 * HALO, 8, BLK), jnp.float32)],
            compiler_params=small,
        )(near, far)

    cores = [(i, i ^ 1) for i in range(lax.axis_size(axes))]
    partner = lax.ppermute(ends, axes, cores)
    chip = join(partner, ends, end=True)
    next_chip = along_chips(chip, axes, 1)
    beyond = along_chips(join(chip, next_chip), axes, 2)
    mine = join(next_chip, beyond)
    other = lax.ppermute(mine, axes, cores)

    vectors = pltpu.VMEM((width, 8, BLK), jnp.float32)
    pairs = pltpu.VMEM((width, 16, BLK), jnp.bfloat16)
    joined = pltpu.VMEM((2 * BASE + block_count, 8, BLK), jnp.float32)
    source = pltpu.VMEM((width, BLK, PIECES), jnp.bfloat16)
    matrix_shape = jax.ShapeDtypeStruct((width - 2, 3 * BLK, 2 * BLK), jnp.bfloat16)
    own_rows = block_count - 2
    first_rows = block_count // 2

    def own_part(first, rows, *matrix):
        return pl.pallas_call(
            functools.partial(own_kernel, first, rows, first + rows == own_rows),
            out_shape=matrix_shape,
            in_specs=[in_vmem] * (1 + len(matrix)),
            out_specs=in_vmem,
            input_output_aliases={1: 0} if matrix else {},
            scratch_shapes=[
                pltpu.VMEM((rows + 2, BLK, PIECES), jnp.bfloat16),
                pltpu.VMEM((rows + 2, 8, BLK), jnp.float32),
            ],
            compiler_params=small,
            cost_estimate=pl.CostEstimate(flops=4 * 10**9, bytes_accessed=10**6, transcendentals=10**6),
        )(wing_jitter, *matrix)

    matrix = own_part(first_rows, own_rows - first_rows, own_part(0, first_rows))
    basis, moments, _ = pl.pallas_call(
        functools.partial(chain_kernel, axes, block_count),
        out_shape=(floats(3, width, 8, BLK), floats(lax.axis_size(axes), BLK), matrix_shape),
        in_specs=[in_smem] + [in_vmem] * 7,
        out_specs=(in_vmem,) * 3,
        input_output_aliases={7: 2},
        scratch_shapes=[
            joined,
            pltpu.VMEM((HALO + 2, BLK, PIECES), jnp.bfloat16),
            pltpu.VMEM((HALO + 2, 8, BLK), jnp.float32),
            *[vectors] * 5,
            *[pairs] * 3,
        ],
        compiler_params=pltpu.CompilerParams(vmem_limit_bytes=12 * 2**20),
    )(live_blocks, wing_jitter, smoothing_row, displacement, partner, mine, other, matrix)
    moments = lax.all_to_all(moments, axes, 0, 0, tiled=True)
    fluid_basis = pl.pallas_call(
        functools.partial(fluid_kernel, axes, fluid_count),
        out_shape=floats(fluid_count, 3, 8, BLK),
        in_specs=[in_smem] + [in_vmem] * 8,
        out_specs=in_vmem,
        scratch_shapes=[
            joined,
            source,
            *[pairs] * 3,
            pltpu.VMEM((fluid_count, 5 * BLK, 2 * BLK), jnp.bfloat16),
        ],
        compiler_params=pltpu.CompilerParams(vmem_limit_bytes=24 * 2**20),
        cost_estimate=pl.CostEstimate(flops=6 * 10**9, bytes_accessed=10**7, transcendentals=2 * 10**6),
    )(live_blocks, wing_jitter, smoothing_row, displacement, fluid_jitter, partner, mine, other, basis)
    coefs, residual, fluid_values, good = pl.pallas_call(
        functools.partial(finish_kernel, block_count, fluid_count),
        out_shape=(
            floats(3, block_count * BLK),
            floats(3, block_count * BLK),
            floats(3, fluid_count * BLK),
            jax.ShapeDtypeStruct((1,), jnp.int32),
        ),
        in_specs=[in_smem] + [in_vmem] * 5,
        out_specs=(in_vmem, in_vmem, in_vmem, in_smem),
        compiler_params=small,
    )(live_blocks, moments, smoothing_row, displacement, basis, fluid_basis)
    return lax.cond(
        good[0] == 1,
        lambda: (coefs, residual, fluid_values),
        lambda: iterate_with_reductions(
            axes, wing_jitter, live_blocks, smoothing, displacement, fluid_jitter
        ),
    )


def solution(mesh):
    placed = (P(None, "dom"), P("dom"), P("dom"), P(None, "dom"), P(None, "dom"))
    return jax.shard_map(
        functools.partial(per_device, "dom"),
        mesh=mesh,
        in_specs=placed,
        out_specs=(P(None, "dom"),) * 3,
        check_vma=False,
    )
```

```python
import functools
import jax
import jax.numpy as jnp
from jax import lax
from jax.experimental import pallas as pl
from jax.experimental.pallas import tpu as pltpu
from jax.sharding import PartitionSpec as P

BLK = 128
ITERS = 3
HALO = 6
BASE = 2 * HALO
PIECES = 48
MAX_AMPLIFICATION = 50.0
MOMENTS = 2 * ITERS + 1
APPLY_UNROLL = 16

stretch_factors = (1.0, 6.0, 6.0)


def pack_kernel(live_ref, jitter_ref, smoothing_ref, displacement_ref, ends_ref):
    live = live_ref[0]
    count = jnp.full((1, BLK), jnp.minimum(live, HALO), jnp.int32).astype(jnp.float32)
    for slot in range(HALO):
        tail_block = live - HALO + slot
        tail_start = pl.multiple_of(jnp.maximum(tail_block, 0) * BLK, BLK)
        starts = ((tail_block >= 0, tail_start), (slot < live, slot * BLK))
        for end, (kept, start) in enumerate(starts):
            lanes = pl.ds(start, BLK)
            mask = kept.astype(jnp.float32)
            ends_ref[end, slot, 0:3, :] = jitter_ref[:, lanes] * mask
            ends_ref[end, slot, 3:4, :] = smoothing_ref[:, lanes] * mask
            ends_ref[end, slot, 4:7, :] = displacement_ref[:, lanes] * mask
            ends_ref[end, slot, 7:8, :] = count


def count_in(row):
    return jnp.max(row).astype(jnp.int32)


def join_kernel(axes, end, near_ref, far_ref, *refs):
    joined_ref, buffer = refs[-2:]
    core = lax.rem(lax.axis_index(axes), 2)
    near = near_ref[core] if end else near_ref[...]
    far = far_ref[core] if end else far_ref[...]
    count = near[0, 7:8, :] + far[0, 7:8, :]
    held = count_in(near[0, 7:8, :])
    buffer[pl.ds(HALO, HALO)] = near
    buffer[pl.ds(HALO + jnp.where(core == 0, -held, held), HALO)] = far
    joined_ref[...] = buffer[pl.ds(HALO, HALO)]
    for slot in range(HALO):
        joined_ref[slot, 7:8, :] = jnp.minimum(count, float(HALO))


def split(values):
    high = values.astype(jnp.bfloat16).astype(jnp.float32)
    rest = values - high
    middle = rest.astype(jnp.bfloat16).astype(jnp.float32)
    return high, middle, rest - middle


def rows_of(row):
    return lax.broadcasted_iota(jnp.int32, (8, BLK), 0) == row


def centred(jitter):
    row = lax.broadcasted_iota(jnp.int32, (8, BLK), 0)
    scale = jnp.where(row == 0, 2.0, 12.0)
    shift = jnp.where(row == 0, 1.0, 6.0)
    return jnp.where(row < 3, jitter * scale - shift, 0.0)


def source_rows(points, norm):
    row = lax.broadcasted_iota(jnp.int32, (8, BLK), 0)
    extended = jnp.where(row >= 4, 1.0, points)
    extended = jnp.where(row == 3, norm, jnp.where(row == 5, points[0:1], extended))
    high, middle, low = split(extended)
    return jnp.concatenate([high, high, middle, high, low, middle], axis=0)


def target_values(points, norm):
    return jnp.where(rows_of(4), norm, -2.0 * points)


def target_groups(values):
    high, middle, low = split(values)
    bases = (jnp.where(rows_of(3), 1.0, high), middle, low)
    slopes = [jnp.where(rows_of(6), 2.0 * piece[0:1], 0.0) for piece in (high, middle, low)]
    slopes[0] = jnp.where(rows_of(5), 4.0, slopes[0])
    return bases, slopes


def target_rows(groups, delta):
    bases, slopes = groups
    if delta:
        bases = [base + float(delta) * slope for base, slope in zip(bases, slopes)]
        bases[0] = jnp.where(rows_of(7), 4.0 * delta * delta, bases[0])
    first = jnp.concatenate([bases[0], bases[1]], axis=0).astype(jnp.bfloat16)
    second = jnp.concatenate([bases[0], bases[2]], axis=0).astype(jnp.bfloat16)
    return jnp.concatenate([first, second, first], axis=0)


PHI_SCALE = 256.0


def wendland_scaled(distances):
    distances = jnp.maximum(distances, 1e-30)
    scaled = distances * lax.rsqrt(distances)
    remain = jnp.maximum(4.0 - scaled, 0.0)
    square = remain * remain
    return square * square * (scaled + 1.0)


def store_pair(ref, values, first_row):
    high = values.astype(jnp.bfloat16)
    low = (values - high.astype(jnp.float32)).astype(jnp.bfloat16)
    ref[pl.ds(first_row, BLK), 0:BLK] = high
    ref[pl.ds(first_row, BLK), BLK : 2 * BLK] = low


def vector_pair(values):
    values = values * (1.0 / PHI_SCALE)
    high = values.astype(jnp.bfloat16).astype(jnp.float32)
    return jnp.concatenate([high, values - high], axis=0).astype(jnp.bfloat16)


def sum_pairs(product, first):
    upper = product[first : first + 8] + product[first + 8 : first + 16]
    return upper[:, :BLK] + upper[:, BLK:]


def join_chain(axes, live, jitter_ref, smoothing_ref, displacement_ref, partner_ref, mine_ref, other_ref, joined):
    block_count = jitter_ref.shape[1] // BLK
    for extra in range(HALO):
        joined[BASE + block_count + extra] = jnp.zeros((8, BLK), jnp.float32)

    def put_own(block, carry):
        lanes = pl.ds(pl.multiple_of(block * BLK, BLK), BLK)
        kept = (block < live).astype(jnp.float32)
        joined[BASE + block, 0:3, :] = jitter_ref[:, lanes]
        joined[BASE + block, 3:4, :] = smoothing_ref[:, lanes] * kept
        joined[BASE + block, 4:7, :] = displacement_ref[:, lanes]
        return carry

    lax.fori_loop(0, block_count, put_own, 0, unroll=8)
    core = lax.rem(lax.axis_index(axes), 2)
    mine, other = mine_ref[...], other_ref[...]
    left_near = jnp.where(core == 0, 0, count_in(partner_ref[0, 0, 7:8, :]))
    right_near = jnp.where(core == 0, count_in(partner_ref[1, 0, 7:8, :]), 0)
    joined[pl.ds(BASE - HALO, HALO)] = partner_ref[0]
    joined[pl.ds(BASE - HALO - left_near, HALO)] = jnp.where(core == 0, mine, other)
    joined[pl.ds(BASE + live, HALO)] = partner_ref[1]
    joined[pl.ds(BASE + live + right_near, HALO)] = jnp.where(core == 0, other, mine)


def parts_of(packed):
    points = centred(packed)
    norm = jnp.sum(points * points, axis=0, keepdims=True)
    inverse = jnp.where(packed[3:4] > 0.0, 1.0 / (1.0 + packed[3:4]), 0.0)
    rhs = jnp.concatenate([packed[4:7], jnp.zeros((5, BLK), jnp.float32)], axis=0)
    return points, norm, jnp.broadcast_to(inverse, (8, BLK)), rhs


def source_of(points, norm):
    return jnp.transpose(source_rows(points, norm)).astype(jnp.bfloat16)


def generate_two(source, target, matrix, block, row):
    first, second = target_groups(target[block]), target_groups(target[block + 1])
    for place in range(4):
        columns = []
        if place < 3:
            columns.append(target_rows(first, place))
        if place > 0:
            columns.append(target_rows(second, place - 1))
        distances = jnp.dot(
            source[block + place],
            jnp.concatenate(columns, axis=1),
            preferred_element_type=jnp.float32,
        )
        values = wendland_scaled(distances)
        if place < 3:
            store_pair(matrix.at[row], values[:, :BLK], place * BLK)
        if place > 0:
            store_pair(matrix.at[row + 1], values[:, -BLK:], (place - 1) * BLK)


def own_kernel(first, rows, last, jitter_ref, *refs):
    matrix, mark_ref, source, target = refs[-4:]
    mark_ref[...] = jnp.zeros_like(mark_ref)

    def prepare(block, carry):
        lanes = pl.ds(pl.multiple_of((first + block) * BLK, BLK), BLK)
        jitter = jnp.concatenate([jitter_ref[:, lanes], jnp.zeros((5, BLK), jnp.float32)], axis=0)
        points = centred(jitter)
        norm = jnp.sum(points * points, axis=0, keepdims=True)
        source[block] = source_of(points, norm)
        target[block] = target_values(points, norm)
        return carry

    lax.fori_loop(0, rows + 2, prepare, 0, unroll=4)

    def generate(pair, carry):
        generate_two(source, target, matrix, 2 * pair, HALO + first + 2 * pair)
        return carry

    lax.fori_loop(0, rows // 2, generate, 0, unroll=4)
    if last:
        for row in range(HALO + first + rows, matrix.shape[0]):
            matrix[row] = jnp.zeros(matrix.shape[1:], matrix.dtype)


def chain_kernel(
    axes, block_count,
    live_ref, jitter_ref, smoothing_ref, displacement_ref, partner_ref, mine_ref, other_ref, _,
    basis_ref, moments_ref, matrix,
    joined, source, target, inverse, w0, z0, z1, z2, b0, b1, b2,
):
    w1_ref, w2_ref, w3_ref = (basis_ref.at[k] for k in range(3))
    live = live_ref[0]
    width = block_count + 2 * HALO
    join_chain(
        axes, live, jitter_ref, smoothing_ref, displacement_ref, partner_ref, mine_ref, other_ref, joined
    )

    def prepare(block, carry):
        _, _, scale, rhs = parts_of(joined[BASE - HALO + block])
        inverse[block] = scale
        w0[block] = rhs
        z0[block] = rhs * scale
        b0[block] = vector_pair(rhs * scale)
        return carry

    lax.fori_loop(0, width, prepare, 0, unroll=4)

    for start in (0, live + HALO - 2):
        for block in range(HALO + 2):
            points, norm, _, _ = parts_of(joined[BASE - HALO + start + block])
            source[block] = source_of(points, norm)
            target[block] = target_values(points, norm)
        for row in range(0, HALO, 2):
            generate_two(source, target, matrix, row, start + row)

    def apply_row(block, values, pairs, place_next):
        near = jnp.concatenate([pairs[block + place] for place in range(3)], axis=1)
        product = jnp.dot(near, matrix[block], preferred_element_type=jnp.float32)
        image = sum_pairs(product, 0) - values[block]
        for back in (1, 2):
            behind = pairs[block - back]
            product = lax.dot_general(
                jnp.concatenate([behind, behind], axis=1),
                matrix[block - back, back * BLK : (back + 1) * BLK, :],
                (((1,), (1,)), ((), ())),
                preferred_element_type=jnp.float32,
            )
            image = image + (product[0:8] + product[8:16])
        place_next(block, image)

    def apply(values, pairs, first, last, place_next):
        def one_row(block, carry):
            apply_row(block, values, pairs, place_next)
            return carry

        lax.fori_loop(first, last, one_row, 0, unroll=APPLY_UNROLL)

    def first_next(block, image):
        scaled = image * inverse[block]
        z1[block] = scaled
        b1[block] = vector_pair(scaled)
        w1_ref[block] = image

    def second_next(block, image):
        scaled = image * inverse[block]
        z2[block] = scaled
        b2[block] = vector_pair(scaled)
        w2_ref[block] = image

    def third_next(block, image):
        w3_ref[block] = image

    apply(z0, b0, 2, width - 2, first_next)
    apply(z1, b1, 4, width - 4, second_next)
    apply(z2, b2, 6, width - 6, third_next)

    def add_up(own, sums):
        block = own + HALO
        kept = (own < live).astype(jnp.float32)
        third = w3_ref[block]
        pairs = (
            (z0[block], w0[block]),
            (z0[block], w1_ref[block]),
            (z1[block], w1_ref[block]),
            (z1[block], w2_ref[block]),
            (z2[block], w2_ref[block]),
            (z2[block], third),
            (third * inverse[block], third),
        )
        return tuple(s + kept * (a * b) for s, (a, b) in zip(sums, pairs))

    zero = jnp.zeros((8, BLK), jnp.float32)
    sums = lax.fori_loop(0, block_count, add_up, (zero,) * MOMENTS, unroll=4)
    lane = lax.broadcasted_iota(jnp.int32, (8, BLK), 1)
    row = lax.broadcasted_iota(jnp.int32, (8, BLK), 0)
    moments = zero
    for k in range(MOMENTS):
        moments = jnp.where(lane == 8 * row + k, jnp.sum(sums[k], axis=1, keepdims=True), moments)
    moments = jnp.sum(moments, axis=0, keepdims=True)
    moments_ref[...] = jnp.broadcast_to(moments, moments_ref.shape)


def fluid_kernel(
    axes, fluid_count,
    live_ref, jitter_ref, smoothing_ref, displacement_ref, fluid_ref, partner_ref, mine_ref, other_ref,
    basis_ref,
    fluid_basis_ref,
    joined, source, b0, b1, b2, matrix,
):
    live = live_ref[0]
    width = jitter_ref.shape[1] // BLK + 2 * HALO
    join_chain(
        axes, live, jitter_ref, smoothing_ref, displacement_ref, partner_ref, mine_ref, other_ref, joined
    )

    def prepare(block, carry):
        points, norm, scale, rhs = parts_of(joined[BASE - HALO + block])
        source[block] = source_of(points, norm)
        b0[block] = vector_pair(rhs * scale)
        b1[block] = vector_pair(basis_ref[0, block] * scale)
        b2[block] = vector_pair(basis_ref[1, block] * scale)
        return carry

    lax.fori_loop(HALO - 2, width - HALO + 2, prepare, 0, unroll=4)

    def anchor_of(index):
        return lax.div(index * live, jnp.int32(fluid_count))

    def generate_fluid(index, carry):
        lanes = pl.ds(pl.multiple_of(index * BLK, BLK), BLK)
        jitter = jnp.concatenate([fluid_ref[:, lanes], jnp.zeros((5, BLK), jnp.float32)], axis=0)
        points = centred(jitter)
        norm = jnp.sum(points * points, axis=0, keepdims=True)
        groups = target_groups(target_values(points, norm))
        first = anchor_of(index) + (HALO - 2)
        for place in range(5):
            columns = target_rows(groups, place - 2)
            distances = jnp.dot(source[first + place], columns, preferred_element_type=jnp.float32)
            store_pair(matrix.at[index], wendland_scaled(distances), place * BLK)
        return carry

    def apply_fluid(index, carry):
        first = anchor_of(index) + (HALO - 2)
        near = [
            jnp.concatenate([ref[first + place] for place in range(5)], axis=1)
            for ref in (b0, b1, b2)
        ]
        near = jnp.concatenate(near, axis=0)
        product = jnp.dot(near, matrix[index], preferred_element_type=jnp.float32)
        for k in range(3):
            fluid_basis_ref[index, k] = sum_pairs(product, 16 * k)
        return carry

    lax.fori_loop(0, fluid_count, generate_fluid, 0, unroll=4)
    lax.fori_loop(0, fluid_count, apply_fluid, 0, unroll=4)


def step_coefficients(moments):
    def inner(left, right):
        total = 0.0
        for i, a in enumerate(left):
            for j, b in enumerate(right):
                total = total + a * b * moments[i + j]
        return total

    one = jnp.ones_like(moments[0])
    solution_part, residual, direction = [], [one], [one]
    norm = moments[0]
    for iteration in range(ITERS):
        image = [
            (direction[k] if k < len(direction) else 0.0) + (direction[k - 1] if k else 0.0)
            for k in range(len(direction) + 1)
        ]
        step = norm / inner(direction, image)
        old = solution_part + [0.0] * (len(direction) - len(solution_part))
        solution_part = [a + step * b for a, b in zip(old, direction)]
        residual = [
            (residual[k] if k < len(residual) else 0.0) - step * image[k] for k in range(len(image))
        ]
        following = inner(residual, residual)
        ratio = following / norm
        direction = [
            residual[k] + ratio * (direction[k] if k < len(direction) else 0.0)
            for k in range(len(residual))
        ]
        norm = following
    spread = 0.0
    for k, a in enumerate(residual):
        spread = spread + jnp.abs(a) * jnp.sqrt(jnp.maximum(moments[2 * k], 0.0))
    return solution_part, residual, spread * spread <= MAX_AMPLIFICATION**2 * norm


def finish_kernel(
    block_count, fluid_count, live_ref, moments_ref, smoothing_ref, displacement_ref,
    basis_ref, fluid_basis_ref, coefs_ref, residual_ref, fluid_ref, good_ref,
):
    live = live_ref[0]
    row = lax.broadcasted_iota(jnp.int32, (8, BLK), 0)
    lane = lax.broadcasted_iota(jnp.int32, (8, BLK), 1)
    summed = jnp.broadcast_to(jnp.sum(moments_ref[...], axis=0, keepdims=True), (8, BLK))
    moments = [
        jnp.sum(jnp.where(lane == 8 * row + k, summed, 0.0), axis=1, keepdims=True)
        for k in range(MOMENTS)
    ]
    solved, left, good = step_coefficients(moments)
    row = lax.broadcasted_iota(jnp.int32, (8, 1), 0)
    good_ref[0] = jnp.min(jnp.where(good | (row > 2), 1.0, 0.0)).astype(jnp.int32)
    solved = [jnp.broadcast_to(v, (8, BLK))[0:3] for v in solved]
    left = [jnp.broadcast_to(v, (8, BLK))[0:3] for v in left]

    def one_block(own, carry):
        lanes = pl.ds(pl.multiple_of(own * BLK, BLK), BLK)
        block = own + HALO
        parts = [displacement_ref[:, lanes]] + [basis_ref[k, block][0:3] for k in range(3)]
        scaled = sum(a * b for a, b in zip(solved, parts)) / (1.0 + smoothing_ref[:, lanes])
        remaining = sum(a * b for a, b in zip(left, parts))
        is_live = own < live
        coefs_ref[:, lanes] = jnp.where(is_live, scaled, 0.0)
        residual_ref[:, lanes] = jnp.where(is_live, remaining, 0.0)
        return carry

    lax.fori_loop(0, block_count, one_block, 0, unroll=4)

    def one_fluid(index, carry):
        lanes = pl.ds(pl.multiple_of(index * BLK, BLK), BLK)
        fluid_ref[:, lanes] = sum(a * fluid_basis_ref[index, k][0:3] for k, a in enumerate(solved))
        return carry

    lax.fori_loop(0, fluid_count, one_fluid, 0, unroll=4)


def wendland(row_points, col_points):
    spread = (row_points[0][:, None] - col_points[0][None, :]) ** 2
    spread = spread + (row_points[1][:, None] - col_points[1][None, :]) ** 2
    spread = spread + (row_points[2][:, None] - col_points[2][None, :]) ** 2
    scaled = jnp.sqrt(spread) * 0.5
    remain = jnp.maximum(1.0 - scaled, 0.0)
    return remain * remain * remain * remain * (4.0 * scaled + 1.0)


def block_ends(blocks, live_count):
    tail_index = live_count - 2 + jnp.arange(2, dtype=jnp.int32)
    tail_flags = (tail_index >= 0).astype(jnp.float32)
    padded = jnp.pad(blocks, ((0, 0), (2, 0), (0, 0)))
    tail_blocks = lax.dynamic_slice_in_dim(padded, live_count, 2, axis=1)
    head_flags = (jnp.arange(2, dtype=jnp.int32) < live_count).astype(jnp.float32)
    return (tail_blocks, tail_flags, blocks[:, :2], head_flags)


def join_left(nearer, farther, pick):
    return jnp.stack([jnp.where(pick, nearer[:, 0], farther[:, 1]), nearer[:, 1]], axis=1)


def join_right(nearer, farther, pick):
    return jnp.stack([nearer[:, 0], jnp.where(pick, nearer[:, 1], farther[:, 0])], axis=1)


def extend(own_blocks, left_pair, right_pair, live_count):
    padded = jnp.concatenate([left_pair, own_blocks, jnp.zeros_like(left_pair)], axis=1)
    return lax.dynamic_update_slice_in_dim(padded, right_pair, live_count + 2, axis=1)


def shifted(block, axes, distance):
    devices = range(lax.axis_size(axes))
    route = [(i - distance, i) for i in devices if i - distance in devices]
    return lax.ppermute(block, axes, route)


def iterate_with_reductions(axes, wing_jitter, live_blocks, smoothing, displacement, fluid_jitter):
    block_count = wing_jitter.shape[1] // BLK
    fluid_count = fluid_jitter.shape[1] // BLK
    live_count = live_blocks[0]
    factors = jnp.array(stretch_factors, jnp.float32)[:, None, None]
    own_points = wing_jitter.reshape(3, block_count, BLK) * factors
    own_flags = (jnp.arange(block_count, dtype=jnp.int32) < live_count).astype(jnp.float32)
    ends_of = {}
    neighbour_counts = {}
    for offset in (1, 2, -1, -2):
        points, counts = shifted((own_points, live_blocks), axes, offset)
        tail_blocks, tail_flags, head_blocks, head_flags = block_ends(points, counts[0])
        neighbour_counts[offset] = counts[0]
        ends_of[offset] = (tail_blocks, tail_flags) if offset > 0 else (head_blocks, head_flags)
    left_pick = ends_of[1][1][0] > 0
    right_pick = ends_of[-1][1][1] > 0
    left_points = join_left(ends_of[1][0], ends_of[2][0], left_pick)
    right_points = join_right(ends_of[-1][0], ends_of[-2][0], right_pick)
    left_flags = join_left(ends_of[1][1][None, :, None], ends_of[2][1][None, :, None], left_pick)
    right_flags = join_right(
        ends_of[-1][1][None, :, None], ends_of[-2][1][None, :, None], right_pick
    )
    ext_points = extend(own_points, left_points, right_points, live_count)
    ext_flags = extend(own_flags[None, :, None], left_flags, right_flags, live_count)
    ext_along = jnp.arange(block_count + 4, dtype=jnp.float32) - 2.0
    ext_points = ext_points.at[0].add(ext_along[:, None]).reshape(3, -1)
    col_flags = jnp.broadcast_to(ext_flags[0], (block_count + 4, BLK)).reshape(-1)
    row_points = (
        own_points.at[0].add(jnp.arange(block_count, dtype=jnp.float32)[:, None]).reshape(3, -1)
    )
    row_mask = jnp.repeat(own_flags, BLK)
    diagonal = 1.0 + smoothing

    def value_context(blocks):
        pieces = {}
        for offset in (1, 2, -1, -2):
            moved = shifted(blocks, axes, offset)
            tail_part, _, head_part, _ = block_ends(moved, neighbour_counts[offset])
            pieces[offset] = tail_part if offset > 0 else head_part
        left_values = join_left(pieces[1], pieces[2], left_pick)
        right_values = join_right(pieces[-1], pieces[-2], right_pick)
        return extend(blocks, left_values, right_values, live_count).reshape(3, -1)

    def apply(vector):
        ext_values = value_context(vector.reshape(3, block_count, BLK))

        def row_group(group):
            first_row = group * (2 * BLK)
            points = lax.dynamic_slice_in_dim(row_points, first_row, 2 * BLK, 1)
            col_points = lax.dynamic_slice_in_dim(ext_points, first_row, 6 * BLK, 1)
            flags = lax.dynamic_slice_in_dim(col_flags, first_row, 6 * BLK, 0)
            kernel = wendland(points, col_points) * flags[None, :]
            col_values = lax.dynamic_slice_in_dim(ext_values, first_row, 6 * BLK, 1)
            return jnp.einsum("cj,ij->ci", col_values, kernel, precision=lax.Precision.HIGHEST)

        result = lax.map(row_group, jnp.arange(block_count // 2, dtype=jnp.int32))
        result = result.transpose(1, 0, 2).reshape(3, -1)
        return result * row_mask + smoothing * vector

    def total(left, right):
        return lax.psum(jnp.sum(left * right, axis=1), axes)

    rhs = displacement * row_mask
    coefs = jnp.zeros_like(rhs)
    residual = rhs
    direction = precond = residual / diagonal
    norm_now = total(residual, precond)
    for iteration in range(ITERS):
        image = apply(direction)
        step_size = norm_now / total(direction, image)
        coefs = coefs + step_size[:, None] * direction
        residual = residual - step_size[:, None] * image
        if iteration + 1 < ITERS:
            precond = residual / diagonal
            norm_next = total(residual, precond)
            direction = precond + (norm_next / norm_now)[:, None] * direction
            norm_now = norm_next
    anchors = jnp.arange(fluid_count, dtype=jnp.int32) * live_count // fluid_count
    fluid_points = fluid_jitter.reshape(3, fluid_count, BLK) * factors
    fluid_points = fluid_points.at[0].add(anchors.astype(jnp.float32)[:, None])
    coef_ext = value_context(coefs.reshape(3, block_count, BLK))

    def fluid_block(points_and_anchor):
        points, anchor = points_and_anchor
        start_col = anchor * BLK
        col_points = lax.dynamic_slice_in_dim(ext_points, start_col, 5 * BLK, 1)
        flags = lax.dynamic_slice_in_dim(col_flags, start_col, 5 * BLK, 0)
        kernel = wendland(points, col_points) * flags[None, :]
        col_values = lax.dynamic_slice_in_dim(coef_ext, start_col, 5 * BLK, 1)
        return jnp.einsum("cj,ij->ci", col_values, kernel, precision=lax.Precision.HIGHEST)

    fluid_values = lax.map(fluid_block, (fluid_points.transpose(1, 0, 2), anchors))
    fluid_values = fluid_values.transpose(1, 0, 2).reshape(3, -1)
    return (coefs, residual, fluid_values)


def along_chips(values, axes, chips):
    count = lax.axis_size(axes)
    route = [(i, i + 2 * chips * (1 - 2 * (i % 2))) for i in range(count)]
    return lax.ppermute(values, axes, [(i, j) for i, j in route if 0 <= j < count])


def per_device(axes, wing_jitter, live_blocks, smoothing, displacement, fluid_jitter):
    block_count = wing_jitter.shape[1] // BLK
    fluid_count = fluid_jitter.shape[1] // BLK
    width = block_count + 2 * HALO
    smoothing_row = smoothing.reshape(1, -1)
    in_smem = pl.BlockSpec(memory_space=pltpu.SMEM)
    in_vmem = pl.BlockSpec(memory_space=pltpu.VMEM)

    def floats(*shape):
        return jax.ShapeDtypeStruct(shape, jnp.float32)

    small = pltpu.CompilerParams(vmem_limit_bytes=8 * 2**20)
    ends = pl.pallas_call(
        pack_kernel,
        out_shape=floats(2, HALO, 8, BLK),
        in_specs=[in_smem] + [in_vmem] * 3,
        out_specs=in_vmem,
        compiler_params=small,
    )(live_blocks, wing_jitter, smoothing_row, displacement)

    def join(near, far, *after, end=False):
        return pl.pallas_call(
            functools.partial(join_kernel, axes, end),
            out_shape=floats(HALO, 8, BLK),
            in_specs=[in_vmem] * 2 + [pl.BlockSpec(memory_space=pl.ANY)] * len(after),
            out_specs=in_vmem,
            scratch_shapes=[pltpu.VMEM((3 * HALO, 8, BLK), jnp.float32)],
            compiler_params=small,
        )(near, far, *after)

    matrix_shape = jax.ShapeDtypeStruct((width - 2, 3 * BLK, 2 * BLK), jnp.bfloat16)
    own_rows = block_count - 2
    first_rows = block_count // 2

    def own_part(first, rows, *matrix):
        return pl.pallas_call(
            functools.partial(own_kernel, first, rows, first + rows == own_rows),
            out_shape=(matrix_shape, floats(8, BLK)),
            in_specs=[in_vmem] * (1 + len(matrix)),
            out_specs=(in_vmem, in_vmem),
            input_output_aliases={1: 0} if matrix else {},
            scratch_shapes=[
                pltpu.VMEM((rows + 2, BLK, PIECES), jnp.bfloat16),
                pltpu.VMEM((rows + 2, 8, BLK), jnp.float32),
            ],
            compiler_params=small,
            cost_estimate=pl.CostEstimate(flops=4 * 10**9, bytes_accessed=10**6, transcendentals=10**6),
        )(wing_jitter, *matrix)

    matrix, first_mark = own_part(0, first_rows)
    matrix, second_mark = own_part(first_rows, own_rows - first_rows, matrix)

    cores = [(i, i ^ 1) for i in range(lax.axis_size(axes))]
    partner = lax.ppermute(ends, axes, cores)
    chip = join(partner, ends, end=True)
    next_chip = along_chips(chip, axes, 1)
    beyond = along_chips(join(chip, next_chip, first_mark), axes, 2)
    mine = join(next_chip, beyond, second_mark)
    other = lax.ppermute(mine, axes, cores)

    vectors = pltpu.VMEM((width, 8, BLK), jnp.float32)
    pairs = pltpu.VMEM((width, 16, BLK), jnp.bfloat16)
    joined = pltpu.VMEM((2 * BASE + block_count, 8, BLK), jnp.float32)
    source = pltpu.VMEM((width, BLK, PIECES), jnp.bfloat16)
    basis, moments, _ = pl.pallas_call(
        functools.partial(chain_kernel, axes, block_count),
        out_shape=(floats(3, width, 8, BLK), floats(lax.axis_size(axes), BLK), matrix_shape),
        in_specs=[in_smem] + [in_vmem] * 7,
        out_specs=(in_vmem,) * 3,
        input_output_aliases={7: 2},
        scratch_shapes=[
            joined,
            pltpu.VMEM((HALO + 2, BLK, PIECES), jnp.bfloat16),
            pltpu.VMEM((HALO + 2, 8, BLK), jnp.float32),
            *[vectors] * 5,
            *[pairs] * 3,
        ],
        compiler_params=pltpu.CompilerParams(vmem_limit_bytes=12 * 2**20),
    )(live_blocks, wing_jitter, smoothing_row, displacement, partner, mine, other, matrix)
    moments = lax.all_to_all(moments, axes, 0, 0, tiled=True)
    fluid_basis = pl.pallas_call(
        functools.partial(fluid_kernel, axes, fluid_count),
        out_shape=floats(fluid_count, 3, 8, BLK),
        in_specs=[in_smem] + [in_vmem] * 8,
        out_specs=in_vmem,
        scratch_shapes=[
            joined,
            source,
            *[pairs] * 3,
            pltpu.VMEM((fluid_count, 5 * BLK, 2 * BLK), jnp.bfloat16),
        ],
        compiler_params=pltpu.CompilerParams(vmem_limit_bytes=24 * 2**20),
        cost_estimate=pl.CostEstimate(flops=6 * 10**9, bytes_accessed=10**7, transcendentals=2 * 10**6),
    )(live_blocks, wing_jitter, smoothing_row, displacement, fluid_jitter, partner, mine, other, basis)
    coefs, residual, fluid_values, good = pl.pallas_call(
        functools.partial(finish_kernel, block_count, fluid_count),
        out_shape=(
            floats(3, block_count * BLK),
            floats(3, block_count * BLK),
            floats(3, fluid_count * BLK),
            jax.ShapeDtypeStruct((1,), jnp.int32),
        ),
        in_specs=[in_smem] + [in_vmem] * 5,
        out_specs=(in_vmem, in_vmem, in_vmem, in_smem),
        compiler_params=small,
    )(live_blocks, moments, smoothing_row, displacement, basis, fluid_basis)
    return lax.cond(
        good[0] == 1,
        lambda: (coefs, residual, fluid_values),
        lambda: iterate_with_reductions(
            axes, wing_jitter, live_blocks, smoothing, displacement, fluid_jitter
        ),
    )


def solution(mesh):
    placed = (P(None, "dom"), P("dom"), P("dom"), P(None, "dom"), P(None, "dom"))
    return jax.shard_map(
        functools.partial(per_device, "dom"),
        mesh=mesh,
        in_specs=placed,
        out_specs=(P(None, "dom"),) * 3,
        check_vma=False,
    )
```

```python
import functools
import jax
import jax.numpy as jnp
from jax import lax
from jax.experimental import pallas as pl
from jax.experimental.pallas import tpu as pltpu
from jax.sharding import PartitionSpec as P

BLK = 128
ITERS = 3
HALO = 6
BASE = 2 * HALO
PIECES = 48
MAX_AMPLIFICATION = 50.0
MOMENTS = 2 * ITERS + 1
APPLY_UNROLL = 16

stretch_factors = (1.0, 6.0, 6.0)


def pack_kernel(live_ref, jitter_ref, smoothing_ref, displacement_ref, ends_ref):
    live = live_ref[0]
    count = jnp.full((1, BLK), jnp.minimum(live, HALO), jnp.int32).astype(jnp.float32)
    for slot in range(HALO):
        tail_block = live - HALO + slot
        tail_start = pl.multiple_of(jnp.maximum(tail_block, 0) * BLK, BLK)
        starts = ((tail_block >= 0, tail_start), (slot < live, slot * BLK))
        for end, (kept, start) in enumerate(starts):
            lanes = pl.ds(start, BLK)
            mask = kept.astype(jnp.float32)
            ends_ref[end, slot, 0:3, :] = jitter_ref[:, lanes] * mask
            ends_ref[end, slot, 3:4, :] = smoothing_ref[:, lanes] * mask
            ends_ref[end, slot, 4:7, :] = displacement_ref[:, lanes] * mask
            ends_ref[end, slot, 7:8, :] = count


def count_in(row):
    return jnp.max(row).astype(jnp.int32)


def join_kernel(axes, end, near_ref, far_ref, *refs):
    joined_ref, buffer = refs[-2:]
    core = lax.rem(lax.axis_index(axes), 2)
    near = near_ref[core] if end else near_ref[...]
    far = far_ref[core] if end else far_ref[...]
    count = near[0, 7:8, :] + far[0, 7:8, :]
    held = count_in(near[0, 7:8, :])
    buffer[pl.ds(HALO, HALO)] = near
    buffer[pl.ds(HALO + jnp.where(core == 0, -held, held), HALO)] = far
    joined_ref[...] = buffer[pl.ds(HALO, HALO)]
    for slot in range(HALO):
        joined_ref[slot, 7:8, :] = jnp.minimum(count, float(HALO))


def split(values):
    high = values.astype(jnp.bfloat16).astype(jnp.float32)
    rest = values - high
    middle = rest.astype(jnp.bfloat16).astype(jnp.float32)
    return high, middle, rest - middle


def rows_of(row):
    return lax.broadcasted_iota(jnp.int32, (8, BLK), 0) == row


def centred(jitter):
    row = lax.broadcasted_iota(jnp.int32, (8, BLK), 0)
    scale = jnp.where(row == 0, 2.0, 12.0)
    shift = jnp.where(row == 0, 1.0, 6.0)
    return jnp.where(row < 3, jitter * scale - shift, 0.0)


def source_rows(points, norm):
    row = lax.broadcasted_iota(jnp.int32, (8, BLK), 0)
    extended = jnp.where(row >= 4, 1.0, points)
    extended = jnp.where(row == 3, norm, jnp.where(row == 5, points[0:1], extended))
    high, middle, low = split(extended)
    return jnp.concatenate([high, high, middle, high, low, middle], axis=0)


def target_values(points, norm):
    return jnp.where(rows_of(4), norm, -2.0 * points)


def target_groups(values):
    high, middle, low = split(values)
    bases = (jnp.where(rows_of(3), 1.0, high), middle, low)
    slopes = [jnp.where(rows_of(6), 2.0 * piece[0:1], 0.0) for piece in (high, middle, low)]
    slopes[0] = jnp.where(rows_of(5), 4.0, slopes[0])
    return bases, slopes


def target_rows(groups, delta):
    bases, slopes = groups
    if delta:
        bases = [base + float(delta) * slope for base, slope in zip(bases, slopes)]
        bases[0] = jnp.where(rows_of(7), 4.0 * delta * delta, bases[0])
    first = jnp.concatenate([bases[0], bases[1]], axis=0).astype(jnp.bfloat16)
    second = jnp.concatenate([bases[0], bases[2]], axis=0).astype(jnp.bfloat16)
    return jnp.concatenate([first, second, first], axis=0)


PHI_SCALE = 256.0


def wendland_scaled(distances):
    distances = jnp.maximum(distances, 1e-30)
    scaled = distances * lax.rsqrt(distances)
    remain = jnp.maximum(4.0 - scaled, 0.0)
    square = remain * remain
    return square * square * (scaled + 1.0)


def store_pair(ref, values, first_row):
    high = values.astype(jnp.bfloat16)
    low = (values - high.astype(jnp.float32)).astype(jnp.bfloat16)
    ref[pl.ds(first_row, BLK), 0:BLK] = high
    ref[pl.ds(first_row, BLK), BLK : 2 * BLK] = low


def vector_pair(values):
    values = values * (1.0 / PHI_SCALE)
    high = values.astype(jnp.bfloat16).astype(jnp.float32)
    return jnp.concatenate([high, values - high], axis=0).astype(jnp.bfloat16)


def sum_pairs(product, first):
    upper = product[first : first + 8] + product[first + 8 : first + 16]
    return upper[:, :BLK] + upper[:, BLK:]


def join_chain(axes, live, jitter_ref, smoothing_ref, displacement_ref, partner_ref, mine_ref, other_ref, joined):
    block_count = jitter_ref.shape[1] // BLK
    for extra in range(HALO):
        joined[BASE + block_count + extra] = jnp.zeros((8, BLK), jnp.float32)

    def put_own(block, carry):
        lanes = pl.ds(pl.multiple_of(block * BLK, BLK), BLK)
        kept = (block < live).astype(jnp.float32)
        joined[BASE + block, 0:3, :] = jitter_ref[:, lanes]
        joined[BASE + block, 3:4, :] = smoothing_ref[:, lanes] * kept
        joined[BASE + block, 4:7, :] = displacement_ref[:, lanes]
        return carry

    lax.fori_loop(0, block_count, put_own, 0, unroll=8)
    core = lax.rem(lax.axis_index(axes), 2)
    mine, other = mine_ref[...], other_ref[...]
    left_near = jnp.where(core == 0, 0, count_in(partner_ref[0, 0, 7:8, :]))
    right_near = jnp.where(core == 0, count_in(partner_ref[1, 0, 7:8, :]), 0)
    joined[pl.ds(BASE - HALO, HALO)] = partner_ref[0]
    joined[pl.ds(BASE - HALO - left_near, HALO)] = jnp.where(core == 0, mine, other)
    joined[pl.ds(BASE + live, HALO)] = partner_ref[1]
    joined[pl.ds(BASE + live + right_near, HALO)] = jnp.where(core == 0, other, mine)


def parts_of(packed):
    points = centred(packed)
    norm = jnp.sum(points * points, axis=0, keepdims=True)
    inverse = jnp.where(packed[3:4] > 0.0, 1.0 / (1.0 + packed[3:4]), 0.0)
    rhs = jnp.concatenate([packed[4:7], jnp.zeros((5, BLK), jnp.float32)], axis=0)
    return points, norm, jnp.broadcast_to(inverse, (8, BLK)), rhs


def source_of(points, norm):
    return jnp.transpose(source_rows(points, norm)).astype(jnp.bfloat16)


def generate_two(source, target, matrix, block, row):
    first, second = target_groups(target[block]), target_groups(target[block + 1])
    for place in range(4):
        columns = []
        if place < 3:
            columns.append(target_rows(first, place))
        if place > 0:
            columns.append(target_rows(second, place - 1))
        distances = jnp.dot(
            source[block + place],
            jnp.concatenate(columns, axis=1),
            preferred_element_type=jnp.float32,
        )
        values = wendland_scaled(distances)
        if place < 3:
            store_pair(matrix.at[row], values[:, :BLK], place * BLK)
        if place > 0:
            store_pair(matrix.at[row + 1], values[:, -BLK:], (place - 1) * BLK)


def own_kernel(first, rows, last, jitter_ref, *refs):
    matrix, mark_ref, source, target = refs[-4:]
    mark_ref[...] = jnp.zeros_like(mark_ref)

    def prepare(block, carry):
        lanes = pl.ds(pl.multiple_of((first + block) * BLK, BLK), BLK)
        jitter = jnp.concatenate([jitter_ref[:, lanes], jnp.zeros((5, BLK), jnp.float32)], axis=0)
        points = centred(jitter)
        norm = jnp.sum(points * points, axis=0, keepdims=True)
        source[block] = source_of(points, norm)
        target[block] = target_values(points, norm)
        return carry

    lax.fori_loop(0, rows + 2, prepare, 0, unroll=4)

    def generate(pair, carry):
        generate_two(source, target, matrix, 2 * pair, HALO + first + 2 * pair)
        return carry

    lax.fori_loop(0, rows // 2, generate, 0, unroll=4)
    if last:
        for row in range(HALO + first + rows, matrix.shape[0]):
            matrix[row] = jnp.zeros(matrix.shape[1:], matrix.dtype)


def chain_kernel(
    axes, block_count,
    live_ref, jitter_ref, smoothing_ref, displacement_ref, partner_ref, mine_ref, other_ref, _,
    basis_ref, moments_ref, matrix,
    joined, source, target, inverse, w0, z0, z1, z2, b0, b1, b2,
):
    w1_ref, w2_ref, w3_ref = (basis_ref.at[k] for k in range(3))
    live = live_ref[0]
    width = block_count + 2 * HALO
    join_chain(
        axes, live, jitter_ref, smoothing_ref, displacement_ref, partner_ref, mine_ref, other_ref, joined
    )

    def prepare(block, carry):
        _, _, scale, rhs = parts_of(joined[BASE - HALO + block])
        inverse[block] = scale
        w0[block] = rhs
        z0[block] = rhs * scale
        b0[block] = vector_pair(rhs * scale)
        return carry

    lax.fori_loop(0, width, prepare, 0, unroll=4)

    for start in (0, live + HALO - 2):
        for block in range(HALO + 2):
            points, norm, _, _ = parts_of(joined[BASE - HALO + start + block])
            source[block] = source_of(points, norm)
            target[block] = target_values(points, norm)
        for row in range(0, HALO, 2):
            generate_two(source, target, matrix, row, start + row)

    def apply_row(block, values, pairs, place_next):
        near = jnp.concatenate([pairs[block + place] for place in range(3)], axis=1)
        product = jnp.dot(near, matrix[block], preferred_element_type=jnp.float32)
        image = sum_pairs(product, 0) - values[block]
        for back in (1, 2):
            behind = pairs[block - back]
            product = lax.dot_general(
                jnp.concatenate([behind, behind], axis=1),
                matrix[block - back, back * BLK : (back + 1) * BLK, :],
                (((1,), (1,)), ((), ())),
                preferred_element_type=jnp.float32,
            )
            image = image + (product[0:8] + product[8:16])
        place_next(block, image)

    def apply(values, pairs, first, last, place_next):
        def one_row(block, carry):
            apply_row(block, values, pairs, place_next)
            return carry

        lax.fori_loop(first, last, one_row, 0, unroll=APPLY_UNROLL)

    def first_next(block, image):
        scaled = image * inverse[block]
        z1[block] = scaled
        b1[block] = vector_pair(scaled)
        w1_ref[block] = image

    def second_next(block, image):
        scaled = image * inverse[block]
        z2[block] = scaled
        b2[block] = vector_pair(scaled)
        w2_ref[block] = image

    def third_next(block, image):
        w3_ref[block] = image

    apply(z0, b0, 2, width - 2, first_next)
    apply(z1, b1, 4, width - 4, second_next)
    apply(z2, b2, 6, width - 6, third_next)

    def add_up(own, sums):
        block = own + HALO
        kept = (own < live).astype(jnp.float32)
        third = w3_ref[block]
        pairs = (
            (z0[block], w0[block]),
            (z0[block], w1_ref[block]),
            (z1[block], w1_ref[block]),
            (z1[block], w2_ref[block]),
            (z2[block], w2_ref[block]),
            (z2[block], third),
            (third * inverse[block], third),
        )
        return tuple(s + kept * (a * b) for s, (a, b) in zip(sums, pairs))

    zero = jnp.zeros((8, BLK), jnp.float32)
    sums = lax.fori_loop(0, block_count, add_up, (zero,) * MOMENTS, unroll=4)
    lane = lax.broadcasted_iota(jnp.int32, (8, BLK), 1)
    row = lax.broadcasted_iota(jnp.int32, (8, BLK), 0)
    moments = zero
    for k in range(MOMENTS):
        moments = jnp.where(lane == 8 * row + k, jnp.sum(sums[k], axis=1, keepdims=True), moments)
    moments = jnp.sum(moments, axis=0, keepdims=True)
    moments_ref[...] = jnp.broadcast_to(moments, moments_ref.shape)


def fluid_kernel(
    axes, fluid_count,
    live_ref, jitter_ref, smoothing_ref, displacement_ref, fluid_ref, partner_ref, mine_ref, other_ref,
    basis_ref,
    fluid_basis_ref,
    joined, source, b0, b1, b2, matrix,
):
    live = live_ref[0]
    width = jitter_ref.shape[1] // BLK + 2 * HALO
    join_chain(
        axes, live, jitter_ref, smoothing_ref, displacement_ref, partner_ref, mine_ref, other_ref, joined
    )

    def prepare(block, carry):
        points, norm, scale, rhs = parts_of(joined[BASE - HALO + block])
        source[block] = source_of(points, norm)
        b0[block] = vector_pair(rhs * scale)
        b1[block] = vector_pair(basis_ref[0, block] * scale)
        b2[block] = vector_pair(basis_ref[1, block] * scale)
        return carry

    lax.fori_loop(HALO - 2, width - HALO + 2, prepare, 0, unroll=4)

    def anchor_of(index):
        return lax.div(index * live, jnp.int32(fluid_count))

    def generate_fluid(index, carry):
        lanes = pl.ds(pl.multiple_of(index * BLK, BLK), BLK)
        jitter = jnp.concatenate([fluid_ref[:, lanes], jnp.zeros((5, BLK), jnp.float32)], axis=0)
        points = centred(jitter)
        norm = jnp.sum(points * points, axis=0, keepdims=True)
        groups = target_groups(target_values(points, norm))
        first = anchor_of(index) + (HALO - 2)
        for place in range(5):
            columns = target_rows(groups, place - 2)
            distances = jnp.dot(source[first + place], columns, preferred_element_type=jnp.float32)
            store_pair(matrix.at[index], wendland_scaled(distances), place * BLK)
        return carry

    def apply_fluid(index, carry):
        first = anchor_of(index) + (HALO - 2)
        near = [
            jnp.concatenate([ref[first + place] for place in range(5)], axis=1)
            for ref in (b0, b1, b2)
        ]
        near = jnp.concatenate(near, axis=0)
        product = jnp.dot(near, matrix[index], preferred_element_type=jnp.float32)
        for k in range(3):
            fluid_basis_ref[index, k] = sum_pairs(product, 16 * k)
        return carry

    lax.fori_loop(0, fluid_count, generate_fluid, 0, unroll=4)
    lax.fori_loop(0, fluid_count, apply_fluid, 0, unroll=4)


def step_coefficients(moments):
    def inner(left, right):
        total = 0.0
        for i, a in enumerate(left):
            for j, b in enumerate(right):
                total = total + a * b * moments[i + j]
        return total

    one = jnp.ones_like(moments[0])
    solution_part, residual, direction = [], [one], [one]
    norm = moments[0]
    for iteration in range(ITERS):
        image = [
            (direction[k] if k < len(direction) else 0.0) + (direction[k - 1] if k else 0.0)
            for k in range(len(direction) + 1)
        ]
        step = norm / inner(direction, image)
        old = solution_part + [0.0] * (len(direction) - len(solution_part))
        solution_part = [a + step * b for a, b in zip(old, direction)]
        residual = [
            (residual[k] if k < len(residual) else 0.0) - step * image[k] for k in range(len(image))
        ]
        following = inner(residual, residual)
        ratio = following / norm
        direction = [
            residual[k] + ratio * (direction[k] if k < len(direction) else 0.0)
            for k in range(len(residual))
        ]
        norm = following
    spread = 0.0
    for k, a in enumerate(residual):
        spread = spread + jnp.abs(a) * jnp.sqrt(jnp.maximum(moments[2 * k], 0.0))
    return solution_part, residual, spread * spread <= MAX_AMPLIFICATION**2 * norm


def finish_kernel(
    block_count, fluid_count, live_ref, moments_ref, smoothing_ref, displacement_ref,
    basis_ref, fluid_basis_ref, coefs_ref, residual_ref, fluid_ref, good_ref,
):
    live = live_ref[0]
    row = lax.broadcasted_iota(jnp.int32, (8, BLK), 0)
    lane = lax.broadcasted_iota(jnp.int32, (8, BLK), 1)
    summed = jnp.broadcast_to(jnp.sum(moments_ref[...], axis=0, keepdims=True), (8, BLK))
    moments = [
        jnp.sum(jnp.where(lane == 8 * row + k, summed, 0.0), axis=1, keepdims=True)
        for k in range(MOMENTS)
    ]
    solved, left, good = step_coefficients(moments)
    row = lax.broadcasted_iota(jnp.int32, (8, 1), 0)
    good_ref[0] = jnp.min(jnp.where(good | (row > 2), 1.0, 0.0)).astype(jnp.int32)
    solved = [jnp.broadcast_to(v, (8, BLK))[0:3] for v in solved]
    left = [jnp.broadcast_to(v, (8, BLK))[0:3] for v in left]

    def one_block(own, carry):
        lanes = pl.ds(pl.multiple_of(own * BLK, BLK), BLK)
        block = own + HALO
        parts = [displacement_ref[:, lanes]] + [basis_ref[k, block][0:3] for k in range(3)]
        scaled = sum(a * b for a, b in zip(solved, parts)) / (1.0 + smoothing_ref[:, lanes])
        remaining = sum(a * b for a, b in zip(left, parts))
        is_live = own < live
        coefs_ref[:, lanes] = jnp.where(is_live, scaled, 0.0)
        residual_ref[:, lanes] = jnp.where(is_live, remaining, 0.0)
        return carry

    lax.fori_loop(0, block_count, one_block, 0, unroll=4)

    def one_fluid(index, carry):
        lanes = pl.ds(pl.multiple_of(index * BLK, BLK), BLK)
        fluid_ref[:, lanes] = sum(a * fluid_basis_ref[index, k][0:3] for k, a in enumerate(solved))
        return carry

    lax.fori_loop(0, fluid_count, one_fluid, 0, unroll=4)


def wendland(row_points, col_points):
    spread = (row_points[0][:, None] - col_points[0][None, :]) ** 2
    spread = spread + (row_points[1][:, None] - col_points[1][None, :]) ** 2
    spread = spread + (row_points[2][:, None] - col_points[2][None, :]) ** 2
    scaled = jnp.sqrt(spread) * 0.5
    remain = jnp.maximum(1.0 - scaled, 0.0)
    return remain * remain * remain * remain * (4.0 * scaled + 1.0)


def block_ends(blocks, live_count):
    tail_index = live_count - 2 + jnp.arange(2, dtype=jnp.int32)
    tail_flags = (tail_index >= 0).astype(jnp.float32)
    padded = jnp.pad(blocks, ((0, 0), (2, 0), (0, 0)))
    tail_blocks = lax.dynamic_slice_in_dim(padded, live_count, 2, axis=1)
    head_flags = (jnp.arange(2, dtype=jnp.int32) < live_count).astype(jnp.float32)
    return (tail_blocks, tail_flags, blocks[:, :2], head_flags)


def join_left(nearer, farther, pick):
    return jnp.stack([jnp.where(pick, nearer[:, 0], farther[:, 1]), nearer[:, 1]], axis=1)


def join_right(nearer, farther, pick):
    return jnp.stack([nearer[:, 0], jnp.where(pick, nearer[:, 1], farther[:, 0])], axis=1)


def extend(own_blocks, left_pair, right_pair, live_count):
    padded = jnp.concatenate([left_pair, own_blocks, jnp.zeros_like(left_pair)], axis=1)
    return lax.dynamic_update_slice_in_dim(padded, right_pair, live_count + 2, axis=1)


def shifted(block, axes, distance):
    devices = range(lax.axis_size(axes))
    route = [(i - distance, i) for i in devices if i - distance in devices]
    return lax.ppermute(block, axes, route)


def iterate_with_reductions(axes, wing_jitter, live_blocks, smoothing, displacement, fluid_jitter):
    block_count = wing_jitter.shape[1] // BLK
    fluid_count = fluid_jitter.shape[1] // BLK
    live_count = live_blocks[0]
    factors = jnp.array(stretch_factors, jnp.float32)[:, None, None]
    own_points = wing_jitter.reshape(3, block_count, BLK) * factors
    own_flags = (jnp.arange(block_count, dtype=jnp.int32) < live_count).astype(jnp.float32)
    ends_of = {}
    neighbour_counts = {}
    for offset in (1, 2, -1, -2):
        points, counts = shifted((own_points, live_blocks), axes, offset)
        tail_blocks, tail_flags, head_blocks, head_flags = block_ends(points, counts[0])
        neighbour_counts[offset] = counts[0]
        ends_of[offset] = (tail_blocks, tail_flags) if offset > 0 else (head_blocks, head_flags)
    left_pick = ends_of[1][1][0] > 0
    right_pick = ends_of[-1][1][1] > 0
    left_points = join_left(ends_of[1][0], ends_of[2][0], left_pick)
    right_points = join_right(ends_of[-1][0], ends_of[-2][0], right_pick)
    left_flags = join_left(ends_of[1][1][None, :, None], ends_of[2][1][None, :, None], left_pick)
    right_flags = join_right(
        ends_of[-1][1][None, :, None], ends_of[-2][1][None, :, None], right_pick
    )
    ext_points = extend(own_points, left_points, right_points, live_count)
    ext_flags = extend(own_flags[None, :, None], left_flags, right_flags, live_count)
    ext_along = jnp.arange(block_count + 4, dtype=jnp.float32) - 2.0
    ext_points = ext_points.at[0].add(ext_along[:, None]).reshape(3, -1)
    col_flags = jnp.broadcast_to(ext_flags[0], (block_count + 4, BLK)).reshape(-1)
    row_points = (
        own_points.at[0].add(jnp.arange(block_count, dtype=jnp.float32)[:, None]).reshape(3, -1)
    )
    row_mask = jnp.repeat(own_flags, BLK)
    diagonal = 1.0 + smoothing

    def value_context(blocks):
        pieces = {}
        for offset in (1, 2, -1, -2):
            moved = shifted(blocks, axes, offset)
            tail_part, _, head_part, _ = block_ends(moved, neighbour_counts[offset])
            pieces[offset] = tail_part if offset > 0 else head_part
        left_values = join_left(pieces[1], pieces[2], left_pick)
        right_values = join_right(pieces[-1], pieces[-2], right_pick)
        return extend(blocks, left_values, right_values, live_count).reshape(3, -1)

    def apply(vector):
        ext_values = value_context(vector.reshape(3, block_count, BLK))

        def row_group(group):
            first_row = group * (2 * BLK)
            points = lax.dynamic_slice_in_dim(row_points, first_row, 2 * BLK, 1)
            col_points = lax.dynamic_slice_in_dim(ext_points, first_row, 6 * BLK, 1)
            flags = lax.dynamic_slice_in_dim(col_flags, first_row, 6 * BLK, 0)
            kernel = wendland(points, col_points) * flags[None, :]
            col_values = lax.dynamic_slice_in_dim(ext_values, first_row, 6 * BLK, 1)
            return jnp.einsum("cj,ij->ci", col_values, kernel, precision=lax.Precision.HIGHEST)

        result = lax.map(row_group, jnp.arange(block_count // 2, dtype=jnp.int32))
        result = result.transpose(1, 0, 2).reshape(3, -1)
        return result * row_mask + smoothing * vector

    def total(left, right):
        return lax.psum(jnp.sum(left * right, axis=1), axes)

    rhs = displacement * row_mask
    coefs = jnp.zeros_like(rhs)
    residual = rhs
    direction = precond = residual / diagonal
    norm_now = total(residual, precond)
    for iteration in range(ITERS):
        image = apply(direction)
        step_size = norm_now / total(direction, image)
        coefs = coefs + step_size[:, None] * direction
        residual = residual - step_size[:, None] * image
        if iteration + 1 < ITERS:
            precond = residual / diagonal
            norm_next = total(residual, precond)
            direction = precond + (norm_next / norm_now)[:, None] * direction
            norm_now = norm_next
    anchors = jnp.arange(fluid_count, dtype=jnp.int32) * live_count // fluid_count
    fluid_points = fluid_jitter.reshape(3, fluid_count, BLK) * factors
    fluid_points = fluid_points.at[0].add(anchors.astype(jnp.float32)[:, None])
    coef_ext = value_context(coefs.reshape(3, block_count, BLK))

    def fluid_block(points_and_anchor):
        points, anchor = points_and_anchor
        start_col = anchor * BLK
        col_points = lax.dynamic_slice_in_dim(ext_points, start_col, 5 * BLK, 1)
        flags = lax.dynamic_slice_in_dim(col_flags, start_col, 5 * BLK, 0)
        kernel = wendland(points, col_points) * flags[None, :]
        col_values = lax.dynamic_slice_in_dim(coef_ext, start_col, 5 * BLK, 1)
        return jnp.einsum("cj,ij->ci", col_values, kernel, precision=lax.Precision.HIGHEST)

    fluid_values = lax.map(fluid_block, (fluid_points.transpose(1, 0, 2), anchors))
    fluid_values = fluid_values.transpose(1, 0, 2).reshape(3, -1)
    return (coefs, residual, fluid_values)


def along_chips(values, axes, chips):
    count = lax.axis_size(axes)
    route = [(i, i + 2 * chips * (1 - 2 * (i % 2))) for i in range(count)]
    return lax.ppermute(values, axes, [(i, j) for i, j in route if 0 <= j < count])


def per_device(axes, wing_jitter, live_blocks, smoothing, displacement, fluid_jitter):
    block_count = wing_jitter.shape[1] // BLK
    fluid_count = fluid_jitter.shape[1] // BLK
    width = block_count + 2 * HALO
    smoothing_row = smoothing.reshape(1, -1)
    in_smem = pl.BlockSpec(memory_space=pltpu.SMEM)
    in_vmem = pl.BlockSpec(memory_space=pltpu.VMEM)

    def floats(*shape):
        return jax.ShapeDtypeStruct(shape, jnp.float32)

    small = pltpu.CompilerParams(vmem_limit_bytes=8 * 2**20)
    ends = pl.pallas_call(
        pack_kernel,
        out_shape=floats(2, HALO, 8, BLK),
        in_specs=[in_smem] + [in_vmem] * 3,
        out_specs=in_vmem,
        compiler_params=small,
    )(live_blocks, wing_jitter, smoothing_row, displacement)

    def join(near, far, *after, end=False):
        return pl.pallas_call(
            functools.partial(join_kernel, axes, end),
            out_shape=floats(HALO, 8, BLK),
            in_specs=[in_vmem] * 2 + [pl.BlockSpec(memory_space=pl.ANY)] * len(after),
            out_specs=in_vmem,
            scratch_shapes=[pltpu.VMEM((3 * HALO, 8, BLK), jnp.float32)],
            compiler_params=small,
        )(near, far, *after)

    matrix_shape = jax.ShapeDtypeStruct((width - 2, 3 * BLK, 2 * BLK), jnp.bfloat16)
    own_rows = block_count - 2
    first_rows = block_count // 2

    def own_part(first, rows, *matrix):
        return pl.pallas_call(
            functools.partial(own_kernel, first, rows, first + rows == own_rows),
            out_shape=(matrix_shape, floats(8, BLK)),
            in_specs=[in_vmem] * (1 + len(matrix)),
            out_specs=(in_vmem, in_vmem),
            input_output_aliases={1: 0} if matrix else {},
            scratch_shapes=[
                pltpu.VMEM((rows + 2, BLK, PIECES), jnp.bfloat16),
                pltpu.VMEM((rows + 2, 8, BLK), jnp.float32),
            ],
            compiler_params=small,
            cost_estimate=pl.CostEstimate(flops=4 * 10**9, bytes_accessed=10**6, transcendentals=10**6),
        )(wing_jitter, *matrix)

    matrix, first_mark = own_part(0, first_rows)
    matrix, second_mark = own_part(first_rows, own_rows - first_rows, matrix)

    cores = [(i, i ^ 1) for i in range(lax.axis_size(axes))]
    partner = lax.ppermute(ends, axes, cores)
    chip = join(partner, ends, end=True)
    next_chip = along_chips(chip, axes, 1)
    beyond = along_chips(join(chip, next_chip, first_mark), axes, 2)
    mine = join(next_chip, beyond, second_mark)
    other = lax.ppermute(mine, axes, cores)

    vectors = pltpu.VMEM((width, 8, BLK), jnp.float32)
    pairs = pltpu.VMEM((width, 16, BLK), jnp.bfloat16)
    joined = pltpu.VMEM((2 * BASE + block_count, 8, BLK), jnp.float32)
    source = pltpu.VMEM((width, BLK, PIECES), jnp.bfloat16)
    basis, moments, _ = pl.pallas_call(
        functools.partial(chain_kernel, axes, block_count),
        out_shape=(floats(3, width, 8, BLK), floats(8, BLK), matrix_shape),
        in_specs=[in_smem] + [in_vmem] * 7,
        out_specs=(in_vmem,) * 3,
        input_output_aliases={7: 2},
        scratch_shapes=[
            joined,
            pltpu.VMEM((HALO + 2, BLK, PIECES), jnp.bfloat16),
            pltpu.VMEM((HALO + 2, 8, BLK), jnp.float32),
            *[vectors] * 5,
            *[pairs] * 3,
        ],
        compiler_params=pltpu.CompilerParams(vmem_limit_bytes=12 * 2**20),
    )(live_blocks, wing_jitter, smoothing_row, displacement, partner, mine, other, matrix)
    moments = moments + lax.ppermute(moments, axes, cores)
    chips = lax.axis_size(axes) // 2
    moments = lax.all_to_all(
        jnp.broadcast_to(moments[0:1], (chips, BLK)),
        axes,
        0,
        0,
        axis_index_groups=[[2 * chip + core for chip in range(chips)] for core in range(2)],
        tiled=True,
    )
    fluid_basis = pl.pallas_call(
        functools.partial(fluid_kernel, axes, fluid_count),
        out_shape=floats(fluid_count, 3, 8, BLK),
        in_specs=[in_smem] + [in_vmem] * 8,
        out_specs=in_vmem,
        scratch_shapes=[
            joined,
            source,
            *[pairs] * 3,
            pltpu.VMEM((fluid_count, 5 * BLK, 2 * BLK), jnp.bfloat16),
        ],
        compiler_params=pltpu.CompilerParams(vmem_limit_bytes=24 * 2**20),
        cost_estimate=pl.CostEstimate(flops=6 * 10**9, bytes_accessed=10**7, transcendentals=2 * 10**6),
    )(live_blocks, wing_jitter, smoothing_row, displacement, fluid_jitter, partner, mine, other, basis)
    coefs, residual, fluid_values, good = pl.pallas_call(
        functools.partial(finish_kernel, block_count, fluid_count),
        out_shape=(
            floats(3, block_count * BLK),
            floats(3, block_count * BLK),
            floats(3, fluid_count * BLK),
            jax.ShapeDtypeStruct((1,), jnp.int32),
        ),
        in_specs=[in_smem] + [in_vmem] * 5,
        out_specs=(in_vmem, in_vmem, in_vmem, in_smem),
        compiler_params=small,
    )(live_blocks, moments, smoothing_row, displacement, basis, fluid_basis)
    return lax.cond(
        good[0] == 1,
        lambda: (coefs, residual, fluid_values),
        lambda: iterate_with_reductions(
            axes, wing_jitter, live_blocks, smoothing, displacement, fluid_jitter
        ),
    )


def solution(mesh):
    placed = (P(None, "dom"), P("dom"), P("dom"), P(None, "dom"), P(None, "dom"))
    return jax.shard_map(
        functools.partial(per_device, "dom"),
        mesh=mesh,
        in_specs=placed,
        out_specs=(P(None, "dom"),) * 3,
        check_vma=False,
    )
```

```python
import functools
import jax
import jax.numpy as jnp
from jax import lax
from jax.experimental import pallas as pl
from jax.experimental.pallas import tpu as pltpu
from jax.sharding import PartitionSpec as P

BLK = 128
ITERS = 3
HALO = 6
BASE = 2 * HALO
PIECES = 48
MAX_AMPLIFICATION = 50.0
MOMENTS = 2 * ITERS + 1
APPLY_UNROLL = 16

stretch_factors = (1.0, 6.0, 6.0)


def pack_kernel(live_ref, jitter_ref, smoothing_ref, displacement_ref, ends_ref):
    live = live_ref[0]
    count = jnp.full((1, BLK), jnp.minimum(live, HALO), jnp.int32).astype(jnp.float32)
    for slot in range(HALO):
        tail_block = live - HALO + slot
        tail_start = pl.multiple_of(jnp.maximum(tail_block, 0) * BLK, BLK)
        starts = ((tail_block >= 0, tail_start), (slot < live, slot * BLK))
        for end, (kept, start) in enumerate(starts):
            lanes = pl.ds(start, BLK)
            mask = kept.astype(jnp.float32)
            ends_ref[end, slot, 0:3, :] = jitter_ref[:, lanes] * mask
            ends_ref[end, slot, 3:4, :] = smoothing_ref[:, lanes] * mask
            ends_ref[end, slot, 4:7, :] = displacement_ref[:, lanes] * mask
            ends_ref[end, slot, 7:8, :] = count


def count_in(row):
    return jnp.max(row).astype(jnp.int32)


def join_kernel(axes, end, near_ref, far_ref, *refs):
    joined_ref, buffer = refs[-2:]
    core = lax.rem(lax.axis_index(axes), 2)
    near = near_ref[core] if end else near_ref[...]
    far = far_ref[core] if end else far_ref[...]
    count = near[0, 7:8, :] + far[0, 7:8, :]
    held = count_in(near[0, 7:8, :])
    buffer[pl.ds(HALO, HALO)] = near
    buffer[pl.ds(HALO + jnp.where(core == 0, -held, held), HALO)] = far
    joined_ref[...] = buffer[pl.ds(HALO, HALO)]
    for slot in range(HALO):
        joined_ref[slot, 7:8, :] = jnp.minimum(count, float(HALO))


def split(values):
    high = values.astype(jnp.bfloat16).astype(jnp.float32)
    rest = values - high
    middle = rest.astype(jnp.bfloat16).astype(jnp.float32)
    return high, middle, rest - middle


def rows_of(row):
    return lax.broadcasted_iota(jnp.int32, (8, BLK), 0) == row


def centred(jitter):
    row = lax.broadcasted_iota(jnp.int32, (8, BLK), 0)
    scale = jnp.where(row == 0, 2.0, 12.0)
    shift = jnp.where(row == 0, 1.0, 6.0)
    return jnp.where(row < 3, jitter * scale - shift, 0.0)


def source_rows(points, norm):
    row = lax.broadcasted_iota(jnp.int32, (8, BLK), 0)
    extended = jnp.where(row >= 4, 1.0, points)
    extended = jnp.where(row == 3, norm, jnp.where(row == 5, points[0:1], extended))
    high, middle, low = split(extended)
    return jnp.concatenate([high, high, middle, high, low, middle], axis=0)


def target_values(points, norm):
    return jnp.where(rows_of(4), norm, -2.0 * points)


def target_groups(values):
    high, middle, low = split(values)
    bases = (jnp.where(rows_of(3), 1.0, high), middle, low)
    slopes = [jnp.where(rows_of(6), 2.0 * piece[0:1], 0.0) for piece in (high, middle, low)]
    slopes[0] = jnp.where(rows_of(5), 4.0, slopes[0])
    return bases, slopes


def target_rows(groups, delta):
    bases, slopes = groups
    if delta:
        bases = [base + float(delta) * slope for base, slope in zip(bases, slopes)]
        bases[0] = jnp.where(rows_of(7), 4.0 * delta * delta, bases[0])
    first = jnp.concatenate([bases[0], bases[1]], axis=0).astype(jnp.bfloat16)
    second = jnp.concatenate([bases[0], bases[2]], axis=0).astype(jnp.bfloat16)
    return jnp.concatenate([first, second, first], axis=0)


PHI_SCALE = 256.0


def wendland_scaled(distances):
    distances = jnp.maximum(distances, 1e-30)
    scaled = distances * lax.rsqrt(distances)
    remain = jnp.maximum(4.0 - scaled, 0.0)
    square = remain * remain
    return square * square * (scaled + 1.0)


def store_pair(ref, values, first_row):
    high = values.astype(jnp.bfloat16)
    low = (values - high.astype(jnp.float32)).astype(jnp.bfloat16)
    ref[pl.ds(first_row, BLK), 0:BLK] = high
    ref[pl.ds(first_row, BLK), BLK : 2 * BLK] = low


def vector_pair(values):
    values = values * (1.0 / PHI_SCALE)
    high = values.astype(jnp.bfloat16).astype(jnp.float32)
    return jnp.concatenate([high, values - high], axis=0).astype(jnp.bfloat16)


def sum_pairs(product, first):
    upper = product[first : first + 8] + product[first + 8 : first + 16]
    return upper[:, :BLK] + upper[:, BLK:]


def join_chain(axes, live, jitter_ref, smoothing_ref, displacement_ref, partner_ref, mine_ref, other_ref, joined):
    block_count = jitter_ref.shape[1] // BLK
    for extra in range(HALO):
        joined[BASE + block_count + extra] = jnp.zeros((8, BLK), jnp.float32)

    def put_own(block, carry):
        lanes = pl.ds(pl.multiple_of(block * BLK, BLK), BLK)
        kept = (block < live).astype(jnp.float32)
        joined[BASE + block, 0:3, :] = jitter_ref[:, lanes]
        joined[BASE + block, 3:4, :] = smoothing_ref[:, lanes] * kept
        joined[BASE + block, 4:7, :] = displacement_ref[:, lanes]
        return carry

    lax.fori_loop(0, block_count, put_own, 0, unroll=8)
    core = lax.rem(lax.axis_index(axes), 2)
    mine, other = mine_ref[...], other_ref[...]
    left_near = jnp.where(core == 0, 0, count_in(partner_ref[0, 0, 7:8, :]))
    right_near = jnp.where(core == 0, count_in(partner_ref[1, 0, 7:8, :]), 0)
    joined[pl.ds(BASE - HALO, HALO)] = partner_ref[0]
    joined[pl.ds(BASE - HALO - left_near, HALO)] = jnp.where(core == 0, mine, other)
    joined[pl.ds(BASE + live, HALO)] = partner_ref[1]
    joined[pl.ds(BASE + live + right_near, HALO)] = jnp.where(core == 0, other, mine)


def parts_of(packed):
    points = centred(packed)
    norm = jnp.sum(points * points, axis=0, keepdims=True)
    inverse = jnp.where(packed[3:4] > 0.0, 1.0 / (1.0 + packed[3:4]), 0.0)
    rhs = jnp.concatenate([packed[4:7], jnp.zeros((5, BLK), jnp.float32)], axis=0)
    return points, norm, jnp.broadcast_to(inverse, (8, BLK)), rhs


def source_of(points, norm):
    return jnp.transpose(source_rows(points, norm)).astype(jnp.bfloat16)


def generate_two(source, target, matrix, block, row):
    first, second = target_groups(target[block]), target_groups(target[block + 1])
    for place in range(4):
        columns = []
        if place < 3:
            columns.append(target_rows(first, place))
        if place > 0:
            columns.append(target_rows(second, place - 1))
        distances = jnp.dot(
            source[block + place],
            jnp.concatenate(columns, axis=1),
            preferred_element_type=jnp.float32,
        )
        values = wendland_scaled(distances)
        if place < 3:
            store_pair(matrix.at[row], values[:, :BLK], place * BLK)
        if place > 0:
            store_pair(matrix.at[row + 1], values[:, -BLK:], (place - 1) * BLK)


def own_kernel(first, rows, last, jitter_ref, *refs):
    matrix, source, target = refs[-3:]

    def prepare(block, carry):
        lanes = pl.ds(pl.multiple_of((first + block) * BLK, BLK), BLK)
        jitter = jnp.concatenate([jitter_ref[:, lanes], jnp.zeros((5, BLK), jnp.float32)], axis=0)
        points = centred(jitter)
        norm = jnp.sum(points * points, axis=0, keepdims=True)
        source[block] = source_of(points, norm)
        target[block] = target_values(points, norm)
        return carry

    lax.fori_loop(0, rows + 2, prepare, 0, unroll=4)

    def generate(pair, carry):
        generate_two(source, target, matrix, 2 * pair, HALO + first + 2 * pair)
        return carry

    lax.fori_loop(0, rows // 2, generate, 0, unroll=4)
    if last:
        for row in range(HALO + first + rows, matrix.shape[0]):
            matrix[row] = jnp.zeros(matrix.shape[1:], matrix.dtype)


def chain_kernel(
    axes, block_count,
    live_ref, jitter_ref, smoothing_ref, displacement_ref, partner_ref, mine_ref, other_ref, _,
    basis_ref, moments_ref, matrix,
    joined, source, target, inverse, w0, z0, z1, z2, b0, b1, b2,
):
    w1_ref, w2_ref, w3_ref = (basis_ref.at[k] for k in range(3))
    live = live_ref[0]
    width = block_count + 2 * HALO
    join_chain(
        axes, live, jitter_ref, smoothing_ref, displacement_ref, partner_ref, mine_ref, other_ref, joined
    )

    def prepare(block, carry):
        _, _, scale, rhs = parts_of(joined[BASE - HALO + block])
        inverse[block] = scale
        w0[block] = rhs
        z0[block] = rhs * scale
        b0[block] = vector_pair(rhs * scale)
        return carry

    lax.fori_loop(0, width, prepare, 0, unroll=4)

    for start in (0, live + HALO - 2):
        for block in range(HALO + 2):
            points, norm, _, _ = parts_of(joined[BASE - HALO + start + block])
            source[block] = source_of(points, norm)
            target[block] = target_values(points, norm)
        for row in range(0, HALO, 2):
            generate_two(source, target, matrix, row, start + row)

    def apply_row(block, values, pairs, place_next):
        near = jnp.concatenate([pairs[block + place] for place in range(3)], axis=1)
        product = jnp.dot(near, matrix[block], preferred_element_type=jnp.float32)
        image = sum_pairs(product, 0) - values[block]
        for back in (1, 2):
            behind = pairs[block - back]
            product = lax.dot_general(
                jnp.concatenate([behind, behind], axis=1),
                matrix[block - back, back * BLK : (back + 1) * BLK, :],
                (((1,), (1,)), ((), ())),
                preferred_element_type=jnp.float32,
            )
            image = image + (product[0:8] + product[8:16])
        place_next(block, image)

    def apply(values, pairs, first, last, place_next):
        def one_row(block, carry):
            apply_row(block, values, pairs, place_next)
            return carry

        lax.fori_loop(first, last, one_row, 0, unroll=APPLY_UNROLL)

    def first_next(block, image):
        scaled = image * inverse[block]
        z1[block] = scaled
        b1[block] = vector_pair(scaled)
        w1_ref[block] = image

    def second_next(block, image):
        scaled = image * inverse[block]
        z2[block] = scaled
        b2[block] = vector_pair(scaled)
        w2_ref[block] = image

    def third_next(block, image):
        w3_ref[block] = image

    apply(z0, b0, 2, width - 2, first_next)
    apply(z1, b1, 4, width - 4, second_next)
    apply(z2, b2, 6, width - 6, third_next)

    def add_up(own, sums):
        block = own + HALO
        kept = (own < live).astype(jnp.float32)
        third = w3_ref[block]
        pairs = (
            (z0[block], w0[block]),
            (z0[block], w1_ref[block]),
            (z1[block], w1_ref[block]),
            (z1[block], w2_ref[block]),
            (z2[block], w2_ref[block]),
            (z2[block], third),
            (third * inverse[block], third),
        )
        return tuple(s + kept * (a * b) for s, (a, b) in zip(sums, pairs))

    zero = jnp.zeros((8, BLK), jnp.float32)
    sums = lax.fori_loop(0, block_count, add_up, (zero,) * MOMENTS, unroll=4)
    lane = lax.broadcasted_iota(jnp.int32, (8, BLK), 1)
    row = lax.broadcasted_iota(jnp.int32, (8, BLK), 0)
    moments = zero
    for k in range(MOMENTS):
        moments = jnp.where(lane == 8 * row + k, jnp.sum(sums[k], axis=1, keepdims=True), moments)
    moments = jnp.sum(moments, axis=0, keepdims=True)
    moments_ref[...] = jnp.broadcast_to(moments, moments_ref.shape)


def fluid_kernel(
    axes, fluid_count,
    live_ref, jitter_ref, smoothing_ref, displacement_ref, fluid_ref, partner_ref, mine_ref, other_ref,
    basis_ref, first_source, second_source,
    fluid_basis_ref,
    joined, source, b0, b1, b2, matrix,
):
    live = live_ref[0]
    width = jitter_ref.shape[1] // BLK + 2 * HALO
    join_chain(
        axes, live, jitter_ref, smoothing_ref, displacement_ref, partner_ref, mine_ref, other_ref, joined
    )

    def prepare(block, carry):
        _, _, scale, rhs = parts_of(joined[BASE - HALO + block])
        b0[block] = vector_pair(rhs * scale)
        b1[block] = vector_pair(basis_ref[0, block] * scale)
        b2[block] = vector_pair(basis_ref[1, block] * scale)
        return carry

    lax.fori_loop(HALO - 2, width - HALO + 2, prepare, 0, unroll=4)
    half = first_source.shape[0] - 2

    def put_source(block, carry):
        source[HALO + block] = first_source[block]
        source[HALO + half + block] = second_source[block]
        return carry

    lax.fori_loop(0, half, put_source, 0, unroll=4)
    for block in (HALO - 2, HALO - 1, HALO + live, HALO + live + 1):
        points, norm, _, _ = parts_of(joined[BASE - HALO + block])
        source[block] = source_of(points, norm)

    def anchor_of(index):
        return lax.div(index * live, jnp.int32(fluid_count))

    def generate_fluid(index, carry):
        lanes = pl.ds(pl.multiple_of(index * BLK, BLK), BLK)
        jitter = jnp.concatenate([fluid_ref[:, lanes], jnp.zeros((5, BLK), jnp.float32)], axis=0)
        points = centred(jitter)
        norm = jnp.sum(points * points, axis=0, keepdims=True)
        groups = target_groups(target_values(points, norm))
        first = anchor_of(index) + (HALO - 2)
        for place in range(5):
            columns = target_rows(groups, place - 2)
            distances = jnp.dot(source[first + place], columns, preferred_element_type=jnp.float32)
            store_pair(matrix.at[index], wendland_scaled(distances), place * BLK)
        return carry

    def apply_fluid(index, carry):
        first = anchor_of(index) + (HALO - 2)
        near = [
            jnp.concatenate([ref[first + place] for place in range(5)], axis=1)
            for ref in (b0, b1, b2)
        ]
        near = jnp.concatenate(near, axis=0)
        product = jnp.dot(near, matrix[index], preferred_element_type=jnp.float32)
        for k in range(3):
            fluid_basis_ref[index, k] = sum_pairs(product, 16 * k)
        return carry

    lax.fori_loop(0, fluid_count, generate_fluid, 0, unroll=4)
    lax.fori_loop(0, fluid_count, apply_fluid, 0, unroll=4)


def step_coefficients(moments):
    def inner(left, right):
        total = 0.0
        for i, a in enumerate(left):
            for j, b in enumerate(right):
                total = total + a * b * moments[i + j]
        return total

    one = jnp.ones_like(moments[0])
    solution_part, residual, direction = [], [one], [one]
    norm = moments[0]
    for iteration in range(ITERS):
        image = [
            (direction[k] if k < len(direction) else 0.0) + (direction[k - 1] if k else 0.0)
            for k in range(len(direction) + 1)
        ]
        step = norm / inner(direction, image)
        old = solution_part + [0.0] * (len(direction) - len(solution_part))
        solution_part = [a + step * b for a, b in zip(old, direction)]
        residual = [
            (residual[k] if k < len(residual) else 0.0) - step * image[k] for k in range(len(image))
        ]
        following = inner(residual, residual)
        ratio = following / norm
        direction = [
            residual[k] + ratio * (direction[k] if k < len(direction) else 0.0)
            for k in range(len(residual))
        ]
        norm = following
    spread = 0.0
    for k, a in enumerate(residual):
        spread = spread + jnp.abs(a) * jnp.sqrt(jnp.maximum(moments[2 * k], 0.0))
    return solution_part, residual, spread * spread <= MAX_AMPLIFICATION**2 * norm


def finish_kernel(
    block_count, fluid_count, live_ref, moments_ref, smoothing_ref, displacement_ref,
    basis_ref, fluid_basis_ref, coefs_ref, residual_ref, fluid_ref, good_ref,
):
    live = live_ref[0]
    row = lax.broadcasted_iota(jnp.int32, (8, BLK), 0)
    lane = lax.broadcasted_iota(jnp.int32, (8, BLK), 1)
    summed = jnp.broadcast_to(jnp.sum(moments_ref[...], axis=0, keepdims=True), (8, BLK))
    moments = [
        jnp.sum(jnp.where(lane == 8 * row + k, summed, 0.0), axis=1, keepdims=True)
        for k in range(MOMENTS)
    ]
    solved, left, good = step_coefficients(moments)
    row = lax.broadcasted_iota(jnp.int32, (8, 1), 0)
    good_ref[0] = jnp.min(jnp.where(good | (row > 2), 1.0, 0.0)).astype(jnp.int32)
    solved = [jnp.broadcast_to(v, (8, BLK))[0:3] for v in solved]
    left = [jnp.broadcast_to(v, (8, BLK))[0:3] for v in left]

    def one_block(own, carry):
        lanes = pl.ds(pl.multiple_of(own * BLK, BLK), BLK)
        block = own + HALO
        parts = [displacement_ref[:, lanes]] + [basis_ref[k, block][0:3] for k in range(3)]
        scaled = sum(a * b for a, b in zip(solved, parts)) / (1.0 + smoothing_ref[:, lanes])
        remaining = sum(a * b for a, b in zip(left, parts))
        is_live = own < live
        coefs_ref[:, lanes] = jnp.where(is_live, scaled, 0.0)
        residual_ref[:, lanes] = jnp.where(is_live, remaining, 0.0)
        return carry

    lax.fori_loop(0, block_count, one_block, 0, unroll=4)

    def one_fluid(index, carry):
        lanes = pl.ds(pl.multiple_of(index * BLK, BLK), BLK)
        fluid_ref[:, lanes] = sum(a * fluid_basis_ref[index, k][0:3] for k, a in enumerate(solved))
        return carry

    lax.fori_loop(0, fluid_count, one_fluid, 0, unroll=4)


def wendland(row_points, col_points):
    spread = (row_points[0][:, None] - col_points[0][None, :]) ** 2
    spread = spread + (row_points[1][:, None] - col_points[1][None, :]) ** 2
    spread = spread + (row_points[2][:, None] - col_points[2][None, :]) ** 2
    scaled = jnp.sqrt(spread) * 0.5
    remain = jnp.maximum(1.0 - scaled, 0.0)
    return remain * remain * remain * remain * (4.0 * scaled + 1.0)


def block_ends(blocks, live_count):
    tail_index = live_count - 2 + jnp.arange(2, dtype=jnp.int32)
    tail_flags = (tail_index >= 0).astype(jnp.float32)
    padded = jnp.pad(blocks, ((0, 0), (2, 0), (0, 0)))
    tail_blocks = lax.dynamic_slice_in_dim(padded, live_count, 2, axis=1)
    head_flags = (jnp.arange(2, dtype=jnp.int32) < live_count).astype(jnp.float32)
    return (tail_blocks, tail_flags, blocks[:, :2], head_flags)


def join_left(nearer, farther, pick):
    return jnp.stack([jnp.where(pick, nearer[:, 0], farther[:, 1]), nearer[:, 1]], axis=1)


def join_right(nearer, farther, pick):
    return jnp.stack([nearer[:, 0], jnp.where(pick, nearer[:, 1], farther[:, 0])], axis=1)


def extend(own_blocks, left_pair, right_pair, live_count):
    padded = jnp.concatenate([left_pair, own_blocks, jnp.zeros_like(left_pair)], axis=1)
    return lax.dynamic_update_slice_in_dim(padded, right_pair, live_count + 2, axis=1)


def shifted(block, axes, distance):
    devices = range(lax.axis_size(axes))
    route = [(i - distance, i) for i in devices if i - distance in devices]
    return lax.ppermute(block, axes, route)


def iterate_with_reductions(axes, wing_jitter, live_blocks, smoothing, displacement, fluid_jitter):
    block_count = wing_jitter.shape[1] // BLK
    fluid_count = fluid_jitter.shape[1] // BLK
    live_count = live_blocks[0]
    factors = jnp.array(stretch_factors, jnp.float32)[:, None, None]
    own_points = wing_jitter.reshape(3, block_count, BLK) * factors
    own_flags = (jnp.arange(block_count, dtype=jnp.int32) < live_count).astype(jnp.float32)
    ends_of = {}
    neighbour_counts = {}
    for offset in (1, 2, -1, -2):
        points, counts = shifted((own_points, live_blocks), axes, offset)
        tail_blocks, tail_flags, head_blocks, head_flags = block_ends(points, counts[0])
        neighbour_counts[offset] = counts[0]
        ends_of[offset] = (tail_blocks, tail_flags) if offset > 0 else (head_blocks, head_flags)
    left_pick = ends_of[1][1][0] > 0
    right_pick = ends_of[-1][1][1] > 0
    left_points = join_left(ends_of[1][0], ends_of[2][0], left_pick)
    right_points = join_right(ends_of[-1][0], ends_of[-2][0], right_pick)
    left_flags = join_left(ends_of[1][1][None, :, None], ends_of[2][1][None, :, None], left_pick)
    right_flags = join_right(
        ends_of[-1][1][None, :, None], ends_of[-2][1][None, :, None], right_pick
    )
    ext_points = extend(own_points, left_points, right_points, live_count)
    ext_flags = extend(own_flags[None, :, None], left_flags, right_flags, live_count)
    ext_along = jnp.arange(block_count + 4, dtype=jnp.float32) - 2.0
    ext_points = ext_points.at[0].add(ext_along[:, None]).reshape(3, -1)
    col_flags = jnp.broadcast_to(ext_flags[0], (block_count + 4, BLK)).reshape(-1)
    row_points = (
        own_points.at[0].add(jnp.arange(block_count, dtype=jnp.float32)[:, None]).reshape(3, -1)
    )
    row_mask = jnp.repeat(own_flags, BLK)
    diagonal = 1.0 + smoothing

    def value_context(blocks):
        pieces = {}
        for offset in (1, 2, -1, -2):
            moved = shifted(blocks, axes, offset)
            tail_part, _, head_part, _ = block_ends(moved, neighbour_counts[offset])
            pieces[offset] = tail_part if offset > 0 else head_part
        left_values = join_left(pieces[1], pieces[2], left_pick)
        right_values = join_right(pieces[-1], pieces[-2], right_pick)
        return extend(blocks, left_values, right_values, live_count).reshape(3, -1)

    def apply(vector):
        ext_values = value_context(vector.reshape(3, block_count, BLK))

        def row_group(group):
            first_row = group * (2 * BLK)
            points = lax.dynamic_slice_in_dim(row_points, first_row, 2 * BLK, 1)
            col_points = lax.dynamic_slice_in_dim(ext_points, first_row, 6 * BLK, 1)
            flags = lax.dynamic_slice_in_dim(col_flags, first_row, 6 * BLK, 0)
            kernel = wendland(points, col_points) * flags[None, :]
            col_values = lax.dynamic_slice_in_dim(ext_values, first_row, 6 * BLK, 1)
            return jnp.einsum("cj,ij->ci", col_values, kernel, precision=lax.Precision.HIGHEST)

        result = lax.map(row_group, jnp.arange(block_count // 2, dtype=jnp.int32))
        result = result.transpose(1, 0, 2).reshape(3, -1)
        return result * row_mask + smoothing * vector

    def total(left, right):
        return lax.psum(jnp.sum(left * right, axis=1), axes)

    rhs = displacement * row_mask
    coefs = jnp.zeros_like(rhs)
    residual = rhs
    direction = precond = residual / diagonal
    norm_now = total(residual, precond)
    for iteration in range(ITERS):
        image = apply(direction)
        step_size = norm_now / total(direction, image)
        coefs = coefs + step_size[:, None] * direction
        residual = residual - step_size[:, None] * image
        if iteration + 1 < ITERS:
            precond = residual / diagonal
            norm_next = total(residual, precond)
            direction = precond + (norm_next / norm_now)[:, None] * direction
            norm_now = norm_next
    anchors = jnp.arange(fluid_count, dtype=jnp.int32) * live_count // fluid_count
    fluid_points = fluid_jitter.reshape(3, fluid_count, BLK) * factors
    fluid_points = fluid_points.at[0].add(anchors.astype(jnp.float32)[:, None])
    coef_ext = value_context(coefs.reshape(3, block_count, BLK))

    def fluid_block(points_and_anchor):
        points, anchor = points_and_anchor
        start_col = anchor * BLK
        col_points = lax.dynamic_slice_in_dim(ext_points, start_col, 5 * BLK, 1)
        flags = lax.dynamic_slice_in_dim(col_flags, start_col, 5 * BLK, 0)
        kernel = wendland(points, col_points) * flags[None, :]
        col_values = lax.dynamic_slice_in_dim(coef_ext, start_col, 5 * BLK, 1)
        return jnp.einsum("cj,ij->ci", col_values, kernel, precision=lax.Precision.HIGHEST)

    fluid_values = lax.map(fluid_block, (fluid_points.transpose(1, 0, 2), anchors))
    fluid_values = fluid_values.transpose(1, 0, 2).reshape(3, -1)
    return (coefs, residual, fluid_values)


def along_chips(values, axes, chips):
    count = lax.axis_size(axes)
    route = [(i, i + 2 * chips * (1 - 2 * (i % 2))) for i in range(count)]
    return lax.ppermute(values, axes, [(i, j) for i, j in route if 0 <= j < count])


def per_device(axes, wing_jitter, live_blocks, smoothing, displacement, fluid_jitter):
    block_count = wing_jitter.shape[1] // BLK
    fluid_count = fluid_jitter.shape[1] // BLK
    width = block_count + 2 * HALO
    smoothing_row = smoothing.reshape(1, -1)
    in_smem = pl.BlockSpec(memory_space=pltpu.SMEM)
    in_vmem = pl.BlockSpec(memory_space=pltpu.VMEM)

    def floats(*shape):
        return jax.ShapeDtypeStruct(shape, jnp.float32)

    small = pltpu.CompilerParams(vmem_limit_bytes=8 * 2**20)
    ends = pl.pallas_call(
        pack_kernel,
        out_shape=floats(2, HALO, 8, BLK),
        in_specs=[in_smem] + [in_vmem] * 3,
        out_specs=in_vmem,
        compiler_params=small,
    )(live_blocks, wing_jitter, smoothing_row, displacement)

    def join(near, far, *after, end=False):
        return pl.pallas_call(
            functools.partial(join_kernel, axes, end),
            out_shape=floats(HALO, 8, BLK),
            in_specs=[in_vmem] * 2 + [pl.BlockSpec(memory_space=pl.ANY)] * len(after),
            out_specs=in_vmem,
            scratch_shapes=[pltpu.VMEM((3 * HALO, 8, BLK), jnp.float32)],
            compiler_params=small,
        )(near, far, *after)

    matrix_shape = jax.ShapeDtypeStruct((width - 2, 3 * BLK, 2 * BLK), jnp.bfloat16)
    own_rows = block_count - 2
    first_rows = block_count // 2

    def own_part(first, rows, *matrix):
        return pl.pallas_call(
            functools.partial(own_kernel, first, rows, first + rows == own_rows),
            out_shape=(matrix_shape, jax.ShapeDtypeStruct((rows + 2, BLK, PIECES), jnp.bfloat16)),
            in_specs=[in_vmem] * (1 + len(matrix)),
            out_specs=(in_vmem, in_vmem),
            input_output_aliases={1: 0} if matrix else {},
            scratch_shapes=[pltpu.VMEM((rows + 2, 8, BLK), jnp.float32)],
            compiler_params=small,
            cost_estimate=pl.CostEstimate(flops=4 * 10**9, bytes_accessed=10**6, transcendentals=10**6),
        )(wing_jitter, *matrix)

    matrix, first_source = own_part(0, first_rows)
    matrix, second_source = own_part(first_rows, own_rows - first_rows, matrix)

    cores = [(i, i ^ 1) for i in range(lax.axis_size(axes))]
    partner = lax.ppermute(ends, axes, cores)
    chip = join(partner, ends, end=True)
    next_chip = along_chips(chip, axes, 1)
    beyond = along_chips(join(chip, next_chip, first_source), axes, 2)
    mine = join(next_chip, beyond, second_source)
    other = lax.ppermute(mine, axes, cores)

    vectors = pltpu.VMEM((width, 8, BLK), jnp.float32)
    pairs = pltpu.VMEM((width, 16, BLK), jnp.bfloat16)
    joined = pltpu.VMEM((2 * BASE + block_count, 8, BLK), jnp.float32)
    source = pltpu.VMEM((width, BLK, PIECES), jnp.bfloat16)
    basis, moments, _ = pl.pallas_call(
        functools.partial(chain_kernel, axes, block_count),
        out_shape=(floats(3, width, 8, BLK), floats(8, BLK), matrix_shape),
        in_specs=[in_smem] + [in_vmem] * 7,
        out_specs=(in_vmem,) * 3,
        input_output_aliases={7: 2},
        scratch_shapes=[
            joined,
            pltpu.VMEM((HALO + 2, BLK, PIECES), jnp.bfloat16),
            pltpu.VMEM((HALO + 2, 8, BLK), jnp.float32),
            *[vectors] * 5,
            *[pairs] * 3,
        ],
        compiler_params=pltpu.CompilerParams(vmem_limit_bytes=12 * 2**20),
    )(live_blocks, wing_jitter, smoothing_row, displacement, partner, mine, other, matrix)
    moments = moments + lax.ppermute(moments, axes, cores)
    chips = lax.axis_size(axes) // 2
    moments = lax.all_to_all(
        jnp.broadcast_to(moments[0:1], (chips, BLK)),
        axes,
        0,
        0,
        axis_index_groups=[[2 * chip + core for chip in range(chips)] for core in range(2)],
        tiled=True,
    )
    fluid_basis = pl.pallas_call(
        functools.partial(fluid_kernel, axes, fluid_count),
        out_shape=floats(fluid_count, 3, 8, BLK),
        in_specs=[in_smem] + [in_vmem] * 10,
        out_specs=in_vmem,
        scratch_shapes=[
            joined,
            source,
            *[pairs] * 3,
            pltpu.VMEM((fluid_count, 5 * BLK, 2 * BLK), jnp.bfloat16),
        ],
        compiler_params=pltpu.CompilerParams(vmem_limit_bytes=24 * 2**20),
        cost_estimate=pl.CostEstimate(flops=6 * 10**9, bytes_accessed=10**7, transcendentals=2 * 10**6),
    )(live_blocks, wing_jitter, smoothing_row, displacement, fluid_jitter, partner, mine, other, basis,
      first_source, second_source)
    coefs, residual, fluid_values, good = pl.pallas_call(
        functools.partial(finish_kernel, block_count, fluid_count),
        out_shape=(
            floats(3, block_count * BLK),
            floats(3, block_count * BLK),
            floats(3, fluid_count * BLK),
            jax.ShapeDtypeStruct((1,), jnp.int32),
        ),
        in_specs=[in_smem] + [in_vmem] * 5,
        out_specs=(in_vmem, in_vmem, in_vmem, in_smem),
        compiler_params=small,
    )(live_blocks, moments, smoothing_row, displacement, basis, fluid_basis)
    return lax.cond(
        good[0] == 1,
        lambda: (coefs, residual, fluid_values),
        lambda: iterate_with_reductions(
            axes, wing_jitter, live_blocks, smoothing, displacement, fluid_jitter
        ),
    )


def solution(mesh):
    placed = (P(None, "dom"), P("dom"), P("dom"), P(None, "dom"), P(None, "dom"))
    return jax.shard_map(
        functools.partial(per_device, "dom"),
        mesh=mesh,
        in_specs=placed,
        out_specs=(P(None, "dom"),) * 3,
        check_vma=False,
    )
```

```python
import functools
import jax
import jax.numpy as jnp
from jax import lax
from jax.experimental import pallas as pl
from jax.experimental.pallas import tpu as pltpu
from jax.sharding import PartitionSpec as P

BLK = 128
ITERS = 3
HALO = 6
BASE = 2 * HALO
PIECES = 48
MAX_AMPLIFICATION = 50.0
MOMENTS = 2 * ITERS + 1
APPLY_UNROLL = 16

stretch_factors = (1.0, 6.0, 6.0)


def pack_kernel(live_ref, jitter_ref, smoothing_ref, displacement_ref, ends_ref):
    live = live_ref[0]
    count = jnp.full((1, BLK), jnp.minimum(live, HALO), jnp.int32).astype(jnp.float32)
    for slot in range(HALO):
        tail_block = live - HALO + slot
        tail_start = pl.multiple_of(jnp.maximum(tail_block, 0) * BLK, BLK)
        starts = ((tail_block >= 0, tail_start), (slot < live, slot * BLK))
        for end, (kept, start) in enumerate(starts):
            lanes = pl.ds(start, BLK)
            mask = kept.astype(jnp.float32)
            ends_ref[end, slot, 0:3, :] = jitter_ref[:, lanes] * mask
            ends_ref[end, slot, 3:4, :] = smoothing_ref[:, lanes] * mask
            ends_ref[end, slot, 4:7, :] = displacement_ref[:, lanes] * mask
            ends_ref[end, slot, 7:8, :] = count


def count_in(row):
    return jnp.max(row).astype(jnp.int32)


def join_kernel(axes, end, near_ref, far_ref, *refs):
    joined_ref, buffer = refs[-2:]
    core = lax.rem(lax.axis_index(axes), 2)
    near = near_ref[core] if end else near_ref[...]
    far = far_ref[core] if end else far_ref[...]
    count = near[0, 7:8, :] + far[0, 7:8, :]
    held = count_in(near[0, 7:8, :])
    buffer[pl.ds(HALO, HALO)] = near
    buffer[pl.ds(HALO + jnp.where(core == 0, -held, held), HALO)] = far
    joined_ref[...] = buffer[pl.ds(HALO, HALO)]
    for slot in range(HALO):
        joined_ref[slot, 7:8, :] = jnp.minimum(count, float(HALO))


def split(values):
    high = values.astype(jnp.bfloat16).astype(jnp.float32)
    rest = values - high
    middle = rest.astype(jnp.bfloat16).astype(jnp.float32)
    return high, middle, rest - middle


def rows_of(row):
    return lax.broadcasted_iota(jnp.int32, (8, BLK), 0) == row


def centred(jitter):
    row = lax.broadcasted_iota(jnp.int32, (8, BLK), 0)
    scale = jnp.where(row == 0, 2.0, 12.0)
    shift = jnp.where(row == 0, 1.0, 6.0)
    return jnp.where(row < 3, jitter * scale - shift, 0.0)


def source_rows(points, norm):
    row = lax.broadcasted_iota(jnp.int32, (8, BLK), 0)
    extended = jnp.where(row >= 4, 1.0, points)
    extended = jnp.where(row == 3, norm, jnp.where(row == 5, points[0:1], extended))
    high, middle, low = split(extended)
    return jnp.concatenate([high, high, middle, high, low, middle], axis=0)


def target_values(points, norm):
    return jnp.where(rows_of(4), norm, -2.0 * points)


def target_groups(values):
    high, middle, low = split(values)
    bases = (jnp.where(rows_of(3), 1.0, high), middle, low)
    slopes = [jnp.where(rows_of(6), 2.0 * piece[0:1], 0.0) for piece in (high, middle, low)]
    slopes[0] = jnp.where(rows_of(5), 4.0, slopes[0])
    return bases, slopes


def target_rows(groups, delta):
    bases, slopes = groups
    if delta:
        bases = [base + float(delta) * slope for base, slope in zip(bases, slopes)]
        bases[0] = jnp.where(rows_of(7), 4.0 * delta * delta, bases[0])
    first = jnp.concatenate([bases[0], bases[1]], axis=0).astype(jnp.bfloat16)
    second = jnp.concatenate([bases[0], bases[2]], axis=0).astype(jnp.bfloat16)
    return jnp.concatenate([first, second, first], axis=0)


PHI_SCALE = 256.0


def wendland_scaled(distances):
    distances = jnp.maximum(distances, 1e-30)
    scaled = distances * lax.rsqrt(distances)
    remain = jnp.maximum(4.0 - scaled, 0.0)
    square = remain * remain
    return square * square * (scaled + 1.0)


def store_pair(ref, values, first_row):
    high = values.astype(jnp.bfloat16)
    low = (values - high.astype(jnp.float32)).astype(jnp.bfloat16)
    ref[pl.ds(first_row, BLK), 0:BLK] = high
    ref[pl.ds(first_row, BLK), BLK : 2 * BLK] = low


def vector_pair(values):
    values = values * (1.0 / PHI_SCALE)
    high = values.astype(jnp.bfloat16).astype(jnp.float32)
    return jnp.concatenate([high, values - high], axis=0).astype(jnp.bfloat16)


def sum_pairs(product, first):
    upper = product[first : first + 8] + product[first + 8 : first + 16]
    return upper[:, :BLK] + upper[:, BLK:]


def join_chain(axes, live, jitter_ref, smoothing_ref, displacement_ref, partner_ref, mine_ref, other_ref, joined):
    block_count = jitter_ref.shape[1] // BLK
    for extra in range(HALO):
        joined[BASE + block_count + extra] = jnp.zeros((8, BLK), jnp.float32)

    def put_own(block, carry):
        lanes = pl.ds(pl.multiple_of(block * BLK, BLK), BLK)
        kept = (block < live).astype(jnp.float32)
        joined[BASE + block, 0:3, :] = jitter_ref[:, lanes]
        joined[BASE + block, 3:4, :] = smoothing_ref[:, lanes] * kept
        joined[BASE + block, 4:7, :] = displacement_ref[:, lanes]
        return carry

    lax.fori_loop(0, block_count, put_own, 0, unroll=8)
    core = lax.rem(lax.axis_index(axes), 2)
    mine, other = mine_ref[...], other_ref[...]
    left_near = jnp.where(core == 0, 0, count_in(partner_ref[0, 0, 7:8, :]))
    right_near = jnp.where(core == 0, count_in(partner_ref[1, 0, 7:8, :]), 0)
    joined[pl.ds(BASE - HALO, HALO)] = partner_ref[0]
    joined[pl.ds(BASE - HALO - left_near, HALO)] = jnp.where(core == 0, mine, other)
    joined[pl.ds(BASE + live, HALO)] = partner_ref[1]
    joined[pl.ds(BASE + live + right_near, HALO)] = jnp.where(core == 0, other, mine)


def parts_of(packed):
    points = centred(packed)
    norm = jnp.sum(points * points, axis=0, keepdims=True)
    inverse = jnp.where(packed[3:4] > 0.0, 1.0 / (1.0 + packed[3:4]), 0.0)
    rhs = jnp.concatenate([packed[4:7], jnp.zeros((5, BLK), jnp.float32)], axis=0)
    return points, norm, jnp.broadcast_to(inverse, (8, BLK)), rhs


def source_of(points, norm):
    return jnp.transpose(source_rows(points, norm)).astype(jnp.bfloat16)


def generate_two(source, target, matrix, block, row):
    first, second = target_groups(target[block]), target_groups(target[block + 1])
    for place in range(4):
        columns = []
        if place < 3:
            columns.append(target_rows(first, place))
        if place > 0:
            columns.append(target_rows(second, place - 1))
        distances = jnp.dot(
            source[block + place],
            jnp.concatenate(columns, axis=1),
            preferred_element_type=jnp.float32,
        )
        values = wendland_scaled(distances)
        if place < 3:
            store_pair(matrix.at[row], values[:, :BLK], place * BLK)
        if place > 0:
            store_pair(matrix.at[row + 1], values[:, -BLK:], (place - 1) * BLK)


def own_kernel(first, rows, last, jitter_ref, *refs):
    matrix, mark_ref, source, target = refs[-4:]
    mark_ref[...] = jnp.zeros_like(mark_ref)

    def prepare(block, carry):
        lanes = pl.ds(pl.multiple_of((first + block) * BLK, BLK), BLK)
        jitter = jnp.concatenate([jitter_ref[:, lanes], jnp.zeros((5, BLK), jnp.float32)], axis=0)
        points = centred(jitter)
        norm = jnp.sum(points * points, axis=0, keepdims=True)
        source[block] = source_of(points, norm)
        target[block] = target_values(points, norm)
        return carry

    lax.fori_loop(0, rows + 2, prepare, 0, unroll=8)

    def generate(pair, carry):
        generate_two(source, target, matrix, 2 * pair, HALO + first + 2 * pair)
        return carry

    lax.fori_loop(0, rows // 2, generate, 0, unroll=4)
    if last:
        for row in range(HALO + first + rows, matrix.shape[0]):
            matrix[row] = jnp.zeros(matrix.shape[1:], matrix.dtype)


def chain_kernel(
    axes, block_count,
    live_ref, jitter_ref, smoothing_ref, displacement_ref, partner_ref, mine_ref, other_ref, _,
    basis_ref, moments_ref, matrix,
    joined, source, target, inverse, w0, z0, z1, z2, b0, b1, b2,
):
    w1_ref, w2_ref, w3_ref = (basis_ref.at[k] for k in range(3))
    live = live_ref[0]
    width = block_count + 2 * HALO
    join_chain(
        axes, live, jitter_ref, smoothing_ref, displacement_ref, partner_ref, mine_ref, other_ref, joined
    )

    def prepare(block, carry):
        _, _, scale, rhs = parts_of(joined[BASE - HALO + block])
        inverse[block] = scale
        w0[block] = rhs
        z0[block] = rhs * scale
        b0[block] = vector_pair(rhs * scale)
        return carry

    lax.fori_loop(0, width, prepare, 0, unroll=8)

    for start in (0, live + HALO - 2):
        for block in range(HALO + 2):
            points, norm, _, _ = parts_of(joined[BASE - HALO + start + block])
            source[block] = source_of(points, norm)
            target[block] = target_values(points, norm)
        for row in range(0, HALO, 2):
            generate_two(source, target, matrix, row, start + row)

    def apply_row(block, values, pairs, place_next):
        near = jnp.concatenate([pairs[block + place] for place in range(3)], axis=1)
        product = jnp.dot(near, matrix[block], preferred_element_type=jnp.float32)
        image = sum_pairs(product, 0) - values[block]
        for back in (1, 2):
            behind = pairs[block - back]
            product = lax.dot_general(
                jnp.concatenate([behind, behind], axis=1),
                matrix[block - back, back * BLK : (back + 1) * BLK, :],
                (((1,), (1,)), ((), ())),
                preferred_element_type=jnp.float32,
            )
            image = image + (product[0:8] + product[8:16])
        place_next(block, image)

    def apply(values, pairs, first, last, place_next):
        def one_row(block, carry):
            apply_row(block, values, pairs, place_next)
            return carry

        lax.fori_loop(first, last, one_row, 0, unroll=APPLY_UNROLL)

    def first_next(block, image):
        scaled = image * inverse[block]
        z1[block] = scaled
        b1[block] = vector_pair(scaled)
        w1_ref[block] = image

    def second_next(block, image):
        scaled = image * inverse[block]
        z2[block] = scaled
        b2[block] = vector_pair(scaled)
        w2_ref[block] = image

    def third_next(block, image):
        w3_ref[block] = image

    apply(z0, b0, 2, width - 2, first_next)
    apply(z1, b1, 4, width - 4, second_next)
    apply(z2, b2, 6, width - 6, third_next)

    def add_up(own, sums):
        block = own + HALO
        kept = (own < live).astype(jnp.float32)
        third = w3_ref[block]
        pairs = (
            (z0[block], w0[block]),
            (z0[block], w1_ref[block]),
            (z1[block], w1_ref[block]),
            (z1[block], w2_ref[block]),
            (z2[block], w2_ref[block]),
            (z2[block], third),
            (third * inverse[block], third),
        )
        return tuple(s + kept * (a * b) for s, (a, b) in zip(sums, pairs))

    zero = jnp.zeros((8, BLK), jnp.float32)
    sums = lax.fori_loop(0, block_count, add_up, (zero,) * MOMENTS, unroll=8)
    lane = lax.broadcasted_iota(jnp.int32, (8, BLK), 1)
    row = lax.broadcasted_iota(jnp.int32, (8, BLK), 0)
    moments = zero
    for k in range(MOMENTS):
        moments = jnp.where(lane == 8 * row + k, jnp.sum(sums[k], axis=1, keepdims=True), moments)
    moments = jnp.sum(moments, axis=0, keepdims=True)
    moments_ref[...] = jnp.broadcast_to(moments, moments_ref.shape)


def fluid_kernel(
    axes, fluid_count,
    live_ref, jitter_ref, smoothing_ref, displacement_ref, fluid_ref, partner_ref, mine_ref, other_ref,
    basis_ref,
    fluid_basis_ref,
    joined, source, b0, b1, b2, matrix,
):
    live = live_ref[0]
    width = jitter_ref.shape[1] // BLK + 2 * HALO
    join_chain(
        axes, live, jitter_ref, smoothing_ref, displacement_ref, partner_ref, mine_ref, other_ref, joined
    )

    def prepare(block, carry):
        points, norm, scale, rhs = parts_of(joined[BASE - HALO + block])
        source[block] = source_of(points, norm)
        b0[block] = vector_pair(rhs * scale)
        b1[block] = vector_pair(basis_ref[0, block] * scale)
        b2[block] = vector_pair(basis_ref[1, block] * scale)
        return carry

    lax.fori_loop(HALO - 2, width - HALO + 2, prepare, 0, unroll=8)

    def anchor_of(index):
        return lax.div(index * live, jnp.int32(fluid_count))

    def generate_fluid(index, carry):
        lanes = pl.ds(pl.multiple_of(index * BLK, BLK), BLK)
        jitter = jnp.concatenate([fluid_ref[:, lanes], jnp.zeros((5, BLK), jnp.float32)], axis=0)
        points = centred(jitter)
        norm = jnp.sum(points * points, axis=0, keepdims=True)
        groups = target_groups(target_values(points, norm))
        first = anchor_of(index) + (HALO - 2)
        for place in range(5):
            columns = target_rows(groups, place - 2)
            distances = jnp.dot(source[first + place], columns, preferred_element_type=jnp.float32)
            store_pair(matrix.at[index], wendland_scaled(distances), place * BLK)
        return carry

    def apply_fluid(index, carry):
        first = anchor_of(index) + (HALO - 2)
        near = [
            jnp.concatenate([ref[first + place] for place in range(5)], axis=1)
            for ref in (b0, b1, b2)
        ]
        near = jnp.concatenate(near, axis=0)
        product = jnp.dot(near, matrix[index], preferred_element_type=jnp.float32)
        for k in range(3):
            fluid_basis_ref[index, k] = sum_pairs(product, 16 * k)
        return carry

    lax.fori_loop(0, fluid_count, generate_fluid, 0, unroll=4)
    lax.fori_loop(0, fluid_count, apply_fluid, 0, unroll=8)


def step_coefficients(moments):
    def inner(left, right):
        total = 0.0
        for i, a in enumerate(left):
            for j, b in enumerate(right):
                total = total + a * b * moments[i + j]
        return total

    one = jnp.ones_like(moments[0])
    solution_part, residual, direction = [], [one], [one]
    norm = moments[0]
    for iteration in range(ITERS):
        image = [
            (direction[k] if k < len(direction) else 0.0) + (direction[k - 1] if k else 0.0)
            for k in range(len(direction) + 1)
        ]
        step = norm / inner(direction, image)
        old = solution_part + [0.0] * (len(direction) - len(solution_part))
        solution_part = [a + step * b for a, b in zip(old, direction)]
        residual = [
            (residual[k] if k < len(residual) else 0.0) - step * image[k] for k in range(len(image))
        ]
        following = inner(residual, residual)
        ratio = following / norm
        direction = [
            residual[k] + ratio * (direction[k] if k < len(direction) else 0.0)
            for k in range(len(residual))
        ]
        norm = following
    spread = 0.0
    for k, a in enumerate(residual):
        spread = spread + jnp.abs(a) * jnp.sqrt(jnp.maximum(moments[2 * k], 0.0))
    return solution_part, residual, spread * spread <= MAX_AMPLIFICATION**2 * norm


def finish_kernel(
    block_count, fluid_count, live_ref, moments_ref, smoothing_ref, displacement_ref,
    basis_ref, fluid_basis_ref, coefs_ref, residual_ref, fluid_ref, good_ref,
):
    live = live_ref[0]
    row = lax.broadcasted_iota(jnp.int32, (8, BLK), 0)
    lane = lax.broadcasted_iota(jnp.int32, (8, BLK), 1)
    summed = jnp.broadcast_to(jnp.sum(moments_ref[...], axis=0, keepdims=True), (8, BLK))
    moments = [
        jnp.sum(jnp.where(lane == 8 * row + k, summed, 0.0), axis=1, keepdims=True)
        for k in range(MOMENTS)
    ]
    solved, left, good = step_coefficients(moments)
    row = lax.broadcasted_iota(jnp.int32, (8, 1), 0)
    good_ref[0] = jnp.min(jnp.where(good | (row > 2), 1.0, 0.0)).astype(jnp.int32)
    solved = [jnp.broadcast_to(v, (8, BLK))[0:3] for v in solved]
    left = [jnp.broadcast_to(v, (8, BLK))[0:3] for v in left]

    def one_block(own, carry):
        lanes = pl.ds(pl.multiple_of(own * BLK, BLK), BLK)
        block = own + HALO
        parts = [displacement_ref[:, lanes]] + [basis_ref[k, block][0:3] for k in range(3)]
        scaled = sum(a * b for a, b in zip(solved, parts)) / (1.0 + smoothing_ref[:, lanes])
        remaining = sum(a * b for a, b in zip(left, parts))
        is_live = own < live
        coefs_ref[:, lanes] = jnp.where(is_live, scaled, 0.0)
        residual_ref[:, lanes] = jnp.where(is_live, remaining, 0.0)
        return carry

    lax.fori_loop(0, block_count, one_block, 0, unroll=8)

    def one_fluid(index, carry):
        lanes = pl.ds(pl.multiple_of(index * BLK, BLK), BLK)
        fluid_ref[:, lanes] = sum(a * fluid_basis_ref[index, k][0:3] for k, a in enumerate(solved))
        return carry

    lax.fori_loop(0, fluid_count, one_fluid, 0, unroll=8)


def wendland(row_points, col_points):
    spread = (row_points[0][:, None] - col_points[0][None, :]) ** 2
    spread = spread + (row_points[1][:, None] - col_points[1][None, :]) ** 2
    spread = spread + (row_points[2][:, None] - col_points[2][None, :]) ** 2
    scaled = jnp.sqrt(spread) * 0.5
    remain = jnp.maximum(1.0 - scaled, 0.0)
    return remain * remain * remain * remain * (4.0 * scaled + 1.0)


def block_ends(blocks, live_count):
    tail_index = live_count - 2 + jnp.arange(2, dtype=jnp.int32)
    tail_flags = (tail_index >= 0).astype(jnp.float32)
    padded = jnp.pad(blocks, ((0, 0), (2, 0), (0, 0)))
    tail_blocks = lax.dynamic_slice_in_dim(padded, live_count, 2, axis=1)
    head_flags = (jnp.arange(2, dtype=jnp.int32) < live_count).astype(jnp.float32)
    return (tail_blocks, tail_flags, blocks[:, :2], head_flags)


def join_left(nearer, farther, pick):
    return jnp.stack([jnp.where(pick, nearer[:, 0], farther[:, 1]), nearer[:, 1]], axis=1)


def join_right(nearer, farther, pick):
    return jnp.stack([nearer[:, 0], jnp.where(pick, nearer[:, 1], farther[:, 0])], axis=1)


def extend(own_blocks, left_pair, right_pair, live_count):
    padded = jnp.concatenate([left_pair, own_blocks, jnp.zeros_like(left_pair)], axis=1)
    return lax.dynamic_update_slice_in_dim(padded, right_pair, live_count + 2, axis=1)


def shifted(block, axes, distance):
    devices = range(lax.axis_size(axes))
    route = [(i - distance, i) for i in devices if i - distance in devices]
    return lax.ppermute(block, axes, route)


def iterate_with_reductions(axes, wing_jitter, live_blocks, smoothing, displacement, fluid_jitter):
    block_count = wing_jitter.shape[1] // BLK
    fluid_count = fluid_jitter.shape[1] // BLK
    live_count = live_blocks[0]
    factors = jnp.array(stretch_factors, jnp.float32)[:, None, None]
    own_points = wing_jitter.reshape(3, block_count, BLK) * factors
    own_flags = (jnp.arange(block_count, dtype=jnp.int32) < live_count).astype(jnp.float32)
    ends_of = {}
    neighbour_counts = {}
    for offset in (1, 2, -1, -2):
        points, counts = shifted((own_points, live_blocks), axes, offset)
        tail_blocks, tail_flags, head_blocks, head_flags = block_ends(points, counts[0])
        neighbour_counts[offset] = counts[0]
        ends_of[offset] = (tail_blocks, tail_flags) if offset > 0 else (head_blocks, head_flags)
    left_pick = ends_of[1][1][0] > 0
    right_pick = ends_of[-1][1][1] > 0
    left_points = join_left(ends_of[1][0], ends_of[2][0], left_pick)
    right_points = join_right(ends_of[-1][0], ends_of[-2][0], right_pick)
    left_flags = join_left(ends_of[1][1][None, :, None], ends_of[2][1][None, :, None], left_pick)
    right_flags = join_right(
        ends_of[-1][1][None, :, None], ends_of[-2][1][None, :, None], right_pick
    )
    ext_points = extend(own_points, left_points, right_points, live_count)
    ext_flags = extend(own_flags[None, :, None], left_flags, right_flags, live_count)
    ext_along = jnp.arange(block_count + 4, dtype=jnp.float32) - 2.0
    ext_points = ext_points.at[0].add(ext_along[:, None]).reshape(3, -1)
    col_flags = jnp.broadcast_to(ext_flags[0], (block_count + 4, BLK)).reshape(-1)
    row_points = (
        own_points.at[0].add(jnp.arange(block_count, dtype=jnp.float32)[:, None]).reshape(3, -1)
    )
    row_mask = jnp.repeat(own_flags, BLK)
    diagonal = 1.0 + smoothing

    def value_context(blocks):
        pieces = {}
        for offset in (1, 2, -1, -2):
            moved = shifted(blocks, axes, offset)
            tail_part, _, head_part, _ = block_ends(moved, neighbour_counts[offset])
            pieces[offset] = tail_part if offset > 0 else head_part
        left_values = join_left(pieces[1], pieces[2], left_pick)
        right_values = join_right(pieces[-1], pieces[-2], right_pick)
        return extend(blocks, left_values, right_values, live_count).reshape(3, -1)

    def apply(vector):
        ext_values = value_context(vector.reshape(3, block_count, BLK))

        def row_group(group):
            first_row = group * (2 * BLK)
            points = lax.dynamic_slice_in_dim(row_points, first_row, 2 * BLK, 1)
            col_points = lax.dynamic_slice_in_dim(ext_points, first_row, 6 * BLK, 1)
            flags = lax.dynamic_slice_in_dim(col_flags, first_row, 6 * BLK, 0)
            kernel = wendland(points, col_points) * flags[None, :]
            col_values = lax.dynamic_slice_in_dim(ext_values, first_row, 6 * BLK, 1)
            return jnp.einsum("cj,ij->ci", col_values, kernel, precision=lax.Precision.HIGHEST)

        result = lax.map(row_group, jnp.arange(block_count // 2, dtype=jnp.int32))
        result = result.transpose(1, 0, 2).reshape(3, -1)
        return result * row_mask + smoothing * vector

    def total(left, right):
        return lax.psum(jnp.sum(left * right, axis=1), axes)

    rhs = displacement * row_mask
    coefs = jnp.zeros_like(rhs)
    residual = rhs
    direction = precond = residual / diagonal
    norm_now = total(residual, precond)
    for iteration in range(ITERS):
        image = apply(direction)
        step_size = norm_now / total(direction, image)
        coefs = coefs + step_size[:, None] * direction
        residual = residual - step_size[:, None] * image
        if iteration + 1 < ITERS:
            precond = residual / diagonal
            norm_next = total(residual, precond)
            direction = precond + (norm_next / norm_now)[:, None] * direction
            norm_now = norm_next
    anchors = jnp.arange(fluid_count, dtype=jnp.int32) * live_count // fluid_count
    fluid_points = fluid_jitter.reshape(3, fluid_count, BLK) * factors
    fluid_points = fluid_points.at[0].add(anchors.astype(jnp.float32)[:, None])
    coef_ext = value_context(coefs.reshape(3, block_count, BLK))

    def fluid_block(points_and_anchor):
        points, anchor = points_and_anchor
        start_col = anchor * BLK
        col_points = lax.dynamic_slice_in_dim(ext_points, start_col, 5 * BLK, 1)
        flags = lax.dynamic_slice_in_dim(col_flags, start_col, 5 * BLK, 0)
        kernel = wendland(points, col_points) * flags[None, :]
        col_values = lax.dynamic_slice_in_dim(coef_ext, start_col, 5 * BLK, 1)
        return jnp.einsum("cj,ij->ci", col_values, kernel, precision=lax.Precision.HIGHEST)

    fluid_values = lax.map(fluid_block, (fluid_points.transpose(1, 0, 2), anchors))
    fluid_values = fluid_values.transpose(1, 0, 2).reshape(3, -1)
    return (coefs, residual, fluid_values)


def along_chips(values, axes, chips):
    count = lax.axis_size(axes)
    route = [(i, i + 2 * chips * (1 - 2 * (i % 2))) for i in range(count)]
    return lax.ppermute(values, axes, [(i, j) for i, j in route if 0 <= j < count])


def per_device(axes, wing_jitter, live_blocks, smoothing, displacement, fluid_jitter):
    block_count = wing_jitter.shape[1] // BLK
    fluid_count = fluid_jitter.shape[1] // BLK
    width = block_count + 2 * HALO
    smoothing_row = smoothing.reshape(1, -1)
    in_smem = pl.BlockSpec(memory_space=pltpu.SMEM)
    in_vmem = pl.BlockSpec(memory_space=pltpu.VMEM)

    def floats(*shape):
        return jax.ShapeDtypeStruct(shape, jnp.float32)

    small = pltpu.CompilerParams(vmem_limit_bytes=8 * 2**20)
    ends = pl.pallas_call(
        pack_kernel,
        out_shape=floats(2, HALO, 8, BLK),
        in_specs=[in_smem] + [in_vmem] * 3,
        out_specs=in_vmem,
        compiler_params=small,
    )(live_blocks, wing_jitter, smoothing_row, displacement)

    def join(near, far, *after, end=False):
        return pl.pallas_call(
            functools.partial(join_kernel, axes, end),
            out_shape=floats(HALO, 8, BLK),
            in_specs=[in_vmem] * 2 + [pl.BlockSpec(memory_space=pl.ANY)] * len(after),
            out_specs=in_vmem,
            scratch_shapes=[pltpu.VMEM((3 * HALO, 8, BLK), jnp.float32)],
            compiler_params=small,
        )(near, far, *after)

    matrix_shape = jax.ShapeDtypeStruct((width - 2, 3 * BLK, 2 * BLK), jnp.bfloat16)
    own_rows = block_count - 2
    first_rows = block_count // 2

    def own_part(first, rows, *matrix):
        return pl.pallas_call(
            functools.partial(own_kernel, first, rows, first + rows == own_rows),
            out_shape=(matrix_shape, floats(8, BLK)),
            in_specs=[in_vmem] * (1 + len(matrix)),
            out_specs=(in_vmem, in_vmem),
            input_output_aliases={1: 0} if matrix else {},
            scratch_shapes=[
                pltpu.VMEM((rows + 2, BLK, PIECES), jnp.bfloat16),
                pltpu.VMEM((rows + 2, 8, BLK), jnp.float32),
            ],
            compiler_params=small,
            cost_estimate=pl.CostEstimate(flops=4 * 10**9, bytes_accessed=10**6, transcendentals=10**6),
        )(wing_jitter, *matrix)

    matrix, first_mark = own_part(0, first_rows)
    matrix, second_mark = own_part(first_rows, own_rows - first_rows, matrix)

    cores = [(i, i ^ 1) for i in range(lax.axis_size(axes))]
    partner = lax.ppermute(ends, axes, cores)
    chip = join(partner, ends, end=True)
    next_chip = along_chips(chip, axes, 1)
    beyond = along_chips(join(chip, next_chip, first_mark), axes, 2)
    mine = join(next_chip, beyond, second_mark)
    other = lax.ppermute(mine, axes, cores)

    vectors = pltpu.VMEM((width, 8, BLK), jnp.float32)
    pairs = pltpu.VMEM((width, 16, BLK), jnp.bfloat16)
    joined = pltpu.VMEM((2 * BASE + block_count, 8, BLK), jnp.float32)
    source = pltpu.VMEM((width, BLK, PIECES), jnp.bfloat16)
    basis, moments, _ = pl.pallas_call(
        functools.partial(chain_kernel, axes, block_count),
        out_shape=(floats(3, width, 8, BLK), floats(lax.axis_size(axes), BLK), matrix_shape),
        in_specs=[in_smem] + [in_vmem] * 7,
        out_specs=(in_vmem,) * 3,
        input_output_aliases={7: 2},
        scratch_shapes=[
            joined,
            pltpu.VMEM((HALO + 2, BLK, PIECES), jnp.bfloat16),
            pltpu.VMEM((HALO + 2, 8, BLK), jnp.float32),
            *[vectors] * 5,
            *[pairs] * 3,
        ],
        compiler_params=pltpu.CompilerParams(vmem_limit_bytes=12 * 2**20),
    )(live_blocks, wing_jitter, smoothing_row, displacement, partner, mine, other, matrix)
    moments = lax.all_to_all(moments, axes, 0, 0, tiled=True)
    fluid_basis = pl.pallas_call(
        functools.partial(fluid_kernel, axes, fluid_count),
        out_shape=floats(fluid_count, 3, 8, BLK),
        in_specs=[in_smem] + [in_vmem] * 8,
        out_specs=in_vmem,
        scratch_shapes=[
            joined,
            source,
            *[pairs] * 3,
            pltpu.VMEM((fluid_count, 5 * BLK, 2 * BLK), jnp.bfloat16),
        ],
        compiler_params=pltpu.CompilerParams(vmem_limit_bytes=24 * 2**20),
        cost_estimate=pl.CostEstimate(flops=6 * 10**9, bytes_accessed=10**7, transcendentals=2 * 10**6),
    )(live_blocks, wing_jitter, smoothing_row, displacement, fluid_jitter, partner, mine, other, basis)
    coefs, residual, fluid_values, good = pl.pallas_call(
        functools.partial(finish_kernel, block_count, fluid_count),
        out_shape=(
            floats(3, block_count * BLK),
            floats(3, block_count * BLK),
            floats(3, fluid_count * BLK),
            jax.ShapeDtypeStruct((1,), jnp.int32),
        ),
        in_specs=[in_smem] + [in_vmem] * 5,
        out_specs=(in_vmem, in_vmem, in_vmem, in_smem),
        compiler_params=small,
    )(live_blocks, moments, smoothing_row, displacement, basis, fluid_basis)
    return lax.cond(
        good[0] == 1,
        lambda: (coefs, residual, fluid_values),
        lambda: iterate_with_reductions(
            axes, wing_jitter, live_blocks, smoothing, displacement, fluid_jitter
        ),
    )


def solution(mesh):
    placed = (P(None, "dom"), P("dom"), P("dom"), P(None, "dom"), P(None, "dom"))
    return jax.shard_map(
        functools.partial(per_device, "dom"),
        mesh=mesh,
        in_specs=placed,
        out_specs=(P(None, "dom"),) * 3,
        check_vma=False,
    )
```
